256 devices in a mesh: dp: 4 (over y_hi, core), vocab: 64 (over x, z, y_lo).
Axes of the slice: x: 4, y: 4 (y_hi: 2, y_lo: 2; y = y_hi * 2 + y_lo), z: 8, core: 2. Of those that a mesh axis runs over, the one named last changes fastest.
Arguments:
- hidden: bfloat16 [512, 8192], P('dp'), may hold values from -6 to 6
- head: bfloat16 [8192, 81920], P('dp', 'vocab'), may hold values from -4 to 4
- token_ids: int32 [512], replicated, may hold values from 0 to 81919
- old_logp: float32 [512], replicated, may hold values from -600 to 1
- advantages: float32 [512], replicated, may hold values from -5 to 5
- lengths: int32 [8], replicated, may hold values from 1 to 64, 256 in all
Outputs:
- log_ratio: float32 [512], P('dp')
- entropy: float32 [512], P('dp')
- grad_hidden: bfloat16 [512, 8192], P('vocab', 'dp')
- grad_head: bfloat16 [8192, 81920], P('dp', 'vocab')
The draws below stay inside these ranges and needn't reach their ends.
Inputs may be any that keep to these rules, and one draw needn't show every extreme that they name: The 8 lengths sum to exactly 256, and the largest is exactly 64.
All inputs are finite; a program needn't handle non-finite values.
Results may differ from the reference program's by a relative error of at most 0.013.
Values may be sent and summed in bfloat16 or wider, within the bound.
A program may use at most 64 MiB of HBM per device.

```python
import math
import jax
import jax.numpy as jnp
import numpy as np
from jax import lax

D = 8192
RESP = 64
VOCAB = 81920
NSEQ = 8
TOKENS = 512
LIVE = 256


logit_spread = 3.5


def shared_pattern(key):
    first = jax.random.randint(jax.random.fold_in(key, 72), (), 0, VOCAB)
    return first


def token_choice(key):
    token_key = jax.random.fold_in(key, 11)
    chosen = jax.random.randint(jax.random.fold_in(token_key, 1), (TOKENS,), 0, VOCAB)
    places = jax.random.permutation(jax.random.fold_in(token_key, 2), TOKENS)[:2]
    chosen = chosen.at[places[0]].set(0).at[places[1]].set(VOCAB - 1)
    return chosen.astype(jnp.int32)


def column_vectors(key, columns):
    vector_key = jax.random.fold_in(key, 21)

    def per_column(column):
        column_key = jax.random.fold_in(vector_key, column)
        normal_part = jax.random.truncated_normal(jax.random.fold_in(column_key, 1), -4.0, 4.0, (D,), jnp.float32)
        return normal_part
    return jax.vmap(per_column)(columns)


def column_scales(key, columns, spread):
    scale_key = jax.random.fold_in(key, 22)

    def per_column(column):
        return jnp.exp(spread * jax.random.uniform(jax.random.fold_in(scale_key, column), (), jnp.float32, -1.0, 1.0))
    return jax.vmap(per_column)(columns)


def head_columns(key, columns, spread, planted):
    first = shared_pattern(key)
    scaling = column_scales(key, columns, spread) * (logit_spread * D ** (-0.5))
    values = column_vectors(key, columns) * scaling[:, None]
    tie_first = (columns == first).astype(jnp.float32) * planted
    values = values * (1.0 - tie_first)[:, None]
    return values


def hidden_rows(key, planted):
    chosen = token_choice(key)
    target_lift = (math.log(VOCAB) + 0.5 * logit_spread ** 2) / logit_spread
    aligned_share = target_lift / math.sqrt(D)
    aligned = column_vectors(key, chosen)
    row_key = jax.random.fold_in(key, 31)
    normal_part = jax.random.truncated_normal(jax.random.fold_in(row_key, 1), -4.0, 4.0, (TOKENS, D), jnp.float32)
    noise_part = normal_part
    values = math.sqrt(1.0 - aligned_share ** 2) * noise_part + aligned_share * aligned
    rows = jnp.arange(TOKENS)
    leading = (rows % RESP == 0).astype(jnp.float32) * planted
    values = values * (1.0 - leading)[:, None]
    return jnp.clip(values, -6.0, 6.0)


def draw_token_ids(key, part):
    return token_choice(key)


def draw_hidden(key, part):
    values = hidden_rows(key, 0.0)
    return values.astype(jnp.bfloat16)


def draw_head(key, part):
    spread, planted = (0.0, 0.0)
    column_block = math.gcd(VOCAB, 4096)
    starts = jnp.arange(VOCAB // column_block, dtype=jnp.int32) * column_block

    def per_block(start):
        columns = start + jnp.arange(column_block, dtype=jnp.int32)
        return head_columns(key, columns, spread, planted).astype(jnp.bfloat16)
    blocks = lax.map(per_block, starts)
    return blocks.reshape(VOCAB, D).T


def draw_old_logp(key, part):
    spread, planted = (0.0, 0.0)
    rounded_rows = lax.optimization_barrier(hidden_rows(key, planted).astype(jnp.bfloat16))
    row_values = rounded_rows.astype(jnp.float32)
    chosen = token_choice(key)
    rounded_target = lax.optimization_barrier(head_columns(key, chosen, spread, planted).astype(jnp.bfloat16))
    target = jnp.sum(row_values * rounded_target.astype(jnp.float32), axis=1)
    column_block = math.gcd(VOCAB, 4096)
    starts = jnp.arange(VOCAB // column_block, dtype=jnp.int32) * column_block

    def advance(carry, start):
        running_top, running_total = carry
        columns = start + jnp.arange(column_block, dtype=jnp.int32)
        rounded_piece = lax.optimization_barrier(head_columns(key, columns, spread, planted).astype(jnp.bfloat16))
        scores = lax.dot_general(row_values, rounded_piece.astype(jnp.float32), (((1,), (1,)), ((), ())), precision=lax.Precision.HIGHEST)
        new_top = jnp.maximum(running_top, jnp.max(scores, axis=1))
        new_total = running_total * jnp.exp(running_top - new_top) + jnp.sum(jnp.exp(scores - new_top[:, None]), axis=1)
        return ((new_top, new_total), None)
    start_state = (jnp.full((TOKENS,), -1e+30, jnp.float32), jnp.zeros((TOKENS,), jnp.float32))
    (final_top, final_total), unused = lax.scan(advance, start_state, starts)
    log_norm = final_top + jnp.log(final_total)
    key = jax.random.fold_in(key, 41)
    offsets = 0.3 * jax.random.truncated_normal(key, -2.0, 2.0, (TOKENS,), jnp.float32)
    return (target - log_norm + offsets).astype(jnp.float32)


def split_up(number_of, total, most, skew):
    portions = [(1 << 20) // math.isqrt(standing ** skew) + 1 for standing in range(2, number_of + 1)]
    surplus, given = total - most - (number_of - 1), [1] * (number_of - 1)
    while surplus > 0:
        candidates = [i for i in range(number_of - 1) if given[i] < most]
        mass, left = sum([portions[i] for i in candidates]), surplus
        for i in candidates:
            addition = min(most - given[i], max(1, left * portions[i] // mass), surplus)
            given[i] = given[i] + addition
            surplus = surplus - addition
    return np.array([most] + given)


def uneven(own_key, amount, total, most, lean):
    if amount == 2:
        one = jax.random.randint(own_key, (), max(1, total - most), min(most, total - 1) + 1)
        return jnp.stack([one, total - one])
    tallies = jnp.asarray(split_up(amount, total, most, lean), jnp.int32)
    pairs = (amount - 1) // 2
    donor, receiver = tallies[1:1 + 2 * pairs:2], tallies[2:2 + 2 * pairs:2]
    slack = jnp.minimum(donor - 1, most - receiver)
    passed = jax.random.randint(jax.random.fold_in(own_key, 1), (pairs,), 0, 1 << 20) % (slack + 1)
    tallies = tallies.at[1:1 + 2 * pairs:2].set(donor - passed).at[2:2 + 2 * pairs:2].set(receiver + passed)
    return tallies[jax.random.permutation(jax.random.fold_in(own_key, 2), amount)]


def centred(own_key, extent, scale, bound, kind=jnp.bfloat16):
    drawn = scale * jax.random.normal(own_key, extent, jnp.float32)
    return jnp.clip(drawn, min=-bound, max=bound).astype(kind)


def setup_inputs(seed: int = 0) -> dict:
    keys = jax.random.split(jax.random.key(seed), 7)
    return {
        "hidden": draw_hidden(jax.random.fold_in(keys[6], 71), 0),
        "head": draw_head(jax.random.fold_in(keys[6], 71), 0),
        "token_ids": draw_token_ids(jax.random.fold_in(keys[6], 71), 0),
        "old_logp": draw_old_logp(jax.random.fold_in(keys[6], 71), 0),
        "advantages": centred(keys[4], (TOKENS,), 1.0, 5.0, jnp.float32),
        "lengths": uneven(keys[5], NSEQ, LIVE, RESP, 2).astype(jnp.int32),
    }


kl_weight = 0.2
entropy_weight = 0.1


def reference(hidden, head, token_ids, old_logp, advantages, lengths):
    positions = jnp.arange(TOKENS, dtype=jnp.int32)
    sequence = positions // RESP
    offset = positions % RESP
    live = (offset < lengths[sequence]).astype(jnp.float32)
    logits = jnp.dot(hidden, head, preferred_element_type=jnp.float32)
    top = jnp.max(logits, axis=1, keepdims=True)
    total = jnp.sum(jnp.exp(logits - top), axis=1)
    lse = top[:, 0] + jnp.log(total)
    probs = jnp.exp(logits - lse[:, None])
    entropy_all = lse - jnp.sum(probs * logits, axis=1)
    target = jnp.take_along_axis(logits, token_ids[:, None].astype(jnp.int32), axis=1)[:, 0]
    log_ratio_all = target - lse - old_logp
    ratio = jnp.exp(log_ratio_all)
    slope = (kl_weight - advantages) * ratio - kl_weight
    onehot = (jnp.arange(VOCAB, dtype=jnp.int32)[None, :] == token_ids[:, None]).astype(jnp.float32)
    dlogits = live[:, None] * (slope[:, None] * (onehot - probs)
                               + entropy_weight * probs * (logits - lse[:, None] + entropy_all[:, None]))
    dlogits = dlogits.astype(jnp.bfloat16)
    grad_hidden = jnp.dot(dlogits, head.T, preferred_element_type=jnp.float32).astype(jnp.bfloat16)
    grad_head = jnp.dot(hidden.T, dlogits, preferred_element_type=jnp.float32).astype(jnp.bfloat16)
    return live * log_ratio_all, live * entropy_all, grad_hidden, grad_head
```

```python
import functools

import jax
import jax.numpy as jnp
from jax import lax
from jax.experimental import pallas as pl
from jax.experimental.pallas import tpu as pltpu
from jax.sharding import PartitionSpec as P

kl_weight = 0.2
entropy_weight = 0.1

F32 = jnp.float32
BF16 = jnp.bfloat16
MESH = pl.DeviceIdType.MESH

RESP = 64
SLOTS = 512
ROWS = 256
GROUP = 128
DEPTH = 2048
COLS = 1280
CC = 256
NC = COLS // CC
TF = 512
NT = DEPTH // TF
TILES_XY = (0, 1, 2)


def slot_of(lens, row):
    end = 0
    slot = row
    for s in range(len(lens) - 1):
        end = end + lens[s]
        slot = slot + jnp.where(row >= end, RESP - lens[s], 0)
    return slot


def iota(shape, dim):
    return lax.broadcasted_iota(jnp.int32, shape, dim)


def merge(parts):
    top = functools.reduce(jnp.maximum, [p[0:1] for p in parts])
    scales = [jnp.exp(p[0:1] - top) for p in parts]
    total = sum(p[1:2] * s for p, s in zip(parts, scales))
    weighted = sum(p[2:3] * s for p, s in zip(parts, scales))
    target = sum(p[3:4] for p in parts)
    return top, total, weighted, target


def main_kernel(
    len_ref, tok_ref, old_ref, adv_ref, hid_ref, head_ref,
    comp_out, dl_out, lr_out, en_out, gh_out,
    spread, head_v, comp, lp, rxc, sy, ryy, logit, st1, st2, stz, stxy, dl_all, sm_all, dle, part, rx1, s2, rx2, gh_acc,
    loc_sem, hs_s, hs_r, lc_s, lc_r, ly_s, ly_r, z_s, z_r, xy_s, xy_r, d_s, d_r, m_s, m_r, a_s, a_r, b_s, b_r, out_sem,
):
    dp = lax.axis_index("dp")
    v = lax.axis_index("vocab")
    y_hi, core = dp // 2, dp % 2
    x, z, y_lo = v // 16, (v // 2) % 8, v % 2
    m = x * 2 + y_lo

    def dp_id(d):
        return {"dp": d, "vocab": v}

    def z_id(k):
        return {"dp": dp, "vocab": x * 16 + ((z + k) % 8) * 2 + y_lo}

    def xy_id(k):
        q = (m + k) % 8
        return {"dp": dp, "vocab": (q // 2) * 16 + z * 2 + q % 2}

    def remote(src, dst, ss, rs, dev):
        return pltpu.make_async_remote_copy(
            src_ref=src, dst_ref=dst, send_sem=ss, recv_sem=rs, device_id=dev, device_id_type=MESH
        )

    head_copy = pltpu.make_async_copy(head_ref, head_v, loc_sem.at[0])
    head_copy.start()
    own_copy = pltpu.make_async_copy(
        hid_ref.at[:, pl.ds(pl.multiple_of(dp * DEPTH, DEPTH), DEPTH)], spread.at[dp], loc_sem.at[1]
    )
    own_copy.start()

    barrier = pltpu.get_barrier_semaphore()
    for k in range(1, 4):
        pl.semaphore_signal(barrier, inc=1, device_id=dp_id((dp + k) % 4), device_id_type=MESH)
    for k in range(1, 8):
        pl.semaphore_signal(barrier, inc=1, device_id=z_id(k), device_id_type=MESH)
        pl.semaphore_signal(barrier, inc=1, device_id=xy_id(k), device_id_type=MESH)
    pl.semaphore_wait(barrier, 17)

    hs = []
    for k in (2, 1, 3):
        d = (dp + k) % 4
        c = remote(
            hid_ref.at[:, pl.ds(pl.multiple_of(d * DEPTH, DEPTH), DEPTH)], spread.at[dp],
            hs_s.at[k - 1], hs_r.at[k - 1], dp_id(d),
        )
        c.start()
        hs.append(c)

    lens = [len_ref[s] for s in range(8)]
    pick = (slot_of(lens, iota((ROWS, 1), 0)) == iota((ROWS, SLOTS), 1)).astype(F32).astype(BF16)
    base = 128 * core + 64 * y_hi
    my_slot = slot_of(lens, base + iota((64, 1), 0))
    my_mask = my_slot == iota((64, SLOTS), 1)
    tok = jnp.sum(jnp.where(my_mask, tok_ref[...], 0), axis=1, keepdims=True)
    old = jnp.sum(jnp.where(my_mask, old_ref[...], 0.0), axis=1, keepdims=True)
    adv = jnp.sum(jnp.where(my_mask, adv_ref[...], 0.0), axis=1, keepdims=True)

    own_copy.wait()
    for c in hs:
        c.wait()

    def compact(t, _):
        cols = pl.ds(pl.multiple_of(t * 256, 256), 256)
        full = spread[:, :, cols].reshape(SLOTS, 256)
        comp[:, cols] = jnp.dot(pick, full, preferred_element_type=F32).astype(BF16)
        return 0

    lax.fori_loop(0, DEPTH // 256, compact, 0)
    comp_copy = pltpu.make_async_copy(comp, comp_out, out_sem.at[0])
    comp_copy.start()
    head_copy.wait()

    def core_copy(j):
        return remote(
            lp.at[j, pl.ds(pl.multiple_of(128 * (1 - core), 128), 128)], rxc.at[j],
            lc_s.at[j], lc_r.at[j], dp_id(y_hi * 2 + 1 - core),
        )

    def y_copy(j):
        return remote(sy.at[j], ryy.at[j], ly_s.at[j], ly_r.at[j], dp_id((1 - y_hi) * 2 + core))

    def product(j, _):
        cols = pl.ds(pl.multiple_of(j * CC, CC), CC)
        lp[j] = jnp.dot(comp[...], head_v[:, cols], preferred_element_type=F32)
        core_copy(j).start()
        return 0

    lax.fori_loop(0, NC, product, 0)

    def chip_sum(j, _):
        core_copy(j).wait()
        far = 64 * (1 - y_hi)
        near = 64 * y_hi
        far_rows = pl.ds(pl.multiple_of(far, 64), 64)
        sy[j] = lp[j, pl.ds(pl.multiple_of(128 * core + far, 64), 64)] + rxc[j, far_rows]
        y_copy(j).start()
        cols = pl.ds(pl.multiple_of(j * CC, CC), CC)
        near_rows = pl.ds(pl.multiple_of(near, 64), 64)
        logit[:, cols] = lp[j, pl.ds(pl.multiple_of(128 * core + near, 64), 64)] + rxc[j, near_rows]
        return 0

    lax.fori_loop(0, NC, chip_sum, 0)

    def full_sum(j, _):
        y_copy(j).wait()
        cols = pl.ds(pl.multiple_of(j * CC, CC), CC)
        logit[:, cols] += ryy[j]
        return 0

    lax.fori_loop(0, NC, full_sum, 0)

    eye = iota((64, 128), 0) == iota((64, 128), 1)

    def to_row(col):
        return jnp.sum(jnp.where(eye, col, 0.0), axis=0, keepdims=True)

    def to_col(row):
        return jnp.sum(jnp.where(eye, row, 0.0), axis=1, keepdims=True)

    l = logit[...]
    hit = iota((64, COLS), 1) == tok - v * COLS
    top = jnp.max(l, axis=1, keepdims=True)
    e = jnp.exp(l - top)
    st1[...] = jnp.concatenate(
        [
            to_row(top),
            to_row(jnp.sum(e, axis=1, keepdims=True)),
            to_row(jnp.sum(e * l, axis=1, keepdims=True)),
            to_row(jnp.sum(jnp.where(hit, l, 0.0), axis=1, keepdims=True)),
            jnp.zeros((4, 128), F32),
        ],
        axis=0,
    )

    def z_copy(k):
        return remote(st1, stz.at[k - 1], z_s.at[k - 1], z_r.at[k - 1], z_id(k))

    def xy_copy(k):
        return remote(st2, stxy.at[k - 1], xy_s.at[k - 1], xy_r.at[k - 1], xy_id(k))

    for k in range(1, 8):
        z_copy(k).start()
    for k in range(1, 8):
        z_copy(k).wait()
    st2[...] = jnp.concatenate(
        list(merge([st1[...]] + [stz[k] for k in range(7)])) + [jnp.zeros((4, 128), F32)], axis=0
    )
    for k in range(1, 8):
        xy_copy(k).start()
    for k in range(1, 8):
        xy_copy(k).wait()
    top, total, weighted, target = merge([st2[...]] + [stxy[k] for k in range(7)])
    lse_row = top + jnp.log(total)
    lse = to_col(lse_row)
    entropy = to_col(lse_row - weighted / total)
    log_ratio = to_col(target) - lse - old
    slope = (kl_weight - adv) * jnp.exp(log_ratio) - kl_weight
    l = logit[...]
    shifted = l - lse
    probs = jnp.exp(shifted)
    grad = slope * (hit.astype(F32) - probs) + entropy_weight * probs * (shifted + entropy)
    mine = pl.ds(pl.multiple_of(base, 64), 64)
    dl_all[mine, :] = grad.astype(BF16)
    lane = iota((64, 128), 1)
    sm_all[mine, :] = jnp.where(lane == 0, log_ratio, jnp.where(lane == 1, entropy, 0.0))

    far = pl.ds(pl.multiple_of(128 * core + 64 * (1 - y_hi), 64), 64)
    y_dev, c_dev = dp_id((1 - y_hi) * 2 + core), dp_id(y_hi * 2 + 1 - core)
    dy = remote(dl_all.at[mine], dl_all.at[mine], d_s.at[0], d_r.at[0], y_dev)
    dc = remote(dl_all.at[mine], dl_all.at[mine], d_s.at[1], d_r.at[1], c_dev)
    dyc = remote(dl_all.at[far], dl_all.at[far], d_s.at[2], d_r.at[2], c_dev)
    dy.start()
    dc.start()
    sm = []
    for k in range(1, 4):
        c = remote(sm_all.at[mine], sm_all.at[mine], m_s.at[k - 1], m_r.at[k - 1], dp_id((dp + k) % 4))
        c.start()
        sm.append(c)
    dy.wait_recv()
    dyc.start()
    dc.wait_recv()
    dyc.wait_recv()
    dl_copy = pltpu.make_async_copy(dl_all, dl_out, out_sem.at[1])
    dl_copy.start()

    row_slot = slot_of(lens, iota((1, ROWS), 1))
    r = iota((SLOTS, 1), 0)
    slot_xy = (r // 128) * 128 + ((r // 8) % 8) * 16 + ((r // 64) % 2) * 8 + r % 8
    slot_z = ((r // 16) % 4) * 128 + (r // 64) * 16 + ((r // 8) % 2) * 8 + r % 8
    me_first = {True: m, False: z}
    id_first = {True: xy_id, False: z_id}
    me_second = {True: z, False: m}
    id_second = {True: z_id, False: xy_id}

    def first_copy(t, k, xy):
        q = (me_first[xy] + k) % 8
        return remote(
            part.at[t, pl.ds(pl.multiple_of(q * 64, 64), 64)], rx1.at[t, k - 1],
            a_s.at[t, k - 1], a_r.at[t, k - 1], id_first[xy](k),
        )

    def second_copy(t, k, xy):
        q = (me_second[xy] + k) % 8
        return remote(
            s2.at[t, pl.ds(pl.multiple_of(q * 16, 16), 16)], rx2.at[t, k - 1],
            b_s.at[t, k - 1], b_r.at[t, k - 1], id_second[xy](k),
        )

    def expand(slots):
        put = (slots == row_slot).astype(F32).astype(BF16)

        def step(j, _):
            cols = pl.ds(pl.multiple_of(j * CC, CC), CC)
            dle[:, cols] = jnp.dot(put, dl_all[:, cols], preferred_element_type=F32).astype(BF16)
            return 0

        lax.fori_loop(0, NC, step, 0)

    def partial(t, xy):
        def step(h, _):
            rows = pl.ds(pl.multiple_of(t * TF + h * 256, 256), 256)
            cols = pl.ds(pl.multiple_of(h * 256, 256), 256)
            part[t, :, cols] = lax.dot_general(
                dle[...], head_v[rows, :], (((1,), (1,)), ((), ())), preferred_element_type=F32
            ).astype(BF16)
            return 0

        lax.fori_loop(0, TF // 256, step, 0)

        def send(k, _):
            first_copy(t, k, xy).start()
            return 0

        lax.fori_loop(1, 8, send, 0)

    order = [(t, t in TILES_XY) for t in range(NT)]
    order = [o for o in order if not o[1]] + [o for o in order if o[1]]
    done = None
    for t, xy in order:
        if done is not xy:
            expand(slot_xy if xy else slot_z)
            done = xy
        partial(t, xy)

    for c in sm:
        c.wait()
    mask = slot_of(lens, iota((ROWS, 1), 0)) == dp * GROUP + iota((ROWS, GROUP), 1)
    vals = sm_all[...]
    lr_out[...] = jnp.sum(jnp.where(mask, vals[:, 0:1], 0.0), axis=0, keepdims=True)
    en_out[...] = jnp.sum(jnp.where(mask, vals[:, 1:2], 0.0), axis=0, keepdims=True)

    for t, xy in order:
        def wait_first(k, _, t=t, xy=xy):
            first_copy(t, k, xy).wait()
            return 0

        lax.fori_loop(1, 8, wait_first, 0)
        acc = part[t, pl.ds(pl.multiple_of(me_first[xy] * 64, 64), 64)].astype(F32)
        for k in range(7):
            acc = acc + rx1[t, k].astype(F32)
        for q in range(8):
            rows = acc[8 * q : 8 * q + 8]
            s2[t, 16 * q : 16 * q + 16] = jnp.concatenate([rows[:, 0:256], rows[:, 256:512]], axis=0).astype(BF16)

        def send_second(k, _, t=t, xy=xy):
            second_copy(t, k, xy).start()
            return 0

        lax.fori_loop(1, 8, send_second, 0)

    for t, xy in order:
        def wait_second(k, _, t=t, xy=xy):
            second_copy(t, k, xy).wait()
            return 0

        lax.fori_loop(1, 8, wait_second, 0)
        acc = s2[t, pl.ds(pl.multiple_of(me_second[xy] * 16, 16), 16)].astype(F32)
        for k in range(7):
            acc = acc + rx2[t, k].astype(F32)
        gh_acc[:, t * TF : t * TF + 256] = acc[0:8]
        gh_acc[:, t * TF + 256 : t * TF + 512] = acc[8:16]
    gh_out[...] = gh_acc[...]
    dy.wait_send()
    dc.wait_send()
    dyc.wait_send()
    comp_copy.wait()
    dl_copy.wait()


def head_kernel(comp_ref, dl_ref, lr_ref, en_ref, gh_ref, gw_out, lr_out, en_out, gh_out):
    gw_out[...] = lax.dot_general(
        comp_ref[...], dl_ref[...], (((0,), (0,)), ((), ())), preferred_element_type=F32
    ).astype(BF16)
    lr_out[...] = lr_ref[...]
    en_out[...] = en_ref[...]
    gh_out[...] = gh_ref[...].astype(BF16)


def local(hidden, head, token_ids, old_logp, advantages, lengths):
    vmem = pl.BlockSpec(memory_space=pltpu.VMEM)
    hbm = pl.BlockSpec(memory_space=pl.ANY)
    dma = pltpu.SemaphoreType.DMA
    comp, dl, lr, en, gh = pl.pallas_call(
        main_kernel,
        out_shape=(
            jax.ShapeDtypeStruct((ROWS, DEPTH), BF16),
            jax.ShapeDtypeStruct((ROWS, COLS), BF16),
            jax.ShapeDtypeStruct((1, GROUP), F32),
            jax.ShapeDtypeStruct((1, GROUP), F32),
            jax.ShapeDtypeStruct((8, DEPTH), F32),
        ),
        in_specs=[pl.BlockSpec(memory_space=pltpu.SMEM), vmem, vmem, vmem, hbm, hbm],
        out_specs=(hbm, hbm, vmem, vmem, vmem),
        scratch_shapes=[
            pltpu.VMEM((4, GROUP, DEPTH), BF16),
            pltpu.VMEM((DEPTH, COLS), BF16),
            pltpu.VMEM((ROWS, DEPTH), BF16),
            pltpu.VMEM((NC, ROWS, CC), F32),
            pltpu.VMEM((NC, 128, CC), F32),
            pltpu.VMEM((NC, 64, CC), F32),
            pltpu.VMEM((NC, 64, CC), F32),
            pltpu.VMEM((64, COLS), F32),
            pltpu.VMEM((8, 128), F32),
            pltpu.VMEM((8, 128), F32),
            pltpu.VMEM((7, 8, 128), F32),
            pltpu.VMEM((7, 8, 128), F32),
            pltpu.VMEM((ROWS, COLS), BF16),
            pltpu.VMEM((ROWS, 128), F32),
            pltpu.VMEM((SLOTS, COLS), BF16),
            pltpu.VMEM((NT, SLOTS, TF), BF16),
            pltpu.VMEM((NT, 7, 64, TF), BF16),
            pltpu.VMEM((NT, 128, 256), BF16),
            pltpu.VMEM((NT, 7, 16, 256), BF16),
            pltpu.VMEM((8, DEPTH), F32),
            dma((2,)), dma((3,)), dma((3,)), dma((NC,)), dma((NC,)), dma((NC,)), dma((NC,)),
            dma((7,)), dma((7,)), dma((7,)), dma((7,)), dma((3,)), dma((3,)), dma((3,)), dma((3,)),
            dma((NT, 7)), dma((NT, 7)), dma((NT, 7)), dma((NT, 7)), dma((2,)),
        ],
        compiler_params=pltpu.CompilerParams(
            collective_id=0, has_side_effects=True, vmem_limit_bytes=48 * 1024 * 1024
        ),
        name="main",
    )(lengths, token_ids[None], old_logp[None], advantages[None], hidden, head)
    whole = lambda shape: pl.BlockSpec(shape, lambda i: (0, 0))
    gw, lr, en, gh = pl.pallas_call(
        head_kernel,
        grid=(DEPTH // 256,),
        out_shape=(
            jax.ShapeDtypeStruct((DEPTH, COLS), BF16),
            jax.ShapeDtypeStruct((1, GROUP), F32),
            jax.ShapeDtypeStruct((1, GROUP), F32),
            jax.ShapeDtypeStruct((8, DEPTH), BF16),
        ),
        in_specs=[
            pl.BlockSpec((ROWS, 256), lambda i: (0, i)), whole((ROWS, COLS)), whole((1, GROUP)), whole((1, GROUP)),
            whole((8, DEPTH)),
        ],
        out_specs=(pl.BlockSpec((256, COLS), lambda i: (i, 0)), whole((1, GROUP)), whole((1, GROUP)), whole((8, DEPTH))),
        compiler_params=pltpu.CompilerParams(vmem_limit_bytes=32 * 1024 * 1024),
        name="head_grad",
    )(comp, dl, lr, en, gh)
    return lr[0], en[0], gh, gw


def solution(mesh):
    in_specs = (P("dp", None), P("dp", "vocab"), P(), P(), P(), P())
    out_specs = (P("dp"), P("dp"), P("vocab", "dp"), P("dp", "vocab"))
    return jax.shard_map(local, mesh=mesh, in_specs=in_specs, out_specs=out_specs, check_vma=False)
```

```python
import functools

import jax
import jax.numpy as jnp
from jax import lax
from jax.experimental import pallas as pl
from jax.experimental.pallas import tpu as pltpu
from jax.sharding import PartitionSpec as P

kl_weight = 0.2
entropy_weight = 0.1

F32 = jnp.float32
BF16 = jnp.bfloat16
MESH = pl.DeviceIdType.MESH

RESP = 64
SLOTS = 512
ROWS = 256
GROUP = 128
DEPTH = 2048
COLS = 1280
CC = 256
NC = COLS // CC
TF = 512
NT = DEPTH // TF
XF = 1408
ZF = DEPTH - XF


def iota(shape, dim):
    return lax.broadcasted_iota(jnp.int32, shape, dim)


def merge(parts):
    top = functools.reduce(jnp.maximum, [p[0:1] for p in parts])
    scales = [jnp.exp(p[0:1] - top) for p in parts]
    total = sum(p[1:2] * s for p, s in zip(parts, scales))
    weighted = sum(p[2:3] * s for p, s in zip(parts, scales))
    target = sum(p[3:4] for p in parts)
    return top, total, weighted, target


def plan(lens):
    ends = [0]
    for z in range(8):
        for x in range(4):
            count = jnp.clip(lens[2 * x + z // 4] - 16 * (z % 4), 0, 16)
            ends.append(ends[-1] + count)
    return ends


def rank_of(lens, ends, slot):
    seq, pos = slot // RESP, slot % RESP
    block = ((seq % 2) * 4 + pos // 16) * 4 + seq // 2
    first = jnp.zeros_like(slot)
    for b in range(1, 32):
        first = jnp.where(block == b, ends[b], first)
    length = jnp.zeros_like(slot)
    for s in range(8):
        length = jnp.where(seq == s, lens[s], length)
    return jnp.where(pos < length, first + pos % 16, -1)


def row_of(rank):
    return jnp.where(rank >= 0, (rank % 8) * 32 + rank // 8, -1)


def onehot(mask):
    return mask.astype(F32).astype(BF16)


def main_kernel(
    len_hbm, tok_hbm, old_hbm, adv_hbm, hid_ref, head_ref,
    turn_out, dl_out, lr_out, en_out, gh_out,
    len_ref, tok_ref, old_ref, adv_ref,
    spread, head_v, comp, lp, rxc, sy, ryy, logit, st1, st2, stz, stxy, dl_all, sm_all, part, rx1, s2, rx2, gat, turned,
    loc_sem, hc_s, hc_r, hx_s, hx_r, hz_s, hz_r, fx_s, fx_r, fz_s, fz_r,
    lc_s, lc_r, ly_s, ly_r, z_s, z_r, xy_s, xy_r, d_s, d_r, m_s, m_r, a_s, a_r, b_s, b_r, g_s, g_r, out_sem,
):
    dp = lax.axis_index("dp")
    v = lax.axis_index("vocab")
    y_hi, core = dp // 2, dp % 2
    x, z, y_lo = v // 16, (v // 2) % 8, v % 2
    m = x * 2 + y_lo

    def dp_id(d):
        return {"dp": d, "vocab": v}

    def z_id(k):
        return {"dp": dp, "vocab": x * 16 + ((z + k) % 8) * 2 + y_lo}

    def xy_id(k):
        q = (m + k) % 8
        return {"dp": dp, "vocab": (q // 2) * 16 + z * 2 + q % 2}

    def remote(src, dst, ss, rs, dev):
        return pltpu.make_async_remote_copy(
            src_ref=src, dst_ref=dst, send_sem=ss, recv_sem=rs, device_id=dev, device_id_type=MESH
        )

    small = [
        pltpu.make_async_copy(a, b, loc_sem.at[2 + i])
        for i, (a, b) in enumerate(((len_hbm, len_ref), (tok_hbm, tok_ref), (old_hbm, old_ref), (adv_hbm, adv_ref)))
    ]
    for c in small:
        c.start()

    barrier = pltpu.get_barrier_semaphore()
    for k in range(1, 4):
        pl.semaphore_signal(barrier, inc=1, device_id=dp_id((dp + k) % 4), device_id_type=MESH)
    for k in range(1, 8):
        pl.semaphore_signal(barrier, inc=1, device_id=z_id(k), device_id_type=MESH)
        pl.semaphore_signal(barrier, inc=1, device_id=xy_id(k), device_id_type=MESH)
    own_copy = pltpu.make_async_copy(
        hid_ref.at[:, pl.ds(pl.multiple_of(dp * DEPTH, DEPTH), DEPTH)], spread.at[dp], loc_sem.at[1]
    )
    own_copy.start()
    head_copy = pltpu.make_async_copy(head_ref, head_v, loc_sem.at[0])
    head_copy.start()
    pl.semaphore_wait(barrier, 17)

    z_rows = pl.ds(pl.multiple_of(16 * z, 16), 16)
    x_rows = pl.ds(pl.multiple_of(32 * x, 32), 32)
    z_cols, x_cols = pl.ds(XF, ZF), pl.ds(0, XF)

    def cross_z(c):
        d = (1 - y_hi) * 2 + c
        src = hid_ref.at[z_rows, pl.ds(pl.multiple_of(d * DEPTH + XF, 128), ZF)]
        return remote(src, spread.at[dp, z_rows, z_cols], hz_s.at[c], hz_r.at[core], dp_id(d))

    def cross_x(c):
        d = (1 - y_hi) * 2 + c
        src = hid_ref.at[x_rows, pl.ds(pl.multiple_of(d * DEPTH, 128), XF)]
        return remote(src, spread.at[dp, x_rows, x_cols], hx_s.at[c], hx_r.at[core], dp_id(d))

    def near_core():
        d = y_hi * 2 + 1 - core
        src = hid_ref.at[:, pl.ds(pl.multiple_of(d * DEPTH, DEPTH), DEPTH)]
        return remote(src, spread.at[dp], hc_s.at[0], hc_r.at[0], dp_id(d))

    def pass_z(g, k):
        ref = spread.at[(1 - y_hi) * 2 + g, z_rows, z_cols]
        return remote(ref, ref, fz_s.at[g, k - 1], fz_r.at[g, k - 1], z_id(k))

    def pass_x(g, k):
        ref = spread.at[(1 - y_hi) * 2 + g, x_rows, x_cols]
        return remote(ref, ref, fx_s.at[g, k - 1], fx_r.at[g, k - 1], xy_id(2 * k))

    for c in (0, 1):
        cross_z(c).start()
        cross_x(c).start()
    near_core().start()

    for g in (0, 1):
        ref = spread.at[(1 - y_hi) * 2 + g, z_rows, z_cols]
        remote(ref, ref, hz_s.at[g], hz_r.at[g], z_id(1)).wait_recv()
        for k in range(1, 8):
            pass_z(g, k).start()
        ref = spread.at[(1 - y_hi) * 2 + g, x_rows, x_cols]
        remote(ref, ref, hx_s.at[g], hx_r.at[g], z_id(1)).wait_recv()
        for k in range(1, 4):
            pass_x(g, k).start()

    for c in small:
        c.wait()
    lens = [len_ref[s] for s in range(8)]
    ends = plan(lens)
    pick = onehot(row_of(rank_of(lens, ends, iota((1, SLOTS), 1))) == iota((ROWS, SLOTS), 0))
    base = 128 * y_hi + 64 * core
    my_mask = row_of(rank_of(lens, ends, iota((1, SLOTS), 1))) == base + iota((64, SLOTS), 0)
    tok = jnp.sum(jnp.where(my_mask, tok_ref[...], 0), axis=1, keepdims=True)
    old = jnp.sum(jnp.where(my_mask, old_ref[...], 0.0), axis=1, keepdims=True)
    adv = jnp.sum(jnp.where(my_mask, adv_ref[...], 0.0), axis=1, keepdims=True)

    own_copy.wait()
    near_core().wait()
    for g in (0, 1):
        cross_z(g).wait_send()
        cross_x(g).wait_send()
        for k in range(1, 8):
            pass_z(g, k).wait()
        for k in range(1, 4):
            pass_x(g, k).wait()

    def compact(t, _):
        cols = pl.ds(pl.multiple_of(t * 256, 256), 256)
        full = spread[:, :, cols].reshape(SLOTS, 256)
        comp[:, cols] = jnp.dot(pick, full, preferred_element_type=F32).astype(BF16)
        return 0

    lax.fori_loop(0, DEPTH // 256, compact, 0)
    head_copy.wait()

    def core_copy(j):
        return remote(
            lp.at[j, :, 1 - core], rxc.at[j],
            lc_s.at[j], lc_r.at[j], dp_id(y_hi * 2 + 1 - core),
        )

    def y_copy(j):
        return remote(sy.at[j], ryy.at[j], ly_s.at[j], ly_r.at[j], dp_id((1 - y_hi) * 2 + core))

    def product(j, _):
        cols = pl.ds(pl.multiple_of(j * CC, CC), CC)
        lp[j] = jnp.dot(comp[...], head_v[:, cols], preferred_element_type=F32).reshape(2, 2, 64, CC)
        core_copy(j).start()
        return 0

    lax.fori_loop(0, NC, product, 0)

    def chip_sum(j, _):
        core_copy(j).wait()
        sy[j] = lp[j, 1 - y_hi, core] + rxc[j, 1 - y_hi]
        y_copy(j).start()
        cols = pl.ds(pl.multiple_of(j * CC, CC), CC)
        logit[:, cols] = lp[j, y_hi, core] + rxc[j, y_hi]
        return 0

    lax.fori_loop(0, NC, chip_sum, 0)

    def full_sum(j, _):
        y_copy(j).wait()
        cols = pl.ds(pl.multiple_of(j * CC, CC), CC)
        logit[:, cols] += ryy[j]
        return 0

    lax.fori_loop(0, NC, full_sum, 0)

    eye = iota((64, 128), 0) == iota((64, 128), 1)

    def to_row(col):
        return jnp.sum(jnp.where(eye, col, 0.0), axis=0, keepdims=True)

    def to_col(row):
        return jnp.sum(jnp.where(eye, row, 0.0), axis=1, keepdims=True)

    l = logit[...]
    hit = iota((64, COLS), 1) == tok - v * COLS
    top = jnp.max(l, axis=1, keepdims=True)
    e = jnp.exp(l - top)
    st1[...] = jnp.concatenate(
        [
            to_row(top),
            to_row(jnp.sum(e, axis=1, keepdims=True)),
            to_row(jnp.sum(e * l, axis=1, keepdims=True)),
            to_row(jnp.sum(jnp.where(hit, l, 0.0), axis=1, keepdims=True)),
            jnp.zeros((4, 128), F32),
        ],
        axis=0,
    )

    def z_copy(k):
        return remote(st1, stz.at[k - 1], z_s.at[k - 1], z_r.at[k - 1], z_id(k))

    def xy_copy(k):
        return remote(st2, stxy.at[k - 1], xy_s.at[k - 1], xy_r.at[k - 1], xy_id(k))

    for k in range(1, 8):
        z_copy(k).start()

    def turn(t, _):
        cols = pl.ds(pl.multiple_of(t * 256, 256), 256)
        turned[cols, :] = comp[:, cols].astype(F32).T.astype(BF16)
        return 0

    lax.fori_loop(0, DEPTH // 256, turn, 0)
    turn_copy = pltpu.make_async_copy(turned, turn_out, out_sem.at[1])
    turn_copy.start()
    for k in range(1, 8):
        z_copy(k).wait()
    st2[...] = jnp.concatenate(
        list(merge([st1[...]] + [stz[k] for k in range(7)])) + [jnp.zeros((4, 128), F32)], axis=0
    )
    for k in range(1, 8):
        xy_copy(k).start()
    for k in range(1, 8):
        xy_copy(k).wait()
    top, total, weighted, target = merge([st2[...]] + [stxy[k] for k in range(7)])
    lse_row = top + jnp.log(total)
    lse = to_col(lse_row)
    entropy = to_col(lse_row - weighted / total)
    log_ratio = to_col(target) - lse - old
    slope = (kl_weight - adv) * jnp.exp(log_ratio) - kl_weight
    l = logit[...]
    shifted = l - lse
    probs = jnp.exp(shifted)
    grad = slope * (hit.astype(F32) - probs) + entropy_weight * probs * (shifted + entropy)
    mine = pl.ds(pl.multiple_of(base, 64), 64)
    dl_all[mine, :] = grad.astype(BF16)

    far = pl.ds(pl.multiple_of(128 * (1 - y_hi) + 64 * core, 64), 64)
    y_dev, c_dev = dp_id((1 - y_hi) * 2 + core), dp_id(y_hi * 2 + 1 - core)
    dy = remote(dl_all.at[mine], dl_all.at[mine], d_s.at[0], d_r.at[0], y_dev)
    dc = remote(dl_all.at[mine], dl_all.at[mine], d_s.at[1], d_r.at[1], c_dev)
    dyc = remote(dl_all.at[far], dl_all.at[far], d_s.at[2], d_r.at[2], c_dev)
    dy.start()
    dc.start()
    lane = iota((64, 128), 1)
    sm_all[mine, :] = jnp.where(lane == 0, log_ratio, jnp.where(lane == 1, entropy, 0.0))
    sm = []
    for k in range(1, 4):
        c = remote(sm_all.at[mine], sm_all.at[mine], m_s.at[k - 1], m_r.at[k - 1], dp_id((dp + k) % 4))
        c.start()
        sm.append(c)

    def first_copy(t, q):
        return remote(
            part.at[t, pl.ds(pl.multiple_of(q * 32, 32), 32)], rx1.at[t, (q - m) % 8 - 1],
            a_s.at[t, q], a_r.at[t, (q - m) % 8 - 1], xy_id((q - m) % 8),
        )

    def partial(half):
        rows = pl.ds(pl.multiple_of(128 * half, 128), 128)

        def step(t, _):
            for h in range(TF // 256):
                feats = pl.ds(pl.multiple_of(t * TF + h * 256, 256), 256)
                part[t, rows, h * 256 : h * 256 + 256] = lax.dot_general(
                    dl_all[rows, :], head_v[feats, :], (((1,), (1,)), ((), ())), preferred_element_type=F32
                ).astype(BF16)
            for i in range(4):
                q = half * 4 + i

                @pl.when(q != m)
                def _():
                    first_copy(t, q).start()

            return 0

        lax.fori_loop(0, NT, step, 0)

    dc.wait_recv()
    partial(y_hi)
    dy.wait_recv()
    dyc.start()
    dyc.wait_recv()
    partial(1 - y_hi)
    dl_copy = pltpu.make_async_copy(dl_all, dl_out, out_sem.at[0])
    dl_copy.start()

    for c in sm:
        c.wait()
    mask = row_of(rank_of(lens, ends, dp * GROUP + iota((1, GROUP), 1))) == iota((ROWS, GROUP), 0)
    vals = sm_all[...]
    lr_out[...] = jnp.sum(jnp.where(mask, vals[:, 0:1], 0.0), axis=0, keepdims=True)
    en_out[...] = jnp.sum(jnp.where(mask, vals[:, 1:2], 0.0), axis=0, keepdims=True)

    def first_row(z_of, member):
        start = jnp.zeros_like(z_of)
        end = jnp.full_like(z_of, ends[4])
        for q in range(1, 8):
            start = jnp.where(z_of == q, ends[4 * q], start)
            end = jnp.where(z_of == q, ends[4 * q + 4], end)
        return (start - member + 7) // 8, end

    col = iota((128, 1), 0)
    start, end = first_row(col // 16, m)
    row = start + col % 8
    row = jnp.where(row * 8 + m < end, row, -1)
    row = row + 32 * ((col // 8) % 2) * (row >= 0).astype(jnp.int32)
    deal = onehot(row == iota((128, 64), 1))

    def second_copy(t, k):
        q = (z + k) % 8
        return remote(
            s2.at[t, pl.ds(pl.multiple_of(q * 16, 16), 16)], rx2.at[t, k - 1],
            b_s.at[t, k - 1], b_r.at[t, k - 1], z_id(k),
        )

    def third_copy(t, k):
        return remote(gat.at[t, 0], gat.at[t, k], g_s.at[t, k - 1], g_r.at[t, k - 1], xy_id(k))

    def first_sum(t, _):
        def wait(k, _):
            remote(rx1.at[t, k], rx1.at[t, k], a_s.at[t, 0], a_r.at[t, k], xy_id(1)).wait_recv()
            return 0

        lax.fori_loop(0, 7, wait, 0)
        acc = part[t, pl.ds(pl.multiple_of(m * 32, 32), 32)].astype(F32)
        for k in range(7):
            acc = acc + rx1[t, k].astype(F32)
        both = jnp.concatenate([acc[:, 0:256], acc[:, 256:512]], axis=0).astype(BF16)
        s2[t] = jnp.dot(deal, both, preferred_element_type=F32).astype(BF16)

        def send(k, _):
            second_copy(t, k).start()
            return 0

        lax.fori_loop(1, 8, send, 0)
        return 0

    lax.fori_loop(0, NT, first_sum, 0)

    def second_sum(t, _):
        def wait(k, _):
            second_copy(t, k).wait()
            return 0

        lax.fori_loop(1, 8, wait, 0)
        acc = s2[t, pl.ds(pl.multiple_of(z * 16, 16), 16)].astype(F32)
        for k in range(7):
            acc = acc + rx2[t, k].astype(F32)
        gat[t, 0] = acc.astype(BF16)

        def send(k, _):
            third_copy(t, k).start()
            return 0

        lax.fori_loop(1, 8, send, 0)
        return 0

    lax.fori_loop(0, NT, second_sum, 0)

    side = iota((16, 1), 0)
    rank = rank_of(lens, ends, 128 * x + 16 * z + 8 * y_lo + side % 8)
    owner = rank % 8
    start, _ = first_row(jnp.zeros_like(owner) + z, owner)
    place = ((m - owner) % 8) * 16 + (side // 8) * 8 + rank // 8 - start
    place = jnp.where(rank >= 0, place, -1)
    take = onehot(place == iota((16, 128), 1))
    for t in range(NT):
        def wait_third(k, _, t=t):
            third_copy(t, k).wait()
            return 0

        lax.fori_loop(1, 8, wait_third, 0)
        rows = jnp.dot(take, gat[t].reshape(128, 256), preferred_element_type=F32)
        gh_out[:, t * TF : t * TF + 256] = rows[0:8]
        gh_out[:, t * TF + 256 : t * TF + 512] = rows[8:16]

    def drain(t, _):
        def one(q, _):
            @pl.when(q != m)
            def _():
                first_copy(t, q).wait_send()

            return 0

        lax.fori_loop(0, 8, one, 0)
        return 0

    lax.fori_loop(0, NT, drain, 0)
    dy.wait_send()
    dc.wait_send()
    dyc.wait_send()
    dl_copy.wait()
    turn_copy.wait()


def head_kernel(turned_ref, dl_ref, lr_ref, en_ref, gh_ref, gw_out, lr_out, en_out, gh_out):
    gw_out[...] = jnp.dot(turned_ref[...], dl_ref[...], preferred_element_type=F32).astype(BF16)
    lr_out[...] = lr_ref[...]
    en_out[...] = en_ref[...]
    gh_out[...] = gh_ref[...].astype(BF16)


def local(hidden, head, token_ids, old_logp, advantages, lengths):
    vmem = pl.BlockSpec(memory_space=pltpu.VMEM)
    hbm = pl.BlockSpec(memory_space=pltpu.HBM)
    dma = pltpu.SemaphoreType.DMA
    turned, dl, lr, en, gh = pl.pallas_call(
        main_kernel,
        out_shape=(
            jax.ShapeDtypeStruct((DEPTH, ROWS), BF16),
            jax.ShapeDtypeStruct((ROWS, COLS), BF16),
            jax.ShapeDtypeStruct((1, GROUP), F32),
            jax.ShapeDtypeStruct((1, GROUP), F32),
            jax.ShapeDtypeStruct((8, DEPTH), F32),
        ),
        in_specs=[hbm] * 6,
        out_specs=(hbm, hbm, vmem, vmem, vmem),
        scratch_shapes=[
            pltpu.SMEM((8,), jnp.int32),
            pltpu.VMEM((1, SLOTS), jnp.int32),
            pltpu.VMEM((1, SLOTS), F32),
            pltpu.VMEM((1, SLOTS), F32),
            pltpu.VMEM((4, GROUP, DEPTH), BF16),
            pltpu.VMEM((DEPTH, COLS), BF16),
            pltpu.VMEM((ROWS, DEPTH), BF16),
            pltpu.VMEM((NC, 2, 2, 64, CC), F32),
            pltpu.VMEM((NC, 2, 64, CC), F32),
            pltpu.VMEM((NC, 64, CC), F32),
            pltpu.VMEM((NC, 64, CC), F32),
            pltpu.VMEM((64, COLS), F32),
            pltpu.VMEM((8, 128), F32),
            pltpu.VMEM((8, 128), F32),
            pltpu.VMEM((7, 8, 128), F32),
            pltpu.VMEM((7, 8, 128), F32),
            pltpu.VMEM((ROWS, COLS), BF16),
            pltpu.VMEM((ROWS, 128), F32),
            pltpu.VMEM((NT, ROWS, TF), BF16),
            pltpu.VMEM((NT, 7, 32, TF), BF16),
            pltpu.VMEM((NT, 128, 256), BF16),
            pltpu.VMEM((NT, 7, 16, 256), BF16),
            pltpu.VMEM((NT, 8, 16, 256), BF16),
            pltpu.VMEM((DEPTH, ROWS), BF16),
            dma((6,)), dma((1,)), dma((1,)), dma((2,)), dma((2,)), dma((2,)), dma((2,)),
            dma((2, 3)), dma((2, 3)), dma((2, 7)), dma((2, 7)),
            dma((NC,)), dma((NC,)), dma((NC,)), dma((NC,)),
            dma((7,)), dma((7,)), dma((7,)), dma((7,)), dma((3,)), dma((3,)), dma((3,)), dma((3,)),
            dma((NT, 8)), dma((NT, 7)), dma((NT, 7)), dma((NT, 7)), dma((NT, 7)), dma((NT, 7)), dma((2,)),
        ],
        compiler_params=pltpu.CompilerParams(
            collective_id=0, has_side_effects=True, vmem_limit_bytes=62 * 1024 * 1024
        ),
        name="main",
    )(lengths, token_ids[None], old_logp[None], advantages[None], hidden, head)
    whole = lambda shape: pl.BlockSpec(shape, lambda i: (0, 0))
    gw, lr, en, gh = pl.pallas_call(
        head_kernel,
        grid=(DEPTH // 256,),
        out_shape=(
            jax.ShapeDtypeStruct((DEPTH, COLS), BF16),
            jax.ShapeDtypeStruct((1, GROUP), F32),
            jax.ShapeDtypeStruct((1, GROUP), F32),
            jax.ShapeDtypeStruct((8, DEPTH), BF16),
        ),
        in_specs=[
            pl.BlockSpec((256, ROWS), lambda i: (i, 0)), whole((ROWS, COLS)), whole((1, GROUP)), whole((1, GROUP)),
            whole((8, DEPTH)),
        ],
        out_specs=(pl.BlockSpec((256, COLS), lambda i: (i, 0)), whole((1, GROUP)), whole((1, GROUP)), whole((8, DEPTH))),
        compiler_params=pltpu.CompilerParams(vmem_limit_bytes=62 * 1024 * 1024),
        name="head_grad",
    )(turned, dl, lr, en, gh)
    return lr[0], en[0], gh, gw


def solution(mesh):
    in_specs = (P("dp", None), P("dp", "vocab"), P(), P(), P(), P())
    out_specs = (P("dp"), P("dp"), P("vocab", "dp"), P("dp", "vocab"))
    return jax.shard_map(local, mesh=mesh, in_specs=in_specs, out_specs=out_specs, check_vma=False)
```

```python
import functools

import jax
import jax.numpy as jnp
from jax import lax
from jax.experimental import pallas as pl
from jax.experimental.pallas import tpu as pltpu
from jax.sharding import PartitionSpec as P

kl_weight = 0.2
entropy_weight = 0.1

F32 = jnp.float32
BF16 = jnp.bfloat16
MESH = pl.DeviceIdType.MESH

RESP = 64
SLOTS = 512
ROWS = 256
GROUP = 128
DEPTH = 2048
COLS = 1280
CC = 256
NC = COLS // CC
TF = 512
NT = DEPTH // TF
XF = 1408
ZF = DEPTH - XF


def iota(shape, dim):
    return lax.broadcasted_iota(jnp.int32, shape, dim)


def merge(parts):
    top = functools.reduce(jnp.maximum, [p[0:1] for p in parts])
    scales = [jnp.exp(p[0:1] - top) for p in parts]
    total = sum(p[1:2] * s for p, s in zip(parts, scales))
    weighted = sum(p[2:3] * s for p, s in zip(parts, scales))
    target = sum(p[3:4] for p in parts)
    return top, total, weighted, target


def plan_z(lens):
    ends = [0]
    for z in range(8):
        for x in range(4):
            ends.append(ends[-1] + jnp.clip(lens[2 * x + z // 4] - 16 * (z % 4), 0, 16))
    return ends


def plan_xy(lens):
    ends = [0]
    for m in range(8):
        for i in range(8):
            ends.append(ends[-1] + jnp.clip(lens[2 * (m // 2) + i // 4] - 16 * (i % 4) - 8 * (m % 2), 0, 8))
    return ends


def rank_of(lens, ends, slot, by_z):
    seq, pos = slot // RESP, slot % RESP
    if by_z:
        block, size = ((seq % 2) * 4 + pos // 16) * 4 + seq // 2, 16
    else:
        block, size = ((seq // 2) * 2 + (pos // 8) % 2) * 8 + (seq % 2) * 4 + pos // 16, 8
    first = jnp.zeros_like(slot)
    for b in range(1, len(ends) - 1):
        first = jnp.where(block == b, ends[b], first)
    length = jnp.zeros_like(slot)
    for s in range(8):
        length = jnp.where(seq == s, lens[s], length)
    return jnp.where(pos < length, first + pos % size, -1)


def row_of(rank):
    return jnp.where(rank >= 0, (rank % 8) * 32 + rank // 8, -1)


def onehot(mask):
    return mask.astype(F32).astype(BF16)


def main_kernel(
    len_hbm, tok_hbm, old_hbm, adv_hbm, hid_ref, head_ref,
    turn_out, dl_out, lr_out, en_out, gh_out,
    len_ref, tok_ref, old_ref, adv_ref,
    spread, head_v, comp, lp, rxc, sy, ryy, logit, lg, st1, st2, st3, stz, stxy, dl_all, dl_z, part, rx1, s2, rx2, gat, turned,
    loc_sem, hc_s, hc_r, hx_s, hx_r, hz_s, hz_r, fx_s, fx_r, fz_s, fz_r,
    lc_s, lc_r, ly_s, ly_r, z_s, z_r, xy_s, xy_r, gc_s, gc_r, gy_s, gy_r, gf_s, gf_r, m_s, m_r, a_s, a_r, b_s, b_r, g_s, g_r, out_sem,
):
    dp = lax.axis_index("dp")
    v = lax.axis_index("vocab")
    y_hi, core = dp // 2, dp % 2
    x, z, y_lo = v // 16, (v // 2) % 8, v % 2
    m = x * 2 + y_lo

    def dp_id(d):
        return {"dp": d, "vocab": v}

    def z_id(k):
        return {"dp": dp, "vocab": x * 16 + ((z + k) % 8) * 2 + y_lo}

    def xy_id(k):
        q = (m + k) % 8
        return {"dp": dp, "vocab": (q // 2) * 16 + z * 2 + q % 2}

    def remote(src, dst, ss, rs, dev):
        return pltpu.make_async_remote_copy(
            src_ref=src, dst_ref=dst, send_sem=ss, recv_sem=rs, device_id=dev, device_id_type=MESH
        )

    small = [
        pltpu.make_async_copy(a, b, loc_sem.at[2 + i])
        for i, (a, b) in enumerate(((len_hbm, len_ref), (tok_hbm, tok_ref), (old_hbm, old_ref), (adv_hbm, adv_ref)))
    ]
    for c in small:
        c.start()

    barrier = pltpu.get_barrier_semaphore()
    for k in range(1, 4):
        pl.semaphore_signal(barrier, inc=1, device_id=dp_id((dp + k) % 4), device_id_type=MESH)
    for k in range(1, 8):
        pl.semaphore_signal(barrier, inc=1, device_id=z_id(k), device_id_type=MESH)
        pl.semaphore_signal(barrier, inc=1, device_id=xy_id(k), device_id_type=MESH)
    own_copy = pltpu.make_async_copy(
        hid_ref.at[:, pl.ds(pl.multiple_of(dp * DEPTH, DEPTH), DEPTH)], spread.at[dp], loc_sem.at[1]
    )
    own_copy.start()
    head_copy = pltpu.make_async_copy(head_ref, head_v, loc_sem.at[0])
    head_copy.start()
    pl.semaphore_wait(barrier, 17)

    z_rows = pl.ds(pl.multiple_of(16 * z, 16), 16)
    x_rows = pl.ds(pl.multiple_of(32 * x, 32), 32)
    z_cols, x_cols = pl.ds(XF, ZF), pl.ds(0, XF)

    def cross_z(c):
        d = (1 - y_hi) * 2 + c
        src = hid_ref.at[z_rows, pl.ds(pl.multiple_of(d * DEPTH + XF, 128), ZF)]
        return remote(src, spread.at[dp, z_rows, z_cols], hz_s.at[c], hz_r.at[core], dp_id(d))

    def cross_x(c):
        d = (1 - y_hi) * 2 + c
        src = hid_ref.at[x_rows, pl.ds(pl.multiple_of(d * DEPTH, 128), XF)]
        return remote(src, spread.at[dp, x_rows, x_cols], hx_s.at[c], hx_r.at[core], dp_id(d))

    def near_core():
        d = y_hi * 2 + 1 - core
        src = hid_ref.at[:, pl.ds(pl.multiple_of(d * DEPTH, DEPTH), DEPTH)]
        return remote(src, spread.at[dp], hc_s.at[0], hc_r.at[0], dp_id(d))

    def pass_z(g, k):
        ref = spread.at[(1 - y_hi) * 2 + g, z_rows, z_cols]
        return remote(ref, ref, fz_s.at[g, k - 1], fz_r.at[g, k - 1], z_id(k))

    def pass_x(g, k):
        ref = spread.at[(1 - y_hi) * 2 + g, x_rows, x_cols]
        return remote(ref, ref, fx_s.at[g, k - 1], fx_r.at[g, k - 1], xy_id(2 * k))

    for c in (0, 1):
        cross_z(c).start()
        cross_x(c).start()
    near_core().start()

    for g in (0, 1):
        ref = spread.at[(1 - y_hi) * 2 + g, z_rows, z_cols]
        remote(ref, ref, hz_s.at[g], hz_r.at[g], z_id(1)).wait_recv()
        for k in range(1, 8):
            pass_z(g, k).start()
        ref = spread.at[(1 - y_hi) * 2 + g, x_rows, x_cols]
        remote(ref, ref, hx_s.at[g], hx_r.at[g], z_id(1)).wait_recv()
        for k in range(1, 4):
            pass_x(g, k).start()

    for c in small:
        c.wait()
    lens = [len_ref[s] for s in range(8)]
    ends_z, ends_xy = plan_z(lens), plan_xy(lens)
    slots = iota((1, SLOTS), 1)
    row_z = row_of(rank_of(lens, ends_z, slots, True))
    hits = row_z == iota((ROWS, SLOTS), 0)
    pick = onehot(hits)
    pick_xy = onehot(row_of(rank_of(lens, ends_xy, slots, False)) == iota((ROWS, SLOTS), 0))
    turn_order = lax.dot_general(pick_xy, pick, (((1,), (1,)), ((), ())), preferred_element_type=F32).astype(BF16)
    tok = jnp.sum(jnp.where(hits, tok_ref[...], 0), axis=1, keepdims=True)
    base = 128 * y_hi + 64 * core
    my_mask = row_z == base + iota((64, SLOTS), 0)
    my_tok = jnp.sum(jnp.where(my_mask, tok_ref[...], 0), axis=1, keepdims=True)
    old = jnp.sum(jnp.where(my_mask, old_ref[...], 0.0), axis=1, keepdims=True)
    adv = jnp.sum(jnp.where(my_mask, adv_ref[...], 0.0), axis=1, keepdims=True)

    own_copy.wait()
    near_core().wait()

    def compact(half, first):
        mine = onehot(row_of(rank_of(lens, ends_z, half * 256 + iota((1, 256), 1), True)) == iota((ROWS, 256), 0))

        def step(t, _):
            cols = pl.ds(pl.multiple_of(t * 256, 256), 256)
            full = spread[pl.ds(2 * half, 2), :, cols].reshape(256, 256)
            rows = jnp.dot(mine, full, preferred_element_type=F32).astype(BF16)
            comp[:, cols] = rows if first else comp[:, cols] + rows
            return 0

        lax.fori_loop(0, DEPTH // 256, step, 0)

    compact(y_hi, True)
    for g in (0, 1):
        cross_z(g).wait_send()
        cross_x(g).wait_send()
        for k in range(1, 8):
            pass_z(g, k).wait()
        for k in range(1, 4):
            pass_x(g, k).wait()
    compact(1 - y_hi, False)
    head_copy.wait()

    def core_copy(j):
        return remote(
            lp.at[j, :, 1 - core], rxc.at[j],
            lc_s.at[j], lc_r.at[j], dp_id(y_hi * 2 + 1 - core),
        )

    def y_copy(j):
        return remote(sy.at[j], ryy.at[j], ly_s.at[j], ly_r.at[j], dp_id((1 - y_hi) * 2 + core))

    def chip_sum(j):
        core_copy(j).wait()
        sy[j] = lp[j, 1 - y_hi, core] + rxc[j, 1 - y_hi]
        y_copy(j).start()
        cols = pl.ds(pl.multiple_of(j * CC, CC), CC)
        logit[:, cols] = lp[j, y_hi, core] + rxc[j, y_hi]

    def product(j, _):
        cols = pl.ds(pl.multiple_of(j * CC, CC), CC)
        lp[j] = jnp.dot(comp[...], head_v[:, cols], preferred_element_type=F32).reshape(2, 2, 64, CC)
        core_copy(j).start()

        @pl.when(j > 0)
        def _():
            chip_sum(j - 1)

        return 0

    lax.fori_loop(0, NC, product, 0)
    chip_sum(NC - 1)

    y_dev, c_dev = dp_id((1 - y_hi) * 2 + core), dp_id(y_hi * 2 + 1 - core)

    def give(j, sems, dev, side):
        ref = lg.at[j, side, core]
        return remote(ref, ref, sems[0].at[j], sems[1].at[j], dev)

    def full_sum(j, _):
        y_copy(j).wait()
        cols = pl.ds(pl.multiple_of(j * CC, CC), CC)
        l = logit[:, cols] + ryy[j]
        logit[:, cols] = l
        lg[j, y_hi, core] = l
        give(j, (gy_s, gy_r), y_dev, y_hi).start()
        give(j, (gc_s, gc_r), c_dev, y_hi).start()
        return 0

    lax.fori_loop(0, NC, full_sum, 0)

    eye = iota((64, 128), 0) == iota((64, 128), 1)

    def to_row(col):
        return jnp.sum(jnp.where(eye, col, 0.0), axis=0, keepdims=True)

    def to_col(row):
        return jnp.sum(jnp.where(eye, row, 0.0), axis=1, keepdims=True)

    l = logit[...]
    hit = iota((64, COLS), 1) == my_tok - v * COLS
    top = jnp.max(l, axis=1, keepdims=True)
    e = jnp.exp(l - top)
    st1[...] = jnp.concatenate(
        [
            to_row(top),
            to_row(jnp.sum(e, axis=1, keepdims=True)),
            to_row(jnp.sum(e * l, axis=1, keepdims=True)),
            to_row(jnp.sum(jnp.where(hit, l, 0.0), axis=1, keepdims=True)),
            jnp.zeros((4, 128), F32),
        ],
        axis=0,
    )

    def z_copy(k):
        return remote(st1, stz.at[k - 1], z_s.at[k - 1], z_r.at[k - 1], z_id(k))

    def xy_copy(k):
        return remote(st2, stxy.at[k - 1], xy_s.at[k - 1], xy_r.at[k - 1], xy_id(k))

    for k in range(1, 8):
        z_copy(k).start()

    def turn(t, _):
        cols = pl.ds(pl.multiple_of(t * 256, 256), 256)
        turned[cols, :] = comp[:, cols].astype(F32).T.astype(BF16)
        return 0

    lax.fori_loop(0, DEPTH // 256, turn, 0)
    turn_copy = pltpu.make_async_copy(turned, turn_out, out_sem.at[1])
    turn_copy.start()
    for k in range(1, 8):
        z_copy(k).wait()
    st2[...] = jnp.concatenate(
        list(merge([st1[...]] + [stz[k] for k in range(7)])) + [jnp.zeros((4, 128), F32)], axis=0
    )
    for k in range(1, 8):
        xy_copy(k).start()

    def forward(j, _):
        give(j, (gy_s, gy_r), y_dev, 1 - y_hi).wait_recv()
        give(j, (gf_s, gf_r), c_dev, 1 - y_hi).start()
        return 0

    lax.fori_loop(0, NC, forward, 0)
    for k in range(1, 8):
        xy_copy(k).wait()
    top, total, weighted, target = merge([st2[...]] + [stxy[k] for k in range(7)])
    lse_row = top + jnp.log(total)
    entropy_row = lse_row - weighted / total
    ratio_row = target - lse_row - to_row(old)
    slope_row = (kl_weight - to_row(adv)) * jnp.exp(ratio_row) - kl_weight
    st3[0] = jnp.concatenate([lse_row, entropy_row, ratio_row, slope_row, jnp.zeros((4, 128), F32)], axis=0)

    def row_copy(k):
        return remote(st3.at[0], st3.at[k], m_s.at[k - 1], m_r.at[k - 1], dp_id((dp + k) % 4))

    for k in range(1, 4):
        row_copy(k).start()

    def arrive(j, _):
        give(j, (gc_s, gc_r), c_dev, y_hi).wait()
        give(j, (gf_s, gf_r), c_dev, 1 - y_hi).wait()
        give(j, (gy_s, gy_r), y_dev, y_hi).wait_send()
        return 0

    lax.fori_loop(0, NC, arrive, 0)
    for k in range(1, 4):
        row_copy(k).wait()

    lse, entropy, log_ratio, slope = [
        jnp.concatenate([to_col(st3[(dp - d) % 4][i : i + 1]) for d in range(4)], axis=0) for i in range(4)
    ]

    def gradient(j, _):
        l = lg[j].reshape(ROWS, CC)
        hit = iota((ROWS, CC), 1) == tok - (v * COLS + j * CC)
        shifted = l - lse
        probs = jnp.exp(shifted)
        grad = slope * (hit.astype(F32) - probs) + entropy_weight * probs * (shifted + entropy)
        dl_all[:, pl.ds(pl.multiple_of(j * CC, CC), CC)] = grad.astype(BF16)
        return 0

    lax.fori_loop(0, NC, gradient, 0)
    dl_copy = pltpu.make_async_copy(dl_all, dl_out, out_sem.at[0])
    dl_copy.start()

    class By:
        pass

    by_xy, by_z = By(), By()
    by_xy.me, by_xy.peer, by_xy.other, by_xy.across, by_xy.rows = m, xy_id, z, z_id, dl_all
    by_z.me, by_z.peer, by_z.other, by_z.across, by_z.rows = z, z_id, m, xy_id, dl_z
    by_xy.starts = [ends_z[4 * q] for q in range(9)]
    by_z.starts = [ends_xy[8 * q] for q in range(9)]
    my_slots = 128 * x + 16 * z + 8 * y_lo + iota((16, 1), 0) % 8
    by_xy.rank = rank_of(lens, ends_z, my_slots, True)
    by_z.rank = rank_of(lens, ends_xy, my_slots, False)

    def first_copy(t, k, by):
        q = (by.me + k) % 8
        return remote(
            part.at[t, pl.ds(pl.multiple_of(q * 32, 32), 32)], rx1.at[t, k - 1],
            a_s.at[t, k - 1], a_r.at[t, k - 1], by.peer(k),
        )

    def partial(t, by):
        for h in range(TF // 256):
            part[t, :, h * 256 : h * 256 + 256] = lax.dot_general(
                by.rows[...], head_v[t * TF + h * 256 : t * TF + h * 256 + 256, :], (((1,), (1,)), ((), ())),
                preferred_element_type=F32,
            ).astype(BF16)

        def send(k, _):
            first_copy(t, k, by).start()
            return 0

        lax.fori_loop(1, 8, send, 0)

    order = [(0, by_xy), (3, by_z), (1, by_xy), (2, by_xy)]
    for t, by in order:
        if by is by_z:
            def reorder(j, _):
                cols = pl.ds(pl.multiple_of(j * CC, CC), CC)
                dl_z[:, cols] = jnp.dot(turn_order, dl_all[:, cols], preferred_element_type=F32).astype(BF16)
                return 0

            lax.fori_loop(0, NC, reorder, 0)
        partial(t, by)

    mask = row_of(rank_of(lens, ends_z, dp * GROUP + iota((1, GROUP), 1), True)) == iota((ROWS, GROUP), 0)
    lr_out[...] = jnp.sum(jnp.where(mask, log_ratio, 0.0), axis=0, keepdims=True)
    en_out[...] = jnp.sum(jnp.where(mask, entropy, 0.0), axis=0, keepdims=True)

    def first_row(by, owner, member):
        start = jnp.zeros_like(owner)
        end = jnp.zeros_like(owner) + by.starts[1]
        for q in range(1, 8):
            start = jnp.where(owner == q, by.starts[q], start)
            end = jnp.where(owner == q, by.starts[q + 1], end)
        return (start - member + 7) // 8, end

    def second_copy(t, k, by):
        q = (by.other + k) % 8
        return remote(
            s2.at[t, pl.ds(pl.multiple_of(q * 16, 16), 16)], rx2.at[t, k - 1],
            b_s.at[t, k - 1], b_r.at[t, k - 1], by.across(k),
        )

    def third_copy(t, k, by):
        return remote(gat.at[t, 0], gat.at[t, k], g_s.at[t, k - 1], g_r.at[t, k - 1], by.peer(k))

    for by in (by_xy, by_z):
        col = iota((128, 1), 0)
        start, end = first_row(by, col // 16, by.me)
        row = start + col % 8
        row = jnp.where(row * 8 + by.me < end, row, -1)
        row = row + 32 * ((col // 8) % 2) * (row >= 0).astype(jnp.int32)
        by.deal = onehot(row == iota((128, 64), 1))
        owner = by.rank % 8
        start, _ = first_row(by, jnp.zeros_like(owner) + by.other, owner)
        place = ((by.me - owner) % 8) * 16 + (iota((16, 1), 0) // 8) * 8 + by.rank // 8 - start
        by.take = onehot(jnp.where(by.rank >= 0, place, -1) == iota((16, 128), 1))

    def each(make):
        def step(k, _):
            make(k)
            return 0

        lax.fori_loop(1, 8, step, 0)

    for t, by in order:
        each(lambda k: first_copy(t, k, by).wait())
        acc = part[t, pl.ds(pl.multiple_of(by.me * 32, 32), 32)].astype(F32)
        for k in range(7):
            acc = acc + rx1[t, k].astype(F32)
        both = jnp.concatenate([acc[:, 0:256], acc[:, 256:512]], axis=0).astype(BF16)
        s2[t] = jnp.dot(by.deal, both, preferred_element_type=F32).astype(BF16)
        each(lambda k: second_copy(t, k, by).start())

    for t, by in order:
        each(lambda k: second_copy(t, k, by).wait())
        acc = s2[t, pl.ds(pl.multiple_of(by.other * 16, 16), 16)].astype(F32)
        for k in range(7):
            acc = acc + rx2[t, k].astype(F32)
        gat[t, 0] = acc.astype(BF16)
        each(lambda k: third_copy(t, k, by).start())

    for t, by in order:
        each(lambda k: third_copy(t, k, by).wait())
        rows = jnp.dot(by.take, gat[t].reshape(128, 256), preferred_element_type=F32)
        gh_out[:, t * TF : t * TF + 256] = rows[0:8]
        gh_out[:, t * TF + 256 : t * TF + 512] = rows[8:16]
    dl_copy.wait()
    turn_copy.wait()


def head_kernel(turned_hbm, dl_hbm, lr_ref, en_ref, gh_ref, gw_out, lr_out, en_out, gh_out, turned, dl, gw, in_sem, out_sem):
    lr_out[...] = lr_ref[...]
    en_out[...] = en_ref[...]
    gh_out[...] = gh_ref[...].astype(BF16)
    dl_copies = []
    for i in range(4):
        c = pltpu.make_async_copy(dl_hbm.at[pl.ds(64 * i, 64)], dl.at[pl.ds(64 * i, 64)], in_sem.at[i])
        c.start()
        dl_copies.append(c)

    def piece(ref, i):
        return ref.at[pl.ds(i * 256, 256)]

    def load(i):
        return pltpu.make_async_copy(piece(turned_hbm, i), piece(turned, i), in_sem.at[4 + i])

    def store(i):
        return pltpu.make_async_copy(piece(gw, i), piece(gw_out, i), out_sem.at[i])

    for i in range(8):
        load(i).start()
    for c in dl_copies:
        c.wait()
    for i in range(8):
        load(i).wait()
        piece(gw, i)[...] = jnp.dot(piece(turned, i)[...], dl[...], preferred_element_type=F32).astype(BF16)
        store(i).start()
    for i in range(8):
        store(i).wait()


def local(hidden, head, token_ids, old_logp, advantages, lengths):
    vmem = pl.BlockSpec(memory_space=pltpu.VMEM)
    hbm = pl.BlockSpec(memory_space=pltpu.HBM)
    dma = pltpu.SemaphoreType.DMA
    turned, dl, lr, en, gh = pl.pallas_call(
        main_kernel,
        out_shape=(
            jax.ShapeDtypeStruct((DEPTH, ROWS), BF16),
            jax.ShapeDtypeStruct((ROWS, COLS), BF16),
            jax.ShapeDtypeStruct((1, GROUP), F32),
            jax.ShapeDtypeStruct((1, GROUP), F32),
            jax.ShapeDtypeStruct((8, DEPTH), F32),
        ),
        in_specs=[hbm] * 6,
        out_specs=(hbm, hbm, vmem, vmem, vmem),
        scratch_shapes=[
            pltpu.SMEM((8,), jnp.int32),
            pltpu.VMEM((1, SLOTS), jnp.int32),
            pltpu.VMEM((1, SLOTS), F32),
            pltpu.VMEM((1, SLOTS), F32),
            pltpu.VMEM((4, GROUP, DEPTH), BF16),
            pltpu.VMEM((DEPTH, COLS), BF16),
            pltpu.VMEM((ROWS, DEPTH), BF16),
            pltpu.VMEM((NC, 2, 2, 64, CC), F32),
            pltpu.VMEM((NC, 2, 64, CC), F32),
            pltpu.VMEM((NC, 64, CC), F32),
            pltpu.VMEM((NC, 64, CC), F32),
            pltpu.VMEM((64, COLS), F32),
            pltpu.VMEM((NC, 2, 2, 64, CC), F32),
            pltpu.VMEM((8, 128), F32),
            pltpu.VMEM((8, 128), F32),
            pltpu.VMEM((4, 8, 128), F32),
            pltpu.VMEM((7, 8, 128), F32),
            pltpu.VMEM((7, 8, 128), F32),
            pltpu.VMEM((ROWS, COLS), BF16),
            pltpu.VMEM((ROWS, COLS), BF16),
            pltpu.VMEM((NT, ROWS, TF), BF16),
            pltpu.VMEM((NT, 7, 32, TF), BF16),
            pltpu.VMEM((NT, 128, 256), BF16),
            pltpu.VMEM((NT, 7, 16, 256), BF16),
            pltpu.VMEM((NT, 8, 16, 256), BF16),
            pltpu.VMEM((DEPTH, ROWS), BF16),
            dma((6,)), dma((1,)), dma((1,)), dma((2,)), dma((2,)), dma((2,)), dma((2,)),
            dma((2, 3)), dma((2, 3)), dma((2, 7)), dma((2, 7)),
            dma((NC,)), dma((NC,)), dma((NC,)), dma((NC,)),
            dma((7,)), dma((7,)), dma((7,)), dma((7,)),
            dma((NC,)), dma((NC,)), dma((NC,)), dma((NC,)), dma((NC,)), dma((NC,)), dma((3,)), dma((3,)),
            dma((NT, 7)), dma((NT, 7)), dma((NT, 7)), dma((NT, 7)), dma((NT, 7)), dma((NT, 7)), dma((2,)),
        ],
        compiler_params=pltpu.CompilerParams(
            collective_id=0, has_side_effects=True, vmem_limit_bytes=62 * 1024 * 1024
        ),
        name="main",
    )(lengths, token_ids[None], old_logp[None], advantages[None], hidden, head)
    gw, lr, en, gh = pl.pallas_call(
        head_kernel,
        out_shape=(
            jax.ShapeDtypeStruct((DEPTH, COLS), BF16),
            jax.ShapeDtypeStruct((1, GROUP), F32),
            jax.ShapeDtypeStruct((1, GROUP), F32),
            jax.ShapeDtypeStruct((8, DEPTH), BF16),
        ),
        in_specs=[hbm, hbm, vmem, vmem, vmem],
        out_specs=(hbm, vmem, vmem, vmem),
        scratch_shapes=[
            pltpu.VMEM((DEPTH, ROWS), BF16), pltpu.VMEM((ROWS, COLS), BF16), pltpu.VMEM((DEPTH, COLS), BF16),
            dma((12,)), dma((8,)),
        ],
        compiler_params=pltpu.CompilerParams(vmem_limit_bytes=62 * 1024 * 1024),
        name="head_grad",
    )(turned, dl, lr, en, gh)
    return lr[0], en[0], gh, gw


def solution(mesh):
    in_specs = (P("dp", None), P("dp", "vocab"), P(), P(), P(), P())
    out_specs = (P("dp"), P("dp"), P("vocab", "dp"), P("dp", "vocab"))
    return jax.shard_map(local, mesh=mesh, in_specs=in_specs, out_specs=out_specs, check_vma=False)
```

```python
import functools

import jax
import jax.numpy as jnp
from jax import lax
from jax.experimental import pallas as pl
from jax.experimental.pallas import tpu as pltpu
from jax.sharding import PartitionSpec as P

kl_weight = 0.2
entropy_weight = 0.1

F32 = jnp.float32
BF16 = jnp.bfloat16
MESH = pl.DeviceIdType.MESH

RESP = 64
SLOTS = 512
ROWS = 256
GROUP = 128
DEPTH = 2048
COLS = 1280
CC = 256
NC = COLS // CC
TF = 512
NT = DEPTH // TF
XF = 1152
ZF = 512
DF = DEPTH - XF - ZF


def iota(shape, dim):
    return lax.broadcasted_iota(jnp.int32, shape, dim)


def merge(parts):
    top = functools.reduce(jnp.maximum, [p[0:1] for p in parts])
    scales = [jnp.exp(p[0:1] - top) for p in parts]
    total = sum(p[1:2] * s for p, s in zip(parts, scales))
    weighted = sum(p[2:3] * s for p, s in zip(parts, scales))
    target = sum(p[3:4] for p in parts)
    return top, total, weighted, target


def plan_z(lens):
    ends = [0]
    for z in range(8):
        for x in range(4):
            ends.append(ends[-1] + jnp.clip(lens[2 * x + z // 4] - 16 * (z % 4), 0, 16))
    return ends


def plan_xy(lens):
    ends = [0]
    for m in range(8):
        for i in range(8):
            ends.append(ends[-1] + jnp.clip(lens[2 * (m // 2) + i // 4] - 16 * (i % 4) - 8 * (m % 2), 0, 8))
    return ends


def rank_of(lens, ends, slot, by_z):
    seq, pos = slot // RESP, slot % RESP
    if by_z:
        block, size = ((seq % 2) * 4 + pos // 16) * 4 + seq // 2, 16
    else:
        block, size = ((seq // 2) * 2 + (pos // 8) % 2) * 8 + (seq % 2) * 4 + pos // 16, 8
    first = jnp.zeros_like(slot)
    for b in range(1, len(ends) - 1):
        first = jnp.where(block == b, ends[b], first)
    length = jnp.zeros_like(slot)
    for s in range(8):
        length = jnp.where(seq == s, lens[s], length)
    return jnp.where(pos < length, first + pos % size, -1), length - pos


def row_of(rank):
    return jnp.where(rank >= 0, (rank % 8) * 32 + rank // 8, -1)


def onehot(mask):
    return mask.astype(F32).astype(BF16)


def main_kernel(
    len_hbm, tok_hbm, old_hbm, adv_hbm, hid_ref, head_ref,
    turned, dl_all, lr_out, en_out, gh_out,
    len_ref, tok_ref, old_ref, adv_ref,
    spread, head_v, comp, lp, rxc, sy, ryy, logit, lg, st1, st2, st3, stz, stxy, dl_z, part, rx1, s2, rx2, pack, give3, get3, pick_ref, order_ref, deal_ref, take_ref,
    loc_sem, hc_s, hc_r, hx_s, hx_r, hz_s, hz_r, hd_s, hd_r, fx_s, fx_r, fz_s, fz_r,
    lc_s, lc_r, ly_s, ly_r, z_s, z_r, xy_s, xy_r, gc_s, gc_r, gy_s, gy_r, gf_s, gf_r, m_s, m_r, a_s, a_r, b_s, b_r, g_s, g_r,
):
    dp = lax.axis_index("dp")
    v = lax.axis_index("vocab")
    y_hi, core = dp // 2, dp % 2
    x, z, y_lo = v // 16, (v // 2) % 8, v % 2
    m = x * 2 + y_lo

    def dp_id(d):
        return {"dp": d, "vocab": v}

    def z_id(k):
        return {"dp": dp, "vocab": x * 16 + ((z + k) % 8) * 2 + y_lo}

    def xy_id(k):
        q = (m + k) % 8
        return {"dp": dp, "vocab": (q // 2) * 16 + z * 2 + q % 2}

    def remote(src, dst, ss, rs, dev):
        return pltpu.make_async_remote_copy(
            src_ref=src, dst_ref=dst, send_sem=ss, recv_sem=rs, device_id=dev, device_id_type=MESH
        )

    small = [
        pltpu.make_async_copy(a, b, loc_sem.at[2 + i])
        for i, (a, b) in enumerate(((len_hbm, len_ref), (tok_hbm, tok_ref), (old_hbm, old_ref), (adv_hbm, adv_ref)))
    ]
    for c in small:
        c.start()

    barrier = pltpu.get_barrier_semaphore()
    for k in range(1, 4):
        pl.semaphore_signal(barrier, inc=1, device_id=dp_id((dp + k) % 4), device_id_type=MESH)
    for k in range(1, 8):
        pl.semaphore_signal(barrier, inc=1, device_id=z_id(k), device_id_type=MESH)
        pl.semaphore_signal(barrier, inc=1, device_id=xy_id(k), device_id_type=MESH)
    own_copy = pltpu.make_async_copy(
        hid_ref.at[:, pl.ds(pl.multiple_of(dp * DEPTH, DEPTH), DEPTH)], spread.at[dp], loc_sem.at[1]
    )
    own_copy.start()
    head_copy = pltpu.make_async_copy(head_ref, head_v, loc_sem.at[0])
    head_copy.start()
    pl.semaphore_wait(barrier, 17)

    z_rows = pl.ds(pl.multiple_of(16 * z, 16), 16)
    x_rows = pl.ds(pl.multiple_of(32 * x, 32), 32)
    z_cols, x_cols = pl.ds(XF, ZF), pl.ds(0, XF)

    def cross(c, sems, rows, start, size):
        d = (1 - y_hi) * 2 + c
        src = hid_ref.at[rows, pl.ds(pl.multiple_of(d * DEPTH + start, 128), size)]
        return remote(src, spread.at[dp, rows, pl.ds(start, size)], sems[0].at[c], sems[1].at[core], dp_id(d))

    def cross_x(c):
        return cross(c, (hx_s, hx_r), x_rows, 0, XF)

    def cross_z(c):
        return cross(c, (hz_s, hz_r), z_rows, XF, ZF)

    def cross_d(c):
        return cross(c, (hd_s, hd_r), pl.ds(0, GROUP), XF + ZF, DF)

    def landed(g, sems, rows, start, size):
        ref = spread.at[(1 - y_hi) * 2 + g, rows, pl.ds(start, size)]
        return remote(ref, ref, sems[0].at[g], sems[1].at[g], z_id(1))

    def near_core():
        d = y_hi * 2 + 1 - core
        src = hid_ref.at[:, pl.ds(pl.multiple_of(d * DEPTH, DEPTH), DEPTH)]
        return remote(src, spread.at[dp], hc_s.at[0], hc_r.at[0], dp_id(d))

    def pass_z(g, k):
        ref = spread.at[(1 - y_hi) * 2 + g, z_rows, z_cols]
        return remote(ref, ref, fz_s.at[g, k - 1], fz_r.at[g, k - 1], z_id(k))

    def pass_x(g, k):
        ref = spread.at[(1 - y_hi) * 2 + g, x_rows, x_cols]
        return remote(ref, ref, fx_s.at[g, k - 1], fx_r.at[g, k - 1], xy_id(2 * k))

    for c in (0, 1):
        cross_x(c).start()
        cross_z(c).start()
    near_core().start()
    for c in (0, 1):
        cross_d(c).start()

    for c in small:
        c.wait()
    lens = [len_ref[s] for s in range(8)]
    ends_z, ends_xy = plan_z(lens), plan_xy(lens)
    slots = iota((1, SLOTS), 1)
    row_z = row_of(rank_of(lens, ends_z, slots, True)[0])
    hits = row_z == iota((ROWS, SLOTS), 0)
    pick_ref[...] = onehot(hits)
    pick_xy = onehot(row_of(rank_of(lens, ends_xy, slots, False)[0]) == iota((ROWS, SLOTS), 0))
    order_ref[...] = lax.dot_general(
        pick_xy, pick_ref[...], (((1,), (1,)), ((), ())), preferred_element_type=F32
    ).astype(BF16)
    tok = jnp.sum(jnp.where(hits, tok_ref[...], 0), axis=1, keepdims=True)
    base = 128 * y_hi + 64 * core
    my_mask = row_z == base + iota((64, SLOTS), 0)
    my_tok = jnp.sum(jnp.where(my_mask, tok_ref[...], 0), axis=1, keepdims=True)
    old = jnp.sum(jnp.where(my_mask, old_ref[...], 0.0), axis=1, keepdims=True)
    adv = jnp.sum(jnp.where(my_mask, adv_ref[...], 0.0), axis=1, keepdims=True)

    class By:
        pass

    by_xy, by_z = By(), By()
    by_xy.me, by_xy.peer, by_xy.other, by_xy.across = m, xy_id, z, z_id
    by_z.me, by_z.peer, by_z.other, by_z.across = z, z_id, m, xy_id
    by_xy.rank = lambda slot: rank_of(lens, ends_z, slot, True)
    by_z.rank = lambda slot: rank_of(lens, ends_xy, slot, False)
    by_xy.slot = lambda second, first: 128 * (first // 2) + 16 * second + 8 * (first % 2)
    by_z.slot = lambda second, first: 128 * (second // 2) + 16 * first + 8 * (second % 2)
    for i, by in enumerate((by_xy, by_z)):
        col = iota((128, 1), 0)
        first, left = by.rank(by.slot(col // 16, col % 8))
        rank = first + (by.me - first) % 8
        row = rank // 8 + 32 * ((col // 8) % 2)
        row = jnp.where((first >= 0) & (rank < first + jnp.minimum(left, 8)), row, -1)
        deal_ref[i] = onehot(row == iota((128, 64), 1))
        rank, _ = by.rank(by.slot(by.other, by.me) + col // 16)
        place = ((by.me - rank) % 8) * 16 + col % 16
        take_ref[i] = onehot(jnp.where(rank >= 0, place, -1) == iota((128, 128), 1))

    for g in (0, 1):
        landed(g, (hx_s, hx_r), x_rows, 0, XF).wait_recv()
        for k in range(1, 4):
            pass_x(g, k).start()
        landed(g, (hz_s, hz_r), z_rows, XF, ZF).wait_recv()
        for k in range(1, 8):
            pass_z(g, k).start()

    own_copy.wait()
    near_core().wait()

    def compact(half, first):
        def step(t, _):
            cols = pl.ds(pl.multiple_of(t * 512, 512), 512)
            full = spread[pl.ds(2 * half, 2), :, cols].reshape(256, 512)
            mine = pick_ref[:, pl.ds(pl.multiple_of(half * 256, 256), 256)]
            rows = jnp.dot(mine, full, preferred_element_type=F32).astype(BF16)
            comp[:, cols] = rows if first else comp[:, cols] + rows
            return 0

        lax.fori_loop(0, DEPTH // 512, step, 0)

    compact(y_hi, True)
    head_copy.wait()
    for g in (0, 1):
        cross_z(g).wait_send()
        cross_x(g).wait_send()
        cross_d(g).wait_send()
        landed(g, (hd_s, hd_r), pl.ds(0, GROUP), XF + ZF, DF).wait_recv()
        for k in range(1, 8):
            pass_z(g, k).wait()
        for k in range(1, 4):
            pass_x(g, k).wait()
    compact(1 - y_hi, False)

    def core_copy(j):
        return remote(
            lp.at[j, :, 1 - core], rxc.at[j],
            lc_s.at[j], lc_r.at[j], dp_id(y_hi * 2 + 1 - core),
        )

    def y_copy(j):
        return remote(sy.at[j], ryy.at[j], ly_s.at[j], ly_r.at[j], dp_id((1 - y_hi) * 2 + core))

    def chip_sum(j):
        core_copy(j).wait()
        sy[j] = lp[j, 1 - y_hi, core] + rxc[j, 1 - y_hi]
        y_copy(j).start()
        cols = pl.ds(pl.multiple_of(j * CC, CC), CC)
        logit[:, cols] = lp[j, y_hi, core] + rxc[j, y_hi]

    def product(j, _):
        cols = pl.ds(pl.multiple_of(j * CC, CC), CC)
        lp[j] = jnp.dot(comp[...], head_v[:, cols], preferred_element_type=F32).reshape(2, 2, 64, CC)
        core_copy(j).start()

        @pl.when(j > 0)
        def _():
            chip_sum(j - 1)

        return 0

    lax.fori_loop(0, NC, product, 0)
    chip_sum(NC - 1)

    y_dev, c_dev = dp_id((1 - y_hi) * 2 + core), dp_id(y_hi * 2 + 1 - core)

    def give(j, sems, dev, side):
        ref = lg.at[j, side, core]
        return remote(ref, ref, sems[0].at[j], sems[1].at[j], dev)

    def full_sum(j, _):
        y_copy(j).wait()
        cols = pl.ds(pl.multiple_of(j * CC, CC), CC)
        l = logit[:, cols] + ryy[j]
        logit[:, cols] = l
        lg[j, y_hi, core] = l
        give(j, (gy_s, gy_r), y_dev, y_hi).start()
        give(j, (gc_s, gc_r), c_dev, y_hi).start()
        return 0

    lax.fori_loop(0, NC, full_sum, 0)

    eye = iota((64, 128), 0) == iota((64, 128), 1)

    def to_row(col):
        return jnp.sum(jnp.where(eye, col, 0.0), axis=0, keepdims=True)

    def to_col(row):
        return jnp.sum(jnp.where(eye, row, 0.0), axis=1, keepdims=True)

    l = logit[...]
    hit = iota((64, COLS), 1) == my_tok - v * COLS
    top = jnp.max(l, axis=1, keepdims=True)
    e = jnp.exp(l - top)
    st1[...] = jnp.concatenate(
        [
            to_row(top),
            to_row(jnp.sum(e, axis=1, keepdims=True)),
            to_row(jnp.sum(e * l, axis=1, keepdims=True)),
            to_row(jnp.sum(jnp.where(hit, l, 0.0), axis=1, keepdims=True)),
            jnp.zeros((4, 128), F32),
        ],
        axis=0,
    )

    def z_copy(k):
        return remote(st1, stz.at[k - 1], z_s.at[k - 1], z_r.at[k - 1], z_id(k))

    def xy_copy(k):
        return remote(st2, stxy.at[k - 1], xy_s.at[k - 1], xy_r.at[k - 1], xy_id(k))

    for k in range(1, 8):
        z_copy(k).start()

    def turn(t, _):
        cols = pl.ds(pl.multiple_of(t * 256, 256), 256)
        turned[cols, :] = comp[:, cols].astype(F32).T.astype(BF16)
        return 0

    lax.fori_loop(0, DEPTH // 256, turn, 0)
    for k in range(1, 8):
        z_copy(k).wait()
    st2[...] = jnp.concatenate(
        list(merge([st1[...]] + [stz[k] for k in range(7)])) + [jnp.zeros((4, 128), F32)], axis=0
    )
    for k in range(1, 8):
        xy_copy(k).start()

    def forward(j, _):
        give(j, (gy_s, gy_r), y_dev, 1 - y_hi).wait_recv()
        give(j, (gf_s, gf_r), c_dev, 1 - y_hi).start()
        return 0

    lax.fori_loop(0, NC, forward, 0)
    for k in range(1, 8):
        xy_copy(k).wait()
    top, total, weighted, target = merge([st2[...]] + [stxy[k] for k in range(7)])
    lse_row = top + jnp.log(total)
    entropy_row = lse_row - weighted / total
    ratio_row = target - lse_row - to_row(old)
    slope_row = (kl_weight - to_row(adv)) * jnp.exp(ratio_row) - kl_weight
    st3[0] = jnp.concatenate([lse_row, entropy_row, ratio_row, slope_row, jnp.zeros((4, 128), F32)], axis=0)

    def row_copy(k):
        return remote(st3.at[0], st3.at[k], m_s.at[k - 1], m_r.at[k - 1], dp_id((dp + k) % 4))

    for k in range(1, 4):
        row_copy(k).start()

    def arrive(j, _):
        give(j, (gc_s, gc_r), c_dev, y_hi).wait()
        give(j, (gf_s, gf_r), c_dev, 1 - y_hi).wait()
        give(j, (gy_s, gy_r), y_dev, y_hi).wait_send()
        return 0

    lax.fori_loop(0, NC, arrive, 0)
    for k in range(1, 4):
        row_copy(k).wait()

    lse, entropy, log_ratio, slope = [
        jnp.concatenate([to_col(st3[(dp - d) % 4][i : i + 1]) for d in range(4)], axis=0) for i in range(4)
    ]

    def gradient(j, _):
        l = lg[j].reshape(ROWS, CC)
        hit = iota((ROWS, CC), 1) == tok - (v * COLS + j * CC)
        shifted = l - lse
        probs = jnp.exp(shifted)
        grad = slope * (hit.astype(F32) - probs) + entropy_weight * probs * (shifted + entropy)
        dl_all[:, pl.ds(pl.multiple_of(j * CC, CC), CC)] = grad.astype(BF16)
        return 0

    lax.fori_loop(0, NC, gradient, 0)

    by_xy.rows, by_z.rows = dl_all, dl_z
    by_xy.deal, by_xy.take, by_xy.pack, by_xy.give, by_xy.get = deal_ref.at[0], take_ref.at[0], pack.at[0], give3.at[0], get3.at[0]
    by_z.deal, by_z.take, by_z.pack, by_z.give, by_z.get = deal_ref.at[1], take_ref.at[1], pack.at[1], give3.at[1], get3.at[1]
    by_xy.s, by_xy.r, by_z.s, by_z.r = g_s.at[0], g_r.at[0], g_s.at[1], g_r.at[1]

    def first_copy(t, k, by):
        q = (by.me + k) % 8
        return remote(
            part.at[t, pl.ds(pl.multiple_of(q * 32, 32), 32)], rx1.at[t, k - 1],
            a_s.at[t, k - 1], a_r.at[t, k - 1], by.peer(k),
        )

    def partial(t, by):
        for h in range(TF // 256):
            part[t, :, h * 256 : h * 256 + 256] = lax.dot_general(
                by.rows[...], head_v[t * TF + h * 256 : t * TF + h * 256 + 256, :], (((1,), (1,)), ((), ())),
                preferred_element_type=F32,
            ).astype(BF16)

        def send(k, _):
            first_copy(t, k, by).start()
            return 0

        lax.fori_loop(1, 8, send, 0)

    order = [(0, by_xy), (3, by_z), (1, by_xy), (2, by_xy)]
    for t, by in order:
        if by is by_z:
            def reorder(j, _):
                cols = pl.ds(pl.multiple_of(j * CC, CC), CC)
                dl_z[:, cols] = jnp.dot(order_ref[...], dl_all[:, cols], preferred_element_type=F32).astype(BF16)
                return 0

            lax.fori_loop(0, NC, reorder, 0)
        partial(t, by)

    mask = row_of(rank_of(lens, ends_z, dp * GROUP + iota((1, GROUP), 1), True)[0]) == iota((ROWS, GROUP), 0)
    lr_out[...] = jnp.sum(jnp.where(mask, log_ratio, 0.0), axis=0, keepdims=True)
    en_out[...] = jnp.sum(jnp.where(mask, entropy, 0.0), axis=0, keepdims=True)

    def second_copy(t, k, by):
        q = (by.other + k) % 8
        return remote(
            s2.at[t, pl.ds(pl.multiple_of(q * 16, 16), 16)], rx2.at[t, k - 1],
            b_s.at[t, k - 1], b_r.at[t, k - 1], by.across(k),
        )

    def third_copy(k, by):
        return remote(by.give.at[(by.me + k) % 8], by.get.at[k], by.s.at[k - 1], by.r.at[k - 1], by.peer(k))

    def each(make):
        def step(k, _):
            make(k)
            return 0

        lax.fori_loop(1, 8, step, 0)

    for t, by in order:
        each(lambda k: first_copy(t, k, by).wait())
        acc = part[t, pl.ds(pl.multiple_of(by.me * 32, 32), 32)].astype(F32)
        for k in range(7):
            acc = acc + rx1[t, k].astype(F32)
        both = jnp.concatenate([acc[:, 0:256], acc[:, 256:512]], axis=0).astype(BF16)
        s2[t] = jnp.dot(by.deal[...], both, preferred_element_type=F32).astype(BF16)
        each(lambda k: second_copy(t, k, by).start())

    pack[...] = jnp.zeros_like(pack)
    by_xy.done, by_xy.tiles, by_xy.count = 0, [], 3
    by_z.done, by_z.tiles, by_z.count = 0, [], 1
    for t, by in order:
        each(lambda k: second_copy(t, k, by).wait())
        acc = s2[t, pl.ds(pl.multiple_of(by.other * 16, 16), 16)].astype(F32)
        for k in range(7):
            acc = acc + rx2[t, k].astype(F32)
        for h in range(2):
            for e in range(2):
                by.pack[:, 4 * by.done + 2 * h + e, :] = acc[8 * h : 8 * h + 8, 128 * e : 128 * e + 128]
        by.tiles.append(t)
        by.done += 1
        if by.done == by.count:
            by.give[...] = by.pack[...].astype(BF16)
            each(lambda k: third_copy(k, by).start())

    for by in (by_z, by_xy):
        by.get[0] = by.give[by.me]
        each(lambda k: third_copy(k, by).wait())
        rows = jnp.dot(by.take[...], by.get[...].reshape(128, 128), preferred_element_type=F32)
        by.pack[...] = rows.reshape(8, 16, 128)
        for i, t in enumerate(by.tiles):
            for c in range(4):
                gh_out[:, t * TF + c * 128 : t * TF + c * 128 + 128] = by.pack[:, 4 * i + c, :]


def head_kernel(turned, dl, lr_ref, en_ref, gh_ref, gw_out, lr_out, en_out, gh_out, gw, out_sem):
    def piece(ref, i):
        return ref.at[pl.ds(i * 256, 256)]

    def store(i):
        return pltpu.make_async_copy(piece(gw, i), piece(gw_out, i), out_sem.at[i])

    for i in range(8):
        piece(gw, i)[...] = jnp.dot(piece(turned, i)[...], dl[...], preferred_element_type=F32).astype(BF16)
        store(i).start()
    lr_out[...] = lr_ref[...]
    en_out[...] = en_ref[...]
    gh_out[...] = gh_ref[...].astype(BF16)
    for i in range(8):
        store(i).wait()


def local(hidden, head, token_ids, old_logp, advantages, lengths):
    vmem = pl.BlockSpec(memory_space=pltpu.VMEM)
    hbm = pl.BlockSpec(memory_space=pltpu.HBM)
    dma = pltpu.SemaphoreType.DMA
    keep = pltpu.with_memory_space_constraint
    turned, dl, lr, en, gh = pl.pallas_call(
        main_kernel,
        out_shape=(
            pltpu.VMEM((DEPTH, ROWS), BF16),
            pltpu.VMEM((ROWS, COLS), BF16),
            pltpu.VMEM((1, GROUP), F32),
            pltpu.VMEM((1, GROUP), F32),
            pltpu.VMEM((8, DEPTH), F32),
        ),
        in_specs=[hbm] * 6,
        out_specs=(vmem,) * 5,
        scratch_shapes=[
            pltpu.SMEM((8,), jnp.int32),
            pltpu.VMEM((1, SLOTS), jnp.int32),
            pltpu.VMEM((1, SLOTS), F32),
            pltpu.VMEM((1, SLOTS), F32),
            pltpu.VMEM((4, GROUP, DEPTH), BF16),
            pltpu.VMEM((DEPTH, COLS), BF16),
            pltpu.VMEM((ROWS, DEPTH), BF16),
            pltpu.VMEM((NC, 2, 2, 64, CC), F32),
            pltpu.VMEM((NC, 2, 64, CC), F32),
            pltpu.VMEM((NC, 64, CC), F32),
            pltpu.VMEM((NC, 64, CC), F32),
            pltpu.VMEM((64, COLS), F32),
            pltpu.VMEM((NC, 2, 2, 64, CC), F32),
            pltpu.VMEM((8, 128), F32),
            pltpu.VMEM((8, 128), F32),
            pltpu.VMEM((4, 8, 128), F32),
            pltpu.VMEM((7, 8, 128), F32),
            pltpu.VMEM((7, 8, 128), F32),
            pltpu.VMEM((ROWS, COLS), BF16),
            pltpu.VMEM((NT, ROWS, TF), BF16),
            pltpu.VMEM((NT, 7, 32, TF), BF16),
            pltpu.VMEM((NT, 128, 256), BF16),
            pltpu.VMEM((NT, 7, 16, 256), BF16),
            pltpu.VMEM((2, 8, 16, 128), F32),
            pltpu.VMEM((2, 8, 16, 128), BF16),
            pltpu.VMEM((2, 8, 16, 128), BF16),
            pltpu.VMEM((ROWS, SLOTS), BF16),
            pltpu.VMEM((ROWS, ROWS), BF16),
            pltpu.VMEM((2, 128, 64), BF16),
            pltpu.VMEM((2, 128, 128), BF16),
            dma((6,)), dma((1,)), dma((1,)), dma((2,)), dma((2,)), dma((2,)), dma((2,)), dma((2,)), dma((2,)),
            dma((2, 3)), dma((2, 3)), dma((2, 7)), dma((2, 7)),
            dma((NC,)), dma((NC,)), dma((NC,)), dma((NC,)),
            dma((7,)), dma((7,)), dma((7,)), dma((7,)),
            dma((NC,)), dma((NC,)), dma((NC,)), dma((NC,)), dma((NC,)), dma((NC,)), dma((3,)), dma((3,)),
            dma((NT, 7)), dma((NT, 7)), dma((NT, 7)), dma((NT, 7)), dma((2, 7)), dma((2, 7)),
        ],
        compiler_params=pltpu.CompilerParams(
            collective_id=0, has_side_effects=True, vmem_limit_bytes=48 * 1024 * 1024
        ),
        name="main",
    )(*[keep(a, pltpu.HBM) for a in (lengths, token_ids[None], old_logp[None], advantages[None], hidden, head)])
    gw, lr, en, gh = pl.pallas_call(
        head_kernel,
        out_shape=(
            jax.ShapeDtypeStruct((DEPTH, COLS), BF16),
            jax.ShapeDtypeStruct((1, GROUP), F32),
            jax.ShapeDtypeStruct((1, GROUP), F32),
            jax.ShapeDtypeStruct((8, DEPTH), BF16),
        ),
        in_specs=[vmem] * 5,
        out_specs=(hbm, vmem, vmem, vmem),
        scratch_shapes=[
            pltpu.VMEM((DEPTH, COLS), BF16), dma((8,)),
        ],
        compiler_params=pltpu.CompilerParams(vmem_limit_bytes=40 * 1024 * 1024),
        name="head_grad",
    )(*[keep(a, pltpu.VMEM) for a in (turned, dl, lr, en, gh)])
    return lr[0], en[0], gh, gw


def solution(mesh):
    in_specs = (P("dp", None), P("dp", "vocab"), P(), P(), P(), P())
    out_specs = (P("dp"), P("dp"), P("vocab", "dp"), P("dp", "vocab"))
    return jax.shard_map(local, mesh=mesh, in_specs=in_specs, out_specs=out_specs, check_vma=False)
```

```python
import functools

import jax
import jax.numpy as jnp
from jax import lax
from jax.experimental import pallas as pl
from jax.experimental.pallas import tpu as pltpu
from jax.sharding import PartitionSpec as P

kl_weight = 0.2
entropy_weight = 0.1

F32 = jnp.float32
BF16 = jnp.bfloat16
MESH = pl.DeviceIdType.MESH

RESP = 64
SLOTS = 512
ROWS = 256
GROUP = 128
DEPTH = 2048
COLS = 1280
CC = 256
NC = COLS // CC
TF = 512
NT = DEPTH // TF
XF = 1024
ZF = 512
DF = DEPTH - XF - ZF
XH = XF // 2


def iota(shape, dim):
    return lax.broadcasted_iota(jnp.int32, shape, dim)


def merge(parts):
    top = functools.reduce(jnp.maximum, [p[0:1] for p in parts])
    scales = [jnp.exp(p[0:1] - top) for p in parts]
    total = sum(p[1:2] * s for p, s in zip(parts, scales))
    weighted = sum(p[2:3] * s for p, s in zip(parts, scales))
    target = sum(p[3:4] for p in parts)
    return top, total, weighted, target


def plan_z(lens):
    ends = [0]
    for z in range(8):
        for x in range(4):
            ends.append(ends[-1] + jnp.clip(lens[2 * x + z // 4] - 16 * (z % 4), 0, 16))
    return ends


def plan_xy(lens):
    ends = [0]
    for m in range(8):
        for i in range(8):
            ends.append(ends[-1] + jnp.clip(lens[2 * (m // 2) + i // 4] - 16 * (i % 4) - 8 * (m % 2), 0, 8))
    return ends


def rank_of(lens, ends, slot, by_z):
    seq, pos = slot // RESP, slot % RESP
    if by_z:
        block, size = ((seq % 2) * 4 + pos // 16) * 4 + seq // 2, 16
    else:
        block, size = ((seq // 2) * 2 + (pos // 8) % 2) * 8 + (seq % 2) * 4 + pos // 16, 8
    first = jnp.zeros_like(slot)
    for b in range(1, len(ends) - 1):
        first = jnp.where(block == b, ends[b], first)
    length = jnp.zeros_like(slot)
    for s in range(8):
        length = jnp.where(seq == s, lens[s], length)
    return jnp.where(pos < length, first + pos % size, -1), length - pos


def row_of(rank):
    return jnp.where(rank >= 0, (rank % 8) * 32 + rank // 8, -1)


def onehot(mask):
    return mask.astype(F32).astype(BF16)


def main_kernel(
    len_hbm, tok_hbm, old_hbm, adv_hbm, hid_ref, head_ref,
    gw, lr_out, en_out, gh_out,
    len_ref, tok_ref, old_ref, adv_ref,
    spread, head_v, comp, lp, rxc, sy, ryy, logit, lg, st1, st2, stz, stxy, turned, dl_all, dl_z, part, rx1, s2, rx2, pack, give3, get3, pick_ref, order_ref, deal_ref, take_ref,
    loc_sem, hc_s, hc_r, hx_s, hx_r, hz_s, hz_r, hd_s, hd_r, fx_s, fx_r, fz_s, fz_r,
    lc_s, lc_r, ly_s, ly_r, z_s, z_r, xy_s, xy_r, gc_s, gc_r, gy_s, gy_r, gf_s, gf_r, a_s, a_r, b_s, b_r, g_s, g_r,
):
    dp = lax.axis_index("dp")
    v = lax.axis_index("vocab")
    y_hi, core = dp // 2, dp % 2
    x, z, y_lo = v // 16, (v // 2) % 8, v % 2
    m = x * 2 + y_lo

    def dp_id(d):
        return {"dp": d, "vocab": v}

    def z_id(k, far=False):
        return {"dp": y_hi * 2 + 1 - core if far else dp, "vocab": x * 16 + ((z + k) % 8) * 2 + y_lo}

    def xy_id(k, far=False):
        q = (m + k) % 8
        return {"dp": (1 - y_hi) * 2 + core if far else dp, "vocab": (q // 2) * 16 + z * 2 + q % 2}

    def remote(src, dst, ss, rs, dev):
        return pltpu.make_async_remote_copy(
            src_ref=src, dst_ref=dst, send_sem=ss, recv_sem=rs, device_id=dev, device_id_type=MESH
        )

    small = [
        pltpu.make_async_copy(a, b, loc_sem.at[2 + i])
        for i, (a, b) in enumerate(((len_hbm, len_ref), (tok_hbm, tok_ref), (old_hbm, old_ref), (adv_hbm, adv_ref)))
    ]
    for c in small:
        c.start()

    barrier = pltpu.get_barrier_semaphore()
    for k in range(1, 4):
        pl.semaphore_signal(barrier, inc=1, device_id=dp_id((dp + k) % 4), device_id_type=MESH)
    for k in range(1, 8):
        for far in (False, True):
            pl.semaphore_signal(barrier, inc=1, device_id=z_id(k, far), device_id_type=MESH)
            pl.semaphore_signal(barrier, inc=1, device_id=xy_id(k, far), device_id_type=MESH)
    own_copy = pltpu.make_async_copy(
        hid_ref.at[:, pl.ds(pl.multiple_of(dp * DEPTH, DEPTH), DEPTH)], spread.at[dp], loc_sem.at[1]
    )
    own_copy.start()
    head_copy = pltpu.make_async_copy(head_ref, head_v, loc_sem.at[0])
    head_copy.start()
    pl.semaphore_wait(barrier, 31)

    z_rows = pl.ds(pl.multiple_of(16 * z, 16), 16)
    x_rows = pl.ds(pl.multiple_of(32 * x, 32), 32)
    z_cols = pl.ds(XF, ZF)

    def cross(c, sems, rows, start, size):
        d = (1 - y_hi) * 2 + c
        src = hid_ref.at[rows, pl.ds(pl.multiple_of(d * DEPTH + start, 128), size)]
        return remote(src, spread.at[dp, rows, pl.ds(start, size)], sems[0].at[c], sems[1].at[core], dp_id(d))

    def cross_x(c, w):
        return cross(c, (hx_s.at[w], hx_r.at[w]), x_rows, w * XH, XH)

    def cross_z(c):
        return cross(c, (hz_s, hz_r), z_rows, XF, ZF)

    def cross_d(c):
        return cross(c, (hd_s, hd_r), pl.ds(0, GROUP), XF + ZF, DF)

    def landed(g, sems, rows, start, size):
        ref = spread.at[(1 - y_hi) * 2 + g, rows, pl.ds(start, size)]
        return remote(ref, ref, sems[0].at[g], sems[1].at[g], z_id(1))

    def near_core():
        d = y_hi * 2 + 1 - core
        src = hid_ref.at[:, pl.ds(pl.multiple_of(d * DEPTH, DEPTH), DEPTH)]
        return remote(src, spread.at[dp], hc_s.at[0], hc_r.at[0], dp_id(d))

    def pass_z(g, k):
        ref = spread.at[(1 - y_hi) * 2 + g, z_rows, z_cols]
        return remote(ref, ref, fz_s.at[g, k - 1], fz_r.at[g, k - 1], z_id(k))

    def pass_x(g, k, w):
        ref = spread.at[(1 - y_hi) * 2 + g, x_rows, pl.ds(w * XH, XH)]
        return remote(ref, ref, fx_s.at[w, g, k - 1], fx_r.at[w, g, k - 1], xy_id(2 * k))

    for c in (0, 1):
        cross_x(c, 0).start()
    for c in (0, 1):
        cross_z(c).start()
    for c in (0, 1):
        cross_x(c, 1).start()
    near_core().start()
    for c in (0, 1):
        cross_d(c).start()

    for c in small:
        c.wait()
    lens = [len_ref[s] for s in range(8)]
    ends_z, ends_xy = plan_z(lens), plan_xy(lens)
    slots = iota((1, SLOTS), 1)
    row_z = row_of(rank_of(lens, ends_z, slots, True)[0])
    hits = row_z == iota((ROWS, SLOTS), 0)
    pick_ref[...] = onehot(hits)
    pick_xy = onehot(row_of(rank_of(lens, ends_xy, slots, False)[0]) == iota((ROWS, SLOTS), 0))
    order_ref[...] = lax.dot_general(
        pick_xy, pick_ref[...], (((1,), (1,)), ((), ())), preferred_element_type=F32
    ).astype(BF16)
    tok = jnp.sum(jnp.where(hits, tok_ref[...], 0), axis=1, keepdims=True)
    base = 128 * y_hi + 64 * core
    my_mask = row_z == base + iota((64, SLOTS), 0)
    my_tok = jnp.sum(jnp.where(my_mask, tok_ref[...], 0), axis=1, keepdims=True)
    old = jnp.sum(jnp.where(hits, old_ref[...], 0.0), axis=1, keepdims=True)
    adv = jnp.sum(jnp.where(hits, adv_ref[...], 0.0), axis=1, keepdims=True)

    class By:
        pass

    by_xy, by_z = By(), By()
    by_xy.me, by_xy.peer, by_xy.other, by_xy.across = m, xy_id, z, z_id
    by_z.me, by_z.peer, by_z.other, by_z.across = z, z_id, m, xy_id
    by_xy.rank = lambda slot: rank_of(lens, ends_z, slot, True)
    by_z.rank = lambda slot: rank_of(lens, ends_xy, slot, False)
    by_xy.slot = lambda second, first: 128 * (first // 2) + 16 * second + 8 * (first % 2)
    by_z.slot = lambda second, first: 128 * (second // 2) + 16 * first + 8 * (second % 2)
    for i, by in enumerate((by_xy, by_z)):
        col = iota((128, 1), 0)
        first, left = by.rank(by.slot(col // 16, col % 8))
        rank = first + (by.me - first) % 8
        row = rank // 8 + 32 * ((col // 8) % 2)
        row = jnp.where((first >= 0) & (rank < first + jnp.minimum(left, 8)), row, -1)
        deal_ref[i] = onehot(row == iota((128, 64), 1))
        rank, _ = by.rank(by.slot(by.other, by.me) + col // 16)
        place = ((by.me - rank) % 8) * 16 + col % 16
        take_ref[i] = onehot(jnp.where(rank >= 0, place, -1) == iota((128, 128), 1))

    def pass_half(w):
        for g in (0, 1):
            landed(g, (hx_s.at[w], hx_r.at[w]), x_rows, w * XH, XH).wait_recv()
            for k in (2, 1, 3):
                pass_x(g, k, w).start()

    pass_half(0)
    for g in (0, 1):
        landed(g, (hz_s, hz_r), z_rows, XF, ZF).wait_recv()
        for k in (4, 3, 5, 2, 6, 1, 7):
            pass_z(g, k).start()
    pass_half(1)

    own_copy.wait()
    near_core().wait()

    def compact(half, first):
        def step(t, _):
            cols = pl.ds(pl.multiple_of(t * 512, 512), 512)
            full = spread[pl.ds(2 * half, 2), :, cols].reshape(256, 512)
            mine = pick_ref[:, pl.ds(pl.multiple_of(half * 256, 256), 256)]
            rows = jnp.dot(mine, full, preferred_element_type=F32).astype(BF16)
            comp[:, cols] = rows if first else comp[:, cols] + rows
            return 0

        lax.fori_loop(0, DEPTH // 512, step, 0)

    compact(y_hi, True)
    head_copy.wait()
    for g in (0, 1):
        cross_z(g).wait_send()
        cross_x(g, 0).wait_send()
        cross_x(g, 1).wait_send()
        cross_d(g).wait_send()
        landed(g, (hd_s, hd_r), pl.ds(0, GROUP), XF + ZF, DF).wait_recv()
        for k in range(1, 8):
            pass_z(g, k).wait()
        for k in range(1, 4):
            pass_x(g, k, 0).wait()
            pass_x(g, k, 1).wait()
    compact(1 - y_hi, False)

    def core_copy(j):
        return remote(
            lp.at[j, :, 1 - core], rxc.at[j],
            lc_s.at[j], lc_r.at[j], dp_id(y_hi * 2 + 1 - core),
        )

    def y_copy(j):
        return remote(sy.at[j], ryy.at[j], ly_s.at[j], ly_r.at[j], dp_id((1 - y_hi) * 2 + core))

    def chip_sum(j):
        core_copy(j).wait()
        sy[j] = lp[j, 1 - y_hi, core] + rxc[j, 1 - y_hi]
        y_copy(j).start()
        cols = pl.ds(pl.multiple_of(j * CC, CC), CC)
        logit[:, cols] = lp[j, y_hi, core] + rxc[j, y_hi]

    def product(j, _):
        cols = pl.ds(pl.multiple_of(j * CC, CC), CC)
        lp[j] = jnp.dot(comp[...], head_v[:, cols], preferred_element_type=F32).reshape(2, 2, 64, CC)
        core_copy(j).start()

        @pl.when(j > 0)
        def _():
            chip_sum(j - 1)

        return 0

    lax.fori_loop(0, NC, product, 0)
    chip_sum(NC - 1)

    y_dev, c_dev = dp_id((1 - y_hi) * 2 + core), dp_id(y_hi * 2 + 1 - core)

    def give(j, sems, dev, side):
        ref = lg.at[j, side, core]
        return remote(ref, ref, sems[0].at[j], sems[1].at[j], dev)

    def full_sum(j, _):
        y_copy(j).wait()
        cols = pl.ds(pl.multiple_of(j * CC, CC), CC)
        l = logit[:, cols] + ryy[j]
        logit[:, cols] = l
        lg[j, y_hi, core] = l
        give(j, (gy_s, gy_r), y_dev, y_hi).start()
        give(j, (gc_s, gc_r), c_dev, y_hi).start()
        return 0

    lax.fori_loop(0, NC, full_sum, 0)

    eye = iota((64, 128), 0) + 64 * core == iota((64, 128), 1)
    eye_all = iota((128, 128), 0) == iota((128, 128), 1)

    def to_row(col):
        return jnp.sum(jnp.where(eye, col, 0.0), axis=0, keepdims=True)

    def to_col(row):
        return jnp.sum(jnp.where(eye_all, row, 0.0), axis=1, keepdims=True)

    l = logit[...]
    hit = iota((64, COLS), 1) == my_tok - v * COLS
    top = jnp.max(l, axis=1, keepdims=True)
    e = jnp.exp(l - top)
    st1[...] = jnp.concatenate(
        [
            jnp.max(jnp.where(eye, top, -1e30), axis=0, keepdims=True),
            to_row(jnp.sum(e, axis=1, keepdims=True)),
            to_row(jnp.sum(e * l, axis=1, keepdims=True)),
            to_row(jnp.sum(jnp.where(hit, l, 0.0), axis=1, keepdims=True)),
            jnp.zeros((4, 128), F32),
        ],
        axis=0,
    )

    def z_copy(i):
        k, far = (i + 1, False) if i < 7 else (i - 7, True)
        return remote(st1, stz.at[i], z_s.at[i], z_r.at[i], z_id(k, far))

    def xy_copy(i):
        k, far = (i + 1, False) if i < 7 else (i - 7, True)
        return remote(st2, stxy.at[i], xy_s.at[i], xy_r.at[i], xy_id(k, far))

    for i in range(15):
        z_copy(i).start()

    def turn(t, _):
        cols = pl.ds(pl.multiple_of(t * 256, 256), 256)
        turned[cols, :] = comp[:, cols].astype(F32).T.astype(BF16)
        return 0

    lax.fori_loop(0, DEPTH // 256, turn, 0)
    for i in range(15):
        z_copy(i).wait()
    st2[...] = jnp.concatenate(
        list(merge([st1[...]] + [stz[i] for i in range(15)])) + [jnp.zeros((4, 128), F32)], axis=0
    )
    for i in range(15):
        xy_copy(i).start()

    def forward(j, _):
        give(j, (gy_s, gy_r), y_dev, 1 - y_hi).wait_recv()
        give(j, (gf_s, gf_r), c_dev, 1 - y_hi).start()
        return 0

    lax.fori_loop(0, NC, forward, 0)
    def arrive(j, _):
        give(j, (gc_s, gc_r), c_dev, y_hi).wait()
        give(j, (gf_s, gf_r), c_dev, 1 - y_hi).wait()
        give(j, (gy_s, gy_r), y_dev, y_hi).wait_send()
        return 0

    lax.fori_loop(0, NC, arrive, 0)
    for i in range(15):
        xy_copy(i).wait()

    def row_values(parts):
        top, total, weighted, target = merge(parts)
        lse = top + jnp.log(total)
        return lse, lse - weighted / total, target

    near_rows = row_values([st2[...]] + [stxy[i] for i in range(7)])
    far_rows = row_values([stxy[i] for i in range(7, 15)])
    low = y_hi == 0
    lse, entropy, target = [
        jnp.concatenate([to_col(jnp.where(low, a, b)), to_col(jnp.where(low, b, a))], axis=0)
        for a, b in zip(near_rows, far_rows)
    ]
    log_ratio = target - lse - old
    slope = (kl_weight - adv) * jnp.exp(log_ratio) - kl_weight

    def gradient(j, _):
        l = lg[j].reshape(ROWS, CC)
        hit = iota((ROWS, CC), 1) == tok - (v * COLS + j * CC)
        shifted = l - lse
        probs = jnp.exp(shifted)
        grad = slope * (hit.astype(F32) - probs) + entropy_weight * probs * (shifted + entropy)
        dl_all[:, pl.ds(pl.multiple_of(j * CC, CC), CC)] = grad.astype(BF16)
        return 0

    lax.fori_loop(0, NC, gradient, 0)

    by_xy.rows, by_z.rows = dl_all, dl_z
    by_xy.deal, by_xy.take, by_xy.pack, by_xy.give, by_xy.get = deal_ref.at[0], take_ref.at[0], pack.at[0], give3.at[0], get3.at[0]
    by_z.deal, by_z.take, by_z.pack, by_z.give, by_z.get = deal_ref.at[1], take_ref.at[1], pack.at[1], give3.at[1], get3.at[1]
    by_xy.s, by_xy.r, by_z.s, by_z.r = g_s.at[0], g_r.at[0], g_s.at[1], g_r.at[1]

    def first_copy(t, k, by):
        q = (by.me + k) % 8
        return remote(
            part.at[t, pl.ds(pl.multiple_of(q * 32, 32), 32)], rx1.at[t, k - 1],
            a_s.at[t, k - 1], a_r.at[t, k - 1], by.peer(k),
        )

    def partial(t, by):
        for h in range(TF // 256):
            part[t, :, h * 256 : h * 256 + 256] = lax.dot_general(
                by.rows[...], head_v[t * TF + h * 256 : t * TF + h * 256 + 256, :], (((1,), (1,)), ((), ())),
                preferred_element_type=F32,
            ).astype(BF16)

        for k in range(1, 8):
            first_copy(t, k, by).start()

    order = [(0, by_xy), (3, by_z), (1, by_xy), (2, by_xy)]
    for t, by in order:
        if by is by_z:
            def reorder(j, _):
                cols = pl.ds(pl.multiple_of(j * CC, CC), CC)
                dl_z[:, cols] = jnp.dot(order_ref[...], dl_all[:, cols], preferred_element_type=F32).astype(BF16)
                return 0

            lax.fori_loop(0, NC, reorder, 0)
        partial(t, by)

    def head_part(t, _):
        rows = pl.ds(pl.multiple_of(t * 256, 256), 256)
        gw[rows, :] = jnp.dot(turned[rows, :], dl_all[...], preferred_element_type=F32).astype(BF16)
        return 0

    lax.fori_loop(0, DEPTH // 256, head_part, 0)

    mask = row_of(rank_of(lens, ends_z, dp * GROUP + iota((1, GROUP), 1), True)[0]) == iota((ROWS, GROUP), 0)
    lr_out[...] = jnp.sum(jnp.where(mask, log_ratio, 0.0), axis=0, keepdims=True)
    en_out[...] = jnp.sum(jnp.where(mask, entropy, 0.0), axis=0, keepdims=True)

    def second_copy(t, k, by):
        q = (by.other + k) % 8
        return remote(
            s2.at[t, pl.ds(pl.multiple_of(q * 16, 16), 16)], rx2.at[t, k - 1],
            b_s.at[t, k - 1], b_r.at[t, k - 1], by.across(k),
        )

    def third_copy(k, by):
        return remote(by.give.at[(by.me + k) % 8], by.get.at[k], by.s.at[k - 1], by.r.at[k - 1], by.peer(k))

    def each(make):
        for k in range(1, 8):
            make(k)

    for t, by in order:
        each(lambda k: first_copy(t, k, by).wait())
        acc = part[t, pl.ds(pl.multiple_of(by.me * 32, 32), 32)].astype(F32)
        for k in range(7):
            acc = acc + rx1[t, k].astype(F32)
        both = jnp.concatenate([acc[:, 0:256], acc[:, 256:512]], axis=0).astype(BF16)
        s2[t] = jnp.dot(by.deal[...], both, preferred_element_type=F32).astype(BF16)
        each(lambda k: second_copy(t, k, by).start())

    pack[...] = jnp.zeros_like(pack)
    by_xy.done, by_xy.tiles, by_xy.count = 0, [], 3
    by_z.done, by_z.tiles, by_z.count = 0, [], 1
    for t, by in order:
        each(lambda k: second_copy(t, k, by).wait())
        acc = s2[t, pl.ds(pl.multiple_of(by.other * 16, 16), 16)].astype(F32)
        for k in range(7):
            acc = acc + rx2[t, k].astype(F32)
        for h in range(2):
            for e in range(2):
                by.pack[:, 4 * by.done + 2 * h + e, :] = acc[8 * h : 8 * h + 8, 128 * e : 128 * e + 128]
        by.tiles.append(t)
        by.done += 1
        if by.done == by.count:
            by.give[...] = by.pack[...].astype(BF16)
            each(lambda k: third_copy(k, by).start())

    for by in (by_z, by_xy):
        by.get[0] = by.give[by.me]
        each(lambda k: third_copy(k, by).wait())
        rows = jnp.dot(by.take[...], by.get[...].reshape(128, 128), preferred_element_type=F32)
        by.pack[...] = rows.reshape(8, 16, 128)
        for i, t in enumerate(by.tiles):
            for c in range(4):
                gh_out[:, t * TF + c * 128 : t * TF + c * 128 + 128] = by.pack[:, 4 * i + c, :]


def store_kernel(gw_ref, lr_ref, en_ref, gh_ref, gw_out, lr_out, en_out, gh_out, sem):
    copy = pltpu.make_async_copy(gw_ref, gw_out, sem.at[0])
    copy.start()
    lr_out[...] = lr_ref[...]
    en_out[...] = en_ref[...]
    gh_out[...] = gh_ref[...].astype(BF16)
    copy.wait()


def local(hidden, head, token_ids, old_logp, advantages, lengths):
    vmem = pl.BlockSpec(memory_space=pltpu.VMEM)
    hbm = pl.BlockSpec(memory_space=pltpu.HBM)
    dma = pltpu.SemaphoreType.DMA
    keep = pltpu.with_memory_space_constraint
    gw, lr, en, gh = pl.pallas_call(
        main_kernel,
        out_shape=(
            pltpu.VMEM((DEPTH, COLS), BF16),
            pltpu.VMEM((1, GROUP), F32),
            pltpu.VMEM((1, GROUP), F32),
            pltpu.VMEM((8, DEPTH), F32),
        ),
        in_specs=[hbm] * 6,
        out_specs=(vmem,) * 4,
        scratch_shapes=[
            pltpu.SMEM((8,), jnp.int32),
            pltpu.VMEM((1, SLOTS), jnp.int32),
            pltpu.VMEM((1, SLOTS), F32),
            pltpu.VMEM((1, SLOTS), F32),
            pltpu.VMEM((4, GROUP, DEPTH), BF16),
            pltpu.VMEM((DEPTH, COLS), BF16),
            pltpu.VMEM((ROWS, DEPTH), BF16),
            pltpu.VMEM((NC, 2, 2, 64, CC), F32),
            pltpu.VMEM((NC, 2, 64, CC), F32),
            pltpu.VMEM((NC, 64, CC), F32),
            pltpu.VMEM((NC, 64, CC), F32),
            pltpu.VMEM((64, COLS), F32),
            pltpu.VMEM((NC, 2, 2, 64, CC), F32),
            pltpu.VMEM((8, 128), F32),
            pltpu.VMEM((8, 128), F32),
            pltpu.VMEM((15, 8, 128), F32),
            pltpu.VMEM((15, 8, 128), F32),
            pltpu.VMEM((DEPTH, ROWS), BF16),
            pltpu.VMEM((ROWS, COLS), BF16),
            pltpu.VMEM((ROWS, COLS), BF16),
            pltpu.VMEM((NT, ROWS, TF), BF16),
            pltpu.VMEM((NT, 7, 32, TF), BF16),
            pltpu.VMEM((NT, 128, 256), BF16),
            pltpu.VMEM((NT, 7, 16, 256), BF16),
            pltpu.VMEM((2, 8, 16, 128), F32),
            pltpu.VMEM((2, 8, 16, 128), BF16),
            pltpu.VMEM((2, 8, 16, 128), BF16),
            pltpu.VMEM((ROWS, SLOTS), BF16),
            pltpu.VMEM((ROWS, ROWS), BF16),
            pltpu.VMEM((2, 128, 64), BF16),
            pltpu.VMEM((2, 128, 128), BF16),
            dma((6,)), dma((1,)), dma((1,)), dma((2, 2)), dma((2, 2)), dma((2,)), dma((2,)), dma((2,)), dma((2,)),
            dma((2, 2, 3)), dma((2, 2, 3)), dma((2, 7)), dma((2, 7)),
            dma((NC,)), dma((NC,)), dma((NC,)), dma((NC,)),
            dma((15,)), dma((15,)), dma((15,)), dma((15,)),
            dma((NC,)), dma((NC,)), dma((NC,)), dma((NC,)), dma((NC,)), dma((NC,)),
            dma((NT, 7)), dma((NT, 7)), dma((NT, 7)), dma((NT, 7)), dma((2, 7)), dma((2, 7)),
        ],
        compiler_params=pltpu.CompilerParams(
            collective_id=0, has_side_effects=True, vmem_limit_bytes=48 * 1024 * 1024
        ),
        name="main",
    )(*[keep(a, pltpu.HBM) for a in (lengths, token_ids[None], old_logp[None], advantages[None], hidden, head)])
    gw, lr, en, gh = pl.pallas_call(
        store_kernel,
        out_shape=(
            jax.ShapeDtypeStruct((DEPTH, COLS), BF16),
            jax.ShapeDtypeStruct((1, GROUP), F32),
            jax.ShapeDtypeStruct((1, GROUP), F32),
            jax.ShapeDtypeStruct((8, DEPTH), BF16),
        ),
        in_specs=[vmem] * 4,
        out_specs=(hbm, vmem, vmem, vmem),
        scratch_shapes=[dma((1,))],
        compiler_params=pltpu.CompilerParams(vmem_limit_bytes=32 * 1024 * 1024),
        name="store",
    )(*[keep(a, pltpu.VMEM) for a in (gw, lr, en, gh)])
    return lr[0], en[0], gh, gw


def solution(mesh):
    in_specs = (P("dp", None), P("dp", "vocab"), P(), P(), P(), P())
    out_specs = (P("dp"), P("dp"), P("vocab", "dp"), P("dp", "vocab"))
    return jax.shard_map(local, mesh=mesh, in_specs=in_specs, out_specs=out_specs, check_vma=False)
```

```python
import functools

import jax
import jax.numpy as jnp
from jax import lax
from jax.experimental import pallas as pl
from jax.experimental.pallas import tpu as pltpu
from jax.sharding import PartitionSpec as P

kl_weight = 0.2
entropy_weight = 0.1

F32 = jnp.float32
BF16 = jnp.bfloat16
MESH = pl.DeviceIdType.MESH

RESP = 64
SLOTS = 512
ROWS = 256
GROUP = 128
DEPTH = 2048
COLS = 1280
CC = 256
NC = COLS // CC
TF = 512
TILES = ((0, 512, True), (1536, 512, False), (512, 512, True), (1024, 256, True), (1280, 256, True))
NT = len(TILES)
RING = (4, 3, 5, 2, 6, 1, 7)
XF = 1024
ZF = 512
DF = DEPTH - XF - ZF
XH = XF // 2


def iota(shape, dim):
    return lax.broadcasted_iota(jnp.int32, shape, dim)


def merge(parts):
    top = functools.reduce(jnp.maximum, [p[0:1] for p in parts])
    scales = [jnp.exp(p[0:1] - top) for p in parts]
    total = sum(p[1:2] * s for p, s in zip(parts, scales))
    weighted = sum(p[2:3] * s for p, s in zip(parts, scales))
    target = sum(p[3:4] for p in parts)
    return top, total, weighted, target


def plan_z(lens):
    ends = [0]
    for z in range(8):
        for x in range(4):
            ends.append(ends[-1] + jnp.clip(lens[2 * x + z // 4] - 16 * (z % 4), 0, 16))
    return ends


def plan_xy(lens):
    ends = [0]
    for m in range(8):
        for i in range(8):
            ends.append(ends[-1] + jnp.clip(lens[2 * (m // 2) + i // 4] - 16 * (i % 4) - 8 * (m % 2), 0, 8))
    return ends


def rank_of(lens, ends, slot, by_z):
    seq, pos = slot // RESP, slot % RESP
    if by_z:
        block, size = ((seq % 2) * 4 + pos // 16) * 4 + seq // 2, 16
    else:
        block, size = ((seq // 2) * 2 + (pos // 8) % 2) * 8 + (seq % 2) * 4 + pos // 16, 8
    first = jnp.zeros_like(slot)
    for b in range(1, len(ends) - 1):
        first = jnp.where(block == b, ends[b], first)
    length = jnp.zeros_like(slot)
    for s in range(8):
        length = jnp.where(seq == s, lens[s], length)
    return jnp.where(pos < length, first + pos % size, -1), length - pos


def row_of(rank):
    return jnp.where(rank >= 0, (rank % 8) * 32 + rank // 8, -1)


def onehot(mask):
    return mask.astype(F32).astype(BF16)


def main_kernel(
    len_hbm, tok_hbm, old_hbm, adv_hbm, hid_ref, head_ref,
    gw, lr_out, en_out, gh_out,
    len_ref, tok_ref, old_ref, adv_ref,
    spread, head_v, comp, lp, rxc, sy, ryy, logit, lg, st1, st2, stz, stxy, turned, dl_all, dl_z, part, rx1, s2, rx2, pack, give3, get3, pick_ref, order_ref, deal_ref, take_ref,
    loc_sem, hc_s, hc_r, hx_s, hx_r, hz_s, hz_r, hd_s, hd_r, fx_s, fx_r, fz_s, fz_r,
    lc_s, lc_r, ly_s, ly_r, z_s, z_r, xy_s, xy_r, gc_s, gc_r, gy_s, gy_r, gf_s, gf_r, a_s, a_r, b_s, b_r, g_s, g_r,
):
    dp = lax.axis_index("dp")
    v = lax.axis_index("vocab")
    y_hi, core = dp // 2, dp % 2
    x, z, y_lo = v // 16, (v // 2) % 8, v % 2
    m = x * 2 + y_lo

    def dp_id(d):
        return {"dp": d, "vocab": v}

    def z_id(k, far=False):
        return {"dp": y_hi * 2 + 1 - core if far else dp, "vocab": x * 16 + ((z + k) % 8) * 2 + y_lo}

    def xy_id(k, far=False):
        q = (m + k) % 8
        return {"dp": (1 - y_hi) * 2 + core if far else dp, "vocab": (q // 2) * 16 + z * 2 + q % 2}

    def remote(src, dst, ss, rs, dev):
        return pltpu.make_async_remote_copy(
            src_ref=src, dst_ref=dst, send_sem=ss, recv_sem=rs, device_id=dev, device_id_type=MESH
        )

    small = [
        pltpu.make_async_copy(a, b, loc_sem.at[2 + i])
        for i, (a, b) in enumerate(((len_hbm, len_ref), (tok_hbm, tok_ref), (old_hbm, old_ref), (adv_hbm, adv_ref)))
    ]
    for c in small:
        c.start()

    barrier = pltpu.get_barrier_semaphore()
    for k in range(1, 4):
        pl.semaphore_signal(barrier, inc=1, device_id=dp_id((dp + k) % 4), device_id_type=MESH)
    for k in range(1, 8):
        for far in (False, True):
            pl.semaphore_signal(barrier, inc=1, device_id=z_id(k, far), device_id_type=MESH)
            pl.semaphore_signal(barrier, inc=1, device_id=xy_id(k, far), device_id_type=MESH)
    own_copy = pltpu.make_async_copy(
        hid_ref.at[:, pl.ds(pl.multiple_of(dp * DEPTH, DEPTH), DEPTH)], spread.at[dp], loc_sem.at[1]
    )
    own_copy.start()
    head_copy = pltpu.make_async_copy(head_ref, head_v, loc_sem.at[0])
    head_copy.start()
    pl.semaphore_wait(barrier, 31)

    z_rows = pl.ds(pl.multiple_of(16 * z, 16), 16)
    x_rows = pl.ds(pl.multiple_of(32 * x, 32), 32)
    z_cols = pl.ds(XF, ZF)

    def cross(c, sems, rows, start, size):
        d = (1 - y_hi) * 2 + c
        src = hid_ref.at[rows, pl.ds(pl.multiple_of(d * DEPTH + start, 128), size)]
        return remote(src, spread.at[dp, rows, pl.ds(start, size)], sems[0].at[c], sems[1].at[core], dp_id(d))

    def cross_x(c, w):
        return cross(c, (hx_s.at[w], hx_r.at[w]), x_rows, w * XH, XH)

    def cross_z(c):
        return cross(c, (hz_s, hz_r), z_rows, XF, ZF)

    def cross_d(c):
        return cross(c, (hd_s, hd_r), pl.ds(0, GROUP), XF + ZF, DF)

    def landed(g, sems, rows, start, size):
        ref = spread.at[(1 - y_hi) * 2 + g, rows, pl.ds(start, size)]
        return remote(ref, ref, sems[0].at[g], sems[1].at[g], z_id(1))

    def near_core():
        d = y_hi * 2 + 1 - core
        src = hid_ref.at[:, pl.ds(pl.multiple_of(d * DEPTH, DEPTH), DEPTH)]
        return remote(src, spread.at[dp], hc_s.at[0], hc_r.at[0], dp_id(d))

    def pass_z(g, k):
        ref = spread.at[(1 - y_hi) * 2 + g, z_rows, z_cols]
        return remote(ref, ref, fz_s.at[g, k - 1], fz_r.at[g, k - 1], z_id(k))

    def pass_x(g, k, w):
        ref = spread.at[(1 - y_hi) * 2 + g, x_rows, pl.ds(w * XH, XH)]
        return remote(ref, ref, fx_s.at[w, g, k - 1], fx_r.at[w, g, k - 1], xy_id(2 * k))

    for c in (0, 1):
        cross_x(c, 0).start()
    for c in (0, 1):
        cross_z(c).start()
    for c in (0, 1):
        cross_x(c, 1).start()
    near_core().start()
    for c in (0, 1):
        cross_d(c).start()

    for c in small:
        c.wait()
    lens = [len_ref[s] for s in range(8)]
    ends_z, ends_xy = plan_z(lens), plan_xy(lens)
    slots = iota((1, SLOTS), 1)
    row_z = row_of(rank_of(lens, ends_z, slots, True)[0])
    hits = row_z == iota((ROWS, SLOTS), 0)
    pick_ref[...] = onehot(hits)

    def pass_half(w):
        for g in (0, 1):
            landed(g, (hx_s.at[w], hx_r.at[w]), x_rows, w * XH, XH).wait_recv()
            for k in (2, 1, 3):
                pass_x(g, k, w).start()

    pass_half(0)
    for g in (0, 1):
        landed(g, (hz_s, hz_r), z_rows, XF, ZF).wait_recv()
        for k in RING:
            pass_z(g, k).start()
    pass_half(1)

    pick_xy = onehot(row_of(rank_of(lens, ends_xy, slots, False)[0]) == iota((ROWS, SLOTS), 0))
    order_ref[...] = lax.dot_general(
        pick_xy, pick_ref[...], (((1,), (1,)), ((), ())), preferred_element_type=F32
    ).astype(BF16)
    tok = jnp.sum(jnp.where(hits, tok_ref[...], 0), axis=1, keepdims=True)
    base = 128 * y_hi + 64 * core
    my_mask = row_z == base + iota((64, SLOTS), 0)
    my_tok = jnp.sum(jnp.where(my_mask, tok_ref[...], 0), axis=1, keepdims=True)
    old = jnp.sum(jnp.where(hits, old_ref[...], 0.0), axis=1, keepdims=True)
    adv = jnp.sum(jnp.where(hits, adv_ref[...], 0.0), axis=1, keepdims=True)

    class By:
        pass

    by_xy, by_z = By(), By()
    by_xy.me, by_xy.peer, by_xy.other, by_xy.across = m, xy_id, z, z_id
    by_z.me, by_z.peer, by_z.other, by_z.across = z, z_id, m, xy_id
    by_xy.rank = lambda slot: rank_of(lens, ends_z, slot, True)
    by_z.rank = lambda slot: rank_of(lens, ends_xy, slot, False)
    by_xy.slot = lambda second, first: 128 * (first // 2) + 16 * second + 8 * (first % 2)
    by_z.slot = lambda second, first: 128 * (second // 2) + 16 * first + 8 * (second % 2)
    for i, by in enumerate((by_xy, by_z)):
        col = iota((128, 1), 0)
        first, left = by.rank(by.slot(col // 16, col % 8))
        rank = first + (by.me - first) % 8
        row = rank // 8 + 32 * ((col // 8) % 2)
        row = jnp.where((first >= 0) & (rank < first + jnp.minimum(left, 8)), row, -1)
        deal_ref[i] = onehot(row == iota((128, 64), 1))
        rank, _ = by.rank(by.slot(by.other, by.me) + col // 16)
        place = ((by.me - rank) % 8) * 16 + col % 16
        take_ref[i] = onehot(jnp.where(rank >= 0, place, -1) == iota((128, 128), 1))

    own_copy.wait()
    near_core().wait()

    def compact(half, first):
        def step(t, _):
            cols = pl.ds(pl.multiple_of(t * 512, 512), 512)
            full = spread[pl.ds(2 * half, 2), :, cols].reshape(256, 512)
            mine = pick_ref[:, pl.ds(pl.multiple_of(half * 256, 256), 256)]
            rows = jnp.dot(mine, full, preferred_element_type=F32).astype(BF16)
            comp[:, cols] = rows if first else comp[:, cols] + rows
            return 0

        lax.fori_loop(0, DEPTH // 512, step, 0)

    compact(y_hi, True)
    head_copy.wait()
    for g in (0, 1):
        cross_z(g).wait_send()
        cross_x(g, 0).wait_send()
        cross_x(g, 1).wait_send()
        cross_d(g).wait_send()
        landed(g, (hd_s, hd_r), pl.ds(0, GROUP), XF + ZF, DF).wait_recv()
        for k in range(1, 8):
            pass_z(g, k).wait()
        for k in range(1, 4):
            pass_x(g, k, 0).wait()
            pass_x(g, k, 1).wait()
    compact(1 - y_hi, False)

    def core_copy(j):
        return remote(
            lp.at[j, :, 1 - core], rxc.at[j],
            lc_s.at[j], lc_r.at[j], dp_id(y_hi * 2 + 1 - core),
        )

    def y_copy(j):
        return remote(sy.at[j], ryy.at[j], ly_s.at[j], ly_r.at[j], dp_id((1 - y_hi) * 2 + core))

    def chip_sum(j):
        core_copy(j).wait()
        sy[j] = lp[j, 1 - y_hi, core] + rxc[j, 1 - y_hi]
        y_copy(j).start()
        cols = pl.ds(pl.multiple_of(j * CC, CC), CC)
        logit[:, cols] = lp[j, y_hi, core] + rxc[j, y_hi]

    def product(j, _):
        cols = pl.ds(pl.multiple_of(j * CC, CC), CC)
        lp[j] = jnp.dot(comp[...], head_v[:, cols], preferred_element_type=F32).reshape(2, 2, 64, CC)
        core_copy(j).start()

        @pl.when(j > 0)
        def _():
            chip_sum(j - 1)

        return 0

    lax.fori_loop(0, NC, product, 0)
    chip_sum(NC - 1)

    y_dev, c_dev = dp_id((1 - y_hi) * 2 + core), dp_id(y_hi * 2 + 1 - core)

    def give(j, sems, dev, side):
        ref = lg.at[j, side, core]
        return remote(ref, ref, sems[0].at[j], sems[1].at[j], dev)

    def full_sum(j, _):
        y_copy(j).wait()
        cols = pl.ds(pl.multiple_of(j * CC, CC), CC)
        l = logit[:, cols] + ryy[j]
        logit[:, cols] = l
        lg[j, y_hi, core] = l
        give(j, (gy_s, gy_r), y_dev, y_hi).start()
        give(j, (gc_s, gc_r), c_dev, y_hi).start()
        return 0

    lax.fori_loop(0, NC, full_sum, 0)

    eye = iota((64, 128), 0) + 64 * core == iota((64, 128), 1)
    eye_all = iota((128, 128), 0) == iota((128, 128), 1)

    def to_row(col):
        return jnp.sum(jnp.where(eye, col, 0.0), axis=0, keepdims=True)

    def to_col(row):
        return jnp.sum(jnp.where(eye_all, row, 0.0), axis=1, keepdims=True)

    l = logit[...]
    hit = iota((64, COLS), 1) == my_tok - v * COLS
    top = jnp.max(l, axis=1, keepdims=True)
    e = jnp.exp(l - top)
    st1[...] = jnp.concatenate(
        [
            jnp.max(jnp.where(eye, top, -1e30), axis=0, keepdims=True),
            to_row(jnp.sum(e, axis=1, keepdims=True)),
            to_row(jnp.sum(e * l, axis=1, keepdims=True)),
            to_row(jnp.sum(jnp.where(hit, l, 0.0), axis=1, keepdims=True)),
            jnp.zeros((4, 128), F32),
        ],
        axis=0,
    )

    stat_peers = [(k, False) for k in RING] + [(k, True) for k in RING + (0,)]

    def z_copy(i):
        return remote(st1, stz.at[i], z_s.at[i], z_r.at[i], z_id(*stat_peers[i]))

    def xy_copy(i):
        return remote(st2, stxy.at[i], xy_s.at[i], xy_r.at[i], xy_id(*stat_peers[i]))

    for i in range(15):
        z_copy(i).start()

    def turn(t, _):
        cols = pl.ds(pl.multiple_of(t * 256, 256), 256)
        turned[cols, :] = comp[:, cols].astype(F32).T.astype(BF16)
        return 0

    lax.fori_loop(0, DEPTH // 256, turn, 0)
    for i in range(15):
        z_copy(i).wait()
    st2[...] = jnp.concatenate(
        list(merge([st1[...]] + [stz[i] for i in range(15)])) + [jnp.zeros((4, 128), F32)], axis=0
    )
    for i in range(15):
        xy_copy(i).start()

    def forward(j, _):
        give(j, (gy_s, gy_r), y_dev, 1 - y_hi).wait_recv()
        give(j, (gf_s, gf_r), c_dev, 1 - y_hi).start()
        return 0

    lax.fori_loop(0, NC, forward, 0)
    def arrive(j, _):
        give(j, (gc_s, gc_r), c_dev, y_hi).wait()
        give(j, (gf_s, gf_r), c_dev, 1 - y_hi).wait()
        give(j, (gy_s, gy_r), y_dev, y_hi).wait_send()
        return 0

    lax.fori_loop(0, NC, arrive, 0)
    for i in range(15):
        xy_copy(i).wait()

    def row_values(parts):
        top, total, weighted, target = merge(parts)
        lse = top + jnp.log(total)
        return lse, lse - weighted / total, target

    near_rows = row_values([st2[...]] + [stxy[i] for i in range(7)])
    far_rows = row_values([stxy[i] for i in range(7, 15)])
    low = y_hi == 0
    lse, entropy, target = [
        jnp.concatenate([to_col(jnp.where(low, a, b)), to_col(jnp.where(low, b, a))], axis=0)
        for a, b in zip(near_rows, far_rows)
    ]
    log_ratio = target - lse - old
    slope = (kl_weight - adv) * jnp.exp(log_ratio) - kl_weight

    def gradient(j, _):
        l = lg[j].reshape(ROWS, CC)
        hit = iota((ROWS, CC), 1) == tok - (v * COLS + j * CC)
        shifted = l - lse
        probs = jnp.exp(shifted)
        grad = slope * (hit.astype(F32) - probs) + entropy_weight * probs * (shifted + entropy)
        dl_all[:, pl.ds(pl.multiple_of(j * CC, CC), CC)] = grad.astype(BF16)
        return 0

    lax.fori_loop(0, NC, gradient, 0)

    by_xy.rows, by_z.rows = dl_all, dl_z
    by_xy.deal, by_xy.take, by_xy.pack, by_xy.give, by_xy.get = deal_ref.at[0], take_ref.at[0], pack.at[0], give3.at[0], get3.at[0]
    by_z.deal, by_z.take, by_z.pack, by_z.give, by_z.get = deal_ref.at[1], take_ref.at[1], pack.at[1], give3.at[1], get3.at[1]
    by_xy.s, by_xy.r, by_z.s, by_z.r = g_s.at[0], g_r.at[0], g_s.at[1], g_r.at[1]

    order = [(t, start, size, by_xy if xy else by_z) for t, (start, size, xy) in enumerate(TILES)]

    def first_copy(t, k, by):
        q, cols = (by.me + k) % 8, pl.ds(0, TILES[t][1])
        return remote(
            part.at[t, pl.ds(pl.multiple_of(q * 32, 32), 32), cols], rx1.at[t, k - 1, :, cols],
            a_s.at[t, k - 1], a_r.at[t, k - 1], by.peer(k),
        )

    for t, start, size, by in order:
        if by is by_z:
            def reorder(j, _):
                cols = pl.ds(pl.multiple_of(j * CC, CC), CC)
                dl_z[:, cols] = jnp.dot(order_ref[...], dl_all[:, cols], preferred_element_type=F32).astype(BF16)
                return 0

            lax.fori_loop(0, NC, reorder, 0)
        for h in range(0, size, 256):
            part[t, :, h : h + 256] = lax.dot_general(
                by.rows[...], head_v[start + h : start + h + 256, :], (((1,), (1,)), ((), ())),
                preferred_element_type=F32,
            ).astype(BF16)
        for k in RING:
            first_copy(t, k, by).start()

    def head_part(t, _):
        rows = pl.ds(pl.multiple_of(t * 256, 256), 256)
        gw[rows, :] = jnp.dot(turned[rows, :], dl_all[...], preferred_element_type=F32).astype(BF16)
        return 0

    lax.fori_loop(0, DEPTH // 256, head_part, 0)

    mask = row_of(rank_of(lens, ends_z, dp * GROUP + iota((1, GROUP), 1), True)[0]) == iota((ROWS, GROUP), 0)
    lr_out[...] = jnp.sum(jnp.where(mask, log_ratio, 0.0), axis=0, keepdims=True)
    en_out[...] = jnp.sum(jnp.where(mask, entropy, 0.0), axis=0, keepdims=True)

    def second_copy(t, k, by):
        q, cols = (by.other + k) % 8, pl.ds(0, TILES[t][1] // 2)
        return remote(
            s2.at[t, pl.ds(pl.multiple_of(q * 16, 16), 16), cols], rx2.at[t, k - 1, :, cols],
            b_s.at[t, k - 1], b_r.at[t, k - 1], by.across(k),
        )

    def third_copy(k, by):
        return remote(by.give.at[(by.me + k) % 8], by.get.at[k], by.s.at[k - 1], by.r.at[k - 1], by.peer(k))

    def each(make):
        for k in RING:
            make(k)

    for t, start, size, by in order:
        half = size // 2
        each(lambda k: first_copy(t, k, by).wait())
        acc = part[t, pl.ds(pl.multiple_of(by.me * 32, 32), 32), :size].astype(F32)
        for k in range(7):
            acc = acc + rx1[t, k, :, :size].astype(F32)
        both = jnp.concatenate([acc[:, :half], acc[:, half:]], axis=0).astype(BF16)
        s2[t, :, :half] = jnp.dot(by.deal[...], both, preferred_element_type=F32).astype(BF16)
        each(lambda k: second_copy(t, k, by).start())

    pack[...] = jnp.zeros_like(pack)
    for by in (by_xy, by_z):
        by.chunks, by.last = [], max(o[0] for o in order if o[3] is by)
    for t, start, size, by in order:
        half = size // 2
        each(lambda k: second_copy(t, k, by).wait())
        acc = s2[t, pl.ds(pl.multiple_of(by.other * 16, 16), 16), :half].astype(F32)
        for k in range(7):
            acc = acc + rx2[t, k, :, :half].astype(F32)
        for h in range(2):
            for e in range(0, half, 128):
                by.pack[:, len(by.chunks), :] = acc[8 * h : 8 * h + 8, e : e + 128]
                by.chunks.append(start + h * half + e)
        if t == by.last:
            by.give[...] = by.pack[...].astype(BF16)
            each(lambda k: third_copy(k, by).start())

    for by in (by_z, by_xy):
        by.get[0] = by.give[by.me]
        each(lambda k: third_copy(k, by).wait())
        rows = jnp.dot(by.take[...], by.get[...].reshape(128, 128), preferred_element_type=F32)
        by.pack[...] = rows.reshape(8, 16, 128)
        for c, start in enumerate(by.chunks):
            gh_out[:, start : start + 128] = by.pack[:, c, :].astype(BF16)


def store_kernel(*refs):
    copies = [pltpu.make_async_copy(refs[i], refs[4 + i], refs[8].at[i]) for i in range(4)]
    for c in copies:
        c.start()
    for c in copies:
        c.wait()


def local(hidden, head, token_ids, old_logp, advantages, lengths):
    vmem = pl.BlockSpec(memory_space=pltpu.VMEM)
    hbm = pl.BlockSpec(memory_space=pltpu.HBM)
    dma = pltpu.SemaphoreType.DMA
    keep = pltpu.with_memory_space_constraint
    gw, lr, en, gh = pl.pallas_call(
        main_kernel,
        out_shape=(
            pltpu.VMEM((DEPTH, COLS), BF16),
            pltpu.VMEM((1, GROUP), F32),
            pltpu.VMEM((1, GROUP), F32),
            pltpu.VMEM((8, DEPTH), BF16),
        ),
        in_specs=[hbm] * 6,
        out_specs=(vmem,) * 4,
        scratch_shapes=[
            pltpu.SMEM((8,), jnp.int32),
            pltpu.VMEM((1, SLOTS), jnp.int32),
            pltpu.VMEM((1, SLOTS), F32),
            pltpu.VMEM((1, SLOTS), F32),
            pltpu.VMEM((4, GROUP, DEPTH), BF16),
            pltpu.VMEM((DEPTH, COLS), BF16),
            pltpu.VMEM((ROWS, DEPTH), BF16),
            pltpu.VMEM((NC, 2, 2, 64, CC), F32),
            pltpu.VMEM((NC, 2, 64, CC), F32),
            pltpu.VMEM((NC, 64, CC), F32),
            pltpu.VMEM((NC, 64, CC), F32),
            pltpu.VMEM((64, COLS), F32),
            pltpu.VMEM((NC, 2, 2, 64, CC), F32),
            pltpu.VMEM((8, 128), F32),
            pltpu.VMEM((8, 128), F32),
            pltpu.VMEM((15, 8, 128), F32),
            pltpu.VMEM((15, 8, 128), F32),
            pltpu.VMEM((DEPTH, ROWS), BF16),
            pltpu.VMEM((ROWS, COLS), BF16),
            pltpu.VMEM((ROWS, COLS), BF16),
            pltpu.VMEM((NT, ROWS, TF), BF16),
            pltpu.VMEM((NT, 7, 32, TF), BF16),
            pltpu.VMEM((NT, 128, 256), BF16),
            pltpu.VMEM((NT, 7, 16, 256), BF16),
            pltpu.VMEM((2, 8, 16, 128), F32),
            pltpu.VMEM((2, 8, 16, 128), BF16),
            pltpu.VMEM((2, 8, 16, 128), BF16),
            pltpu.VMEM((ROWS, SLOTS), BF16),
            pltpu.VMEM((ROWS, ROWS), BF16),
            pltpu.VMEM((2, 128, 64), BF16),
            pltpu.VMEM((2, 128, 128), BF16),
            dma((6,)), dma((1,)), dma((1,)), dma((2, 2)), dma((2, 2)), dma((2,)), dma((2,)), dma((2,)), dma((2,)),
            dma((2, 2, 3)), dma((2, 2, 3)), dma((2, 7)), dma((2, 7)),
            dma((NC,)), dma((NC,)), dma((NC,)), dma((NC,)),
            dma((15,)), dma((15,)), dma((15,)), dma((15,)),
            dma((NC,)), dma((NC,)), dma((NC,)), dma((NC,)), dma((NC,)), dma((NC,)),
            dma((NT, 7)), dma((NT, 7)), dma((NT, 7)), dma((NT, 7)), dma((2, 7)), dma((2, 7)),
        ],
        compiler_params=pltpu.CompilerParams(
            collective_id=0, has_side_effects=True, vmem_limit_bytes=48 * 1024 * 1024
        ),
        name="main",
    )(*[keep(a, pltpu.HBM) for a in (lengths, token_ids[None], old_logp[None], advantages[None], hidden, head)])
    gw, lr, en, gh = pl.pallas_call(
        store_kernel,
        out_shape=(
            jax.ShapeDtypeStruct((DEPTH, COLS), BF16),
            jax.ShapeDtypeStruct((1, GROUP), F32),
            jax.ShapeDtypeStruct((1, GROUP), F32),
            jax.ShapeDtypeStruct((8, DEPTH), BF16),
        ),
        in_specs=[vmem] * 4,
        out_specs=(hbm,) * 4,
        scratch_shapes=[dma((4,))],
        compiler_params=pltpu.CompilerParams(vmem_limit_bytes=32 * 1024 * 1024),
        name="store",
    )(*[keep(a, pltpu.VMEM) for a in (gw, lr, en, gh)])
    return lr[0], en[0], gh, gw


def solution(mesh):
    in_specs = (P("dp", None), P("dp", "vocab"), P(), P(), P(), P())
    out_specs = (P("dp"), P("dp"), P("vocab", "dp"), P("dp", "vocab"))
    return jax.shard_map(local, mesh=mesh, in_specs=in_specs, out_specs=out_specs, check_vma=False)
```

```python
import functools

import jax
import jax.numpy as jnp
from jax import lax
from jax.experimental import pallas as pl
from jax.experimental.pallas import tpu as pltpu
from jax.sharding import PartitionSpec as P

kl_weight = 0.2
entropy_weight = 0.1

F32 = jnp.float32
BF16 = jnp.bfloat16
MESH = pl.DeviceIdType.MESH

RESP = 64
SLOTS = 512
ROWS = 256
GROUP = 128
DEPTH = 2048
COLS = 1280
CC = 256
NC = COLS // CC
TF = 512
TILES = ((0, 512, True), (1536, 512, False), (512, 512, True), (1024, 256, True), (1280, 256, True))
NT = len(TILES)
RING = (4, 3, 5, 2, 6, 1, 7)
XF = 1024
ZF = 384
DF = DEPTH - XF - ZF
XH = XF // 2


def iota(shape, dim):
    return lax.broadcasted_iota(jnp.int32, shape, dim)


def merge(parts):
    top = functools.reduce(jnp.maximum, [p[0:1] for p in parts])
    scales = [jnp.exp(p[0:1] - top) for p in parts]
    total = sum(p[1:2] * s for p, s in zip(parts, scales))
    weighted = sum(p[2:3] * s for p, s in zip(parts, scales))
    target = sum(p[3:4] for p in parts)
    return top, total, weighted, target


def plan_z(lens):
    ends = [0]
    for z in range(8):
        for x in range(4):
            ends.append(ends[-1] + jnp.clip(lens[2 * x + z // 4] - 16 * (z % 4), 0, 16))
    return ends


def plan_xy(lens):
    ends = [0]
    for m in range(8):
        for i in range(8):
            ends.append(ends[-1] + jnp.clip(lens[2 * (m // 2) + i // 4] - 16 * (i % 4) - 8 * (m % 2), 0, 8))
    return ends


def rank_of(lens, ends, slot, by_z):
    seq, pos = slot // RESP, slot % RESP
    if by_z:
        block, size = ((seq % 2) * 4 + pos // 16) * 4 + seq // 2, 16
    else:
        block, size = ((seq // 2) * 2 + (pos // 8) % 2) * 8 + (seq % 2) * 4 + pos // 16, 8
    first = jnp.zeros_like(slot)
    for b in range(1, len(ends) - 1):
        first = jnp.where(block == b, ends[b], first)
    length = jnp.zeros_like(slot)
    for s in range(8):
        length = jnp.where(seq == s, lens[s], length)
    return jnp.where(pos < length, first + pos % size, -1), length - pos


def row_of(rank):
    return jnp.where(rank >= 0, (rank % 8) * 32 + rank // 8, -1)


def onehot(mask):
    return mask.astype(F32).astype(BF16)


def main_kernel(
    len_hbm, tok_hbm, old_hbm, adv_hbm, hid_ref, head_ref,
    gw, lr_out, en_out, gh_out,
    len_ref, tok_ref, old_ref, adv_ref,
    spread, head_v, comp, lp, rxc, sy, ryy, logit, lg, st1, st2, stz, stxy, turned, dl_all, dl_z, part, rx1, s2, rx2, pack, give3, get3, pick_ref, order_ref, deal_ref, take_ref,
    loc_sem, hc_s, hc_r, hx_s, hx_r, hz_s, hz_r, hd_s, hd_r, fx_s, fx_r, fz_s, fz_r,
    lc_s, lc_r, ly_s, ly_r, z_s, z_r, xy_s, xy_r, gc_s, gc_r, gy_s, gy_r, gf_s, gf_r, a_s, a_r, b_s, b_r, g_s, g_r,
):
    dp = lax.axis_index("dp")
    v = lax.axis_index("vocab")
    y_hi, core = dp // 2, dp % 2
    x, z, y_lo = v // 16, (v // 2) % 8, v % 2
    m = x * 2 + y_lo

    def dp_id(d):
        return {"dp": d, "vocab": v}

    def z_id(k, far=False):
        return {"dp": y_hi * 2 + 1 - core if far else dp, "vocab": x * 16 + ((z + k) % 8) * 2 + y_lo}

    def xy_id(k, far=False):
        q = (m + k) % 8
        return {"dp": (1 - y_hi) * 2 + core if far else dp, "vocab": (q // 2) * 16 + z * 2 + q % 2}

    def remote(src, dst, ss, rs, dev):
        return pltpu.make_async_remote_copy(
            src_ref=src, dst_ref=dst, send_sem=ss, recv_sem=rs, device_id=dev, device_id_type=MESH
        )

    barrier = pltpu.get_barrier_semaphore()
    for k in range(1, 4):
        pl.semaphore_signal(barrier, inc=1, device_id=dp_id((dp + k) % 4), device_id_type=MESH)
    for k in range(1, 8):
        for far in (False, True):
            pl.semaphore_signal(barrier, inc=1, device_id=z_id(k, far), device_id_type=MESH)
            pl.semaphore_signal(barrier, inc=1, device_id=xy_id(k, far), device_id_type=MESH)
    small = [
        pltpu.make_async_copy(a, b, loc_sem.at[2 + i])
        for i, (a, b) in enumerate(((len_hbm, len_ref), (tok_hbm, tok_ref), (old_hbm, old_ref), (adv_hbm, adv_ref)))
    ]
    for c in small:
        c.start()

    own_copy = pltpu.make_async_copy(
        hid_ref.at[:, pl.ds(pl.multiple_of(dp * DEPTH, DEPTH), DEPTH)], spread.at[dp], loc_sem.at[1]
    )
    own_copy.start()
    head_copy = pltpu.make_async_copy(head_ref, head_v, loc_sem.at[0])
    head_copy.start()
    pl.semaphore_wait(barrier, 31)

    z_rows = pl.ds(pl.multiple_of(16 * z, 16), 16)
    x_rows = pl.ds(pl.multiple_of(32 * x, 32), 32)
    z_cols = pl.ds(XF, ZF)

    def cross(c, sems, rows, start, size):
        d = (1 - y_hi) * 2 + c
        src = hid_ref.at[rows, pl.ds(pl.multiple_of(d * DEPTH + start, 128), size)]
        return remote(src, spread.at[dp, rows, pl.ds(start, size)], sems[0].at[c], sems[1].at[core], dp_id(d))

    def cross_x(c, w):
        return cross(c, (hx_s.at[w], hx_r.at[w]), x_rows, w * XH, XH)

    def cross_z(c):
        return cross(c, (hz_s, hz_r), z_rows, XF, ZF)

    def cross_d(c):
        return cross(c, (hd_s, hd_r), pl.ds(0, GROUP), XF + ZF, DF)

    def landed(g, sems, rows, start, size):
        ref = spread.at[(1 - y_hi) * 2 + g, rows, pl.ds(start, size)]
        return remote(ref, ref, sems[0].at[g], sems[1].at[g], z_id(1))

    def near_core():
        d = y_hi * 2 + 1 - core
        src = hid_ref.at[:, pl.ds(pl.multiple_of(d * DEPTH, DEPTH), DEPTH)]
        return remote(src, spread.at[dp], hc_s.at[0], hc_r.at[0], dp_id(d))

    def pass_z(g, k):
        ref = spread.at[(1 - y_hi) * 2 + g, z_rows, z_cols]
        return remote(ref, ref, fz_s.at[g, k - 1], fz_r.at[g, k - 1], z_id(k))

    def pass_x(g, k, w):
        ref = spread.at[(1 - y_hi) * 2 + g, x_rows, pl.ds(w * XH, XH)]
        return remote(ref, ref, fx_s.at[w, g, k - 1], fx_r.at[w, g, k - 1], xy_id(2 * k))

    for c in (0, 1):
        cross_x(c, 0).start()
    for c in (0, 1):
        cross_z(c).start()
    for c in (0, 1):
        cross_x(c, 1).start()
    near_core().start()
    for c in (0, 1):
        cross_d(c).start()

    for c in small:
        c.wait()
    lens = [len_ref[s] for s in range(8)]
    ends_z, ends_xy = plan_z(lens), plan_xy(lens)
    slots = iota((1, SLOTS), 1)
    row_z = row_of(rank_of(lens, ends_z, slots, True)[0])
    hits = row_z == iota((ROWS, SLOTS), 0)
    pick_ref[...] = onehot(hits)

    def pass_half(w):
        for g in (0, 1):
            landed(g, (hx_s.at[w], hx_r.at[w]), x_rows, w * XH, XH).wait_recv()
            for k in (2, 1, 3):
                pass_x(g, k, w).start()

    pass_half(0)
    for g in (0, 1):
        landed(g, (hz_s, hz_r), z_rows, XF, ZF).wait_recv()
        for k in RING:
            pass_z(g, k).start()
    pass_half(1)

    pick_xy = onehot(row_of(rank_of(lens, ends_xy, slots, False)[0]) == iota((ROWS, SLOTS), 0))
    order_ref[...] = lax.dot_general(
        pick_xy, pick_ref[...], (((1,), (1,)), ((), ())), preferred_element_type=F32
    ).astype(BF16)
    tok = jnp.sum(jnp.where(hits, tok_ref[...], 0), axis=1, keepdims=True)
    base = 128 * y_hi + 64 * core
    my_mask = row_z == base + iota((64, SLOTS), 0)
    my_tok = jnp.sum(jnp.where(my_mask, tok_ref[...], 0), axis=1, keepdims=True)
    old = jnp.sum(jnp.where(hits, old_ref[...], 0.0), axis=1, keepdims=True)
    adv = jnp.sum(jnp.where(hits, adv_ref[...], 0.0), axis=1, keepdims=True)

    class By:
        pass

    by_xy, by_z = By(), By()
    by_xy.me, by_xy.peer, by_xy.other, by_xy.across = m, xy_id, z, z_id
    by_z.me, by_z.peer, by_z.other, by_z.across = z, z_id, m, xy_id
    by_xy.rank = lambda slot: rank_of(lens, ends_z, slot, True)
    by_z.rank = lambda slot: rank_of(lens, ends_xy, slot, False)
    by_xy.slot = lambda second, first: 128 * (first // 2) + 16 * second + 8 * (first % 2)
    by_z.slot = lambda second, first: 128 * (second // 2) + 16 * first + 8 * (second % 2)
    for i, by in enumerate((by_xy, by_z)):
        col = iota((128, 1), 0)
        first, left = by.rank(by.slot(col // 16, col % 8))
        rank = first + (by.me - first) % 8
        row = rank // 8 + 32 * ((col // 8) % 2)
        row = jnp.where((first >= 0) & (rank < first + jnp.minimum(left, 8)), row, -1)
        deal_ref[i] = onehot(row == iota((128, 64), 1))
        rank, _ = by.rank(by.slot(by.other, by.me) + col // 16)
        place = ((by.me - rank) % 8) * 16 + col % 16
        take_ref[i] = onehot(jnp.where(rank >= 0, place, -1) == iota((128, 128), 1))

    own_copy.wait()
    near_core().wait()

    def compact(half, first):
        def step(t, _):
            cols = pl.ds(pl.multiple_of(t * 512, 512), 512)
            full = spread[pl.ds(2 * half, 2), :, cols].reshape(256, 512)
            mine = pick_ref[:, pl.ds(pl.multiple_of(half * 256, 256), 256)]
            rows = jnp.dot(mine, full, preferred_element_type=F32).astype(BF16)
            comp[:, cols] = rows if first else comp[:, cols] + rows
            return 0

        lax.fori_loop(0, DEPTH // 512, step, 0)

    compact(y_hi, True)
    head_copy.wait()
    for g in (0, 1):
        cross_z(g).wait_send()
        cross_x(g, 0).wait_send()
        cross_x(g, 1).wait_send()
        cross_d(g).wait_send()
        landed(g, (hd_s, hd_r), pl.ds(0, GROUP), XF + ZF, DF).wait_recv()
        for k in range(1, 8):
            pass_z(g, k).wait()
        for k in range(1, 4):
            pass_x(g, k, 0).wait()
            pass_x(g, k, 1).wait()
    compact(1 - y_hi, False)

    def core_copy(j):
        return remote(
            lp.at[j, :, 1 - core], rxc.at[j],
            lc_s.at[j], lc_r.at[j], dp_id(y_hi * 2 + 1 - core),
        )

    def y_copy(j):
        return remote(sy.at[j], ryy.at[j], ly_s.at[j], ly_r.at[j], dp_id((1 - y_hi) * 2 + core))

    def chip_sum(j):
        core_copy(j).wait()
        sy[j] = lp[j, 1 - y_hi, core] + rxc[j, 1 - y_hi]
        y_copy(j).start()
        cols = pl.ds(pl.multiple_of(j * CC, CC), CC)
        logit[:, cols] = lp[j, y_hi, core] + rxc[j, y_hi]

    def product(j, _):
        cols = pl.ds(pl.multiple_of(j * CC, CC), CC)
        lp[j] = jnp.dot(comp[...], head_v[:, cols], preferred_element_type=F32).reshape(2, 2, 64, CC)
        core_copy(j).start()

        @pl.when(j > 0)
        def _():
            chip_sum(j - 1)

        return 0

    lax.fori_loop(0, NC, product, 0)
    chip_sum(NC - 1)

    y_dev, c_dev = dp_id((1 - y_hi) * 2 + core), dp_id(y_hi * 2 + 1 - core)

    def give(j, sems, dev, side):
        ref = lg.at[j, side, core]
        return remote(ref, ref, sems[0].at[j], sems[1].at[j], dev)

    def full_sum(j):
        y_copy(j).wait()
        cols = pl.ds(pl.multiple_of(j * CC, CC), CC)
        l = logit[:, cols] + ryy[j]
        logit[:, cols] = l
        lg[j, y_hi, core] = l
        give(j, (gy_s, gy_r), y_dev, y_hi).start()
        give(j, (gc_s, gc_r), c_dev, y_hi).start()

    for j in range(NC):
        full_sum(j)

    eye = iota((64, 128), 0) + 64 * core == iota((64, 128), 1)
    eye_all = iota((128, 128), 0) == iota((128, 128), 1)

    def to_row(col):
        return jnp.sum(jnp.where(eye, col, 0.0), axis=0, keepdims=True)

    def to_col(row):
        return jnp.sum(jnp.where(eye_all, row, 0.0), axis=1, keepdims=True)

    l = logit[...]
    hit = iota((64, COLS), 1) == my_tok - v * COLS
    top = jnp.max(l, axis=1, keepdims=True)
    e = jnp.exp(l - top)
    st1[...] = jnp.concatenate(
        [
            jnp.max(jnp.where(eye, top, -1e30), axis=0, keepdims=True),
            to_row(jnp.sum(e, axis=1, keepdims=True)),
            to_row(jnp.sum(e * l, axis=1, keepdims=True)),
            to_row(jnp.sum(jnp.where(hit, l, 0.0), axis=1, keepdims=True)),
            jnp.zeros((4, 128), F32),
        ],
        axis=0,
    )

    stat_peers = [(k, False) for k in RING] + [(k, True) for k in RING + (0,)]

    def z_copy(i):
        return remote(st1, stz.at[i], z_s.at[i], z_r.at[i], z_id(*stat_peers[i]))

    def xy_copy(i):
        return remote(st2, stxy.at[i], xy_s.at[i], xy_r.at[i], xy_id(*stat_peers[i]))

    for i in range(15):
        z_copy(i).start()

    def turn(t, _):
        cols = pl.ds(pl.multiple_of(t * 256, 256), 256)
        turned[cols, :] = comp[:, cols].astype(F32).T.astype(BF16)
        return 0

    lax.fori_loop(0, DEPTH // 256, turn, 0)
    for i in range(15):
        z_copy(i).wait()
    st2[...] = jnp.concatenate(
        list(merge([st1[...]] + [stz[i] for i in range(15)])) + [jnp.zeros((4, 128), F32)], axis=0
    )
    for i in range(15):
        xy_copy(i).start()

    def forward(j):
        give(j, (gy_s, gy_r), y_dev, 1 - y_hi).wait_recv()
        give(j, (gf_s, gf_r), c_dev, 1 - y_hi).start()

    for j in range(NC):
        forward(j)
    def arrive(j):
        give(j, (gc_s, gc_r), c_dev, y_hi).wait()
        give(j, (gf_s, gf_r), c_dev, 1 - y_hi).wait()
        give(j, (gy_s, gy_r), y_dev, y_hi).wait_send()

    for j in range(NC):
        arrive(j)
    for i in range(15):
        xy_copy(i).wait()

    def row_values(parts):
        top, total, weighted, target = merge(parts)
        lse = top + jnp.log(total)
        return lse, lse - weighted / total, target

    near_rows = row_values([st2[...]] + [stxy[i] for i in range(7)])
    far_rows = row_values([stxy[i] for i in range(7, 15)])
    low = y_hi == 0
    lse, entropy, target = [
        jnp.concatenate([to_col(jnp.where(low, a, b)), to_col(jnp.where(low, b, a))], axis=0)
        for a, b in zip(near_rows, far_rows)
    ]
    log_ratio = target - lse - old
    slope = (kl_weight - adv) * jnp.exp(log_ratio) - kl_weight

    def gradient(j):
        l = lg[j].reshape(ROWS, CC)
        hit = iota((ROWS, CC), 1) == tok - (v * COLS + j * CC)
        shifted = l - lse
        probs = jnp.exp(shifted)
        grad = slope * (hit.astype(F32) - probs) + entropy_weight * probs * (shifted + entropy)
        dl_all[:, pl.ds(pl.multiple_of(j * CC, CC), CC)] = grad.astype(BF16)

    for j in range(NC):
        gradient(j)

    by_xy.rows, by_z.rows = dl_all, dl_z
    by_xy.deal, by_xy.take, by_xy.pack, by_xy.give, by_xy.get = deal_ref.at[0], take_ref.at[0], pack.at[0], give3.at[0], get3.at[0]
    by_z.deal, by_z.take, by_z.pack, by_z.give, by_z.get = deal_ref.at[1], take_ref.at[1], pack.at[1], give3.at[1], get3.at[1]
    by_xy.s, by_xy.r, by_z.s, by_z.r = g_s.at[0], g_r.at[0], g_s.at[1], g_r.at[1]

    order = [(t, start, size, by_xy if xy else by_z) for t, (start, size, xy) in enumerate(TILES)]

    def first_copy(t, k, by):
        q, cols = (by.me + k) % 8, pl.ds(0, TILES[t][1])
        return remote(
            part.at[t, pl.ds(pl.multiple_of(q * 32, 32), 32), cols], rx1.at[t, k - 1, :, cols],
            a_s.at[t, k - 1], a_r.at[t, k - 1], by.peer(k),
        )

    for t, start, size, by in order:
        if by is by_z:
            def reorder(j, _):
                cols = pl.ds(pl.multiple_of(j * CC, CC), CC)
                dl_z[:, cols] = jnp.dot(order_ref[...], dl_all[:, cols], preferred_element_type=F32).astype(BF16)
                return 0

            lax.fori_loop(0, NC, reorder, 0)
        for h in range(0, size, 256):
            part[t, :, h : h + 256] = lax.dot_general(
                by.rows[...], head_v[start + h : start + h + 256, :], (((1,), (1,)), ((), ())),
                preferred_element_type=F32,
            ).astype(BF16)
        for k in RING:
            first_copy(t, k, by).start()

    def head_part(t, _):
        rows = pl.ds(pl.multiple_of(t * 256, 256), 256)
        gw[rows, :] = jnp.dot(turned[rows, :], dl_all[...], preferred_element_type=F32).astype(BF16)
        return 0

    lax.fori_loop(0, DEPTH // 256, head_part, 0)

    mask = row_of(rank_of(lens, ends_z, dp * GROUP + iota((1, GROUP), 1), True)[0]) == iota((ROWS, GROUP), 0)
    lr_out[...] = jnp.sum(jnp.where(mask, log_ratio, 0.0), axis=0, keepdims=True)
    en_out[...] = jnp.sum(jnp.where(mask, entropy, 0.0), axis=0, keepdims=True)

    def second_copy(t, k, by):
        q, cols = (by.other + k) % 8, pl.ds(0, TILES[t][1] // 2)
        return remote(
            s2.at[t, pl.ds(pl.multiple_of(q * 16, 16), 16), cols], rx2.at[t, k - 1, :, cols],
            b_s.at[t, k - 1], b_r.at[t, k - 1], by.across(k),
        )

    def third_copy(k, by):
        return remote(by.give.at[(by.me + k) % 8], by.get.at[k], by.s.at[k - 1], by.r.at[k - 1], by.peer(k))

    def each(make):
        for k in RING:
            make(k)

    for t, start, size, by in order:
        half = size // 2
        each(lambda k: first_copy(t, k, by).wait())
        acc = part[t, pl.ds(pl.multiple_of(by.me * 32, 32), 32), :size].astype(F32)
        for k in range(7):
            acc = acc + rx1[t, k, :, :size].astype(F32)
        both = jnp.concatenate([acc[:, :half], acc[:, half:]], axis=0).astype(BF16)
        s2[t, :, :half] = jnp.dot(by.deal[...], both, preferred_element_type=F32).astype(BF16)
        each(lambda k: second_copy(t, k, by).start())

    pack[...] = jnp.zeros_like(pack)
    for by in (by_xy, by_z):
        by.chunks, by.last = [], max(o[0] for o in order if o[3] is by)
    for t, start, size, by in order:
        half = size // 2
        each(lambda k: second_copy(t, k, by).wait())
        acc = s2[t, pl.ds(pl.multiple_of(by.other * 16, 16), 16), :half].astype(F32)
        for k in range(7):
            acc = acc + rx2[t, k, :, :half].astype(F32)
        for h in range(2):
            for e in range(0, half, 128):
                by.pack[:, len(by.chunks), :] = acc[8 * h : 8 * h + 8, e : e + 128]
                by.chunks.append(start + h * half + e)
        if t == by.last:
            by.give[...] = by.pack[...].astype(BF16)
            each(lambda k: third_copy(k, by).start())

    for by in (by_z, by_xy):
        by.get[0] = by.give[by.me]
        each(lambda k: third_copy(k, by).wait())
        rows = jnp.dot(by.take[...], by.get[...].reshape(128, 128), preferred_element_type=F32)
        by.pack[...] = rows.reshape(8, 16, 128)
        for c, start in enumerate(by.chunks):
            gh_out[:, start : start + 128] = by.pack[:, c, :].astype(BF16)


def store_kernel(*refs):
    copies = [pltpu.make_async_copy(refs[i], refs[4 + i], refs[8].at[i]) for i in range(4)]
    for c in copies:
        c.start()
    for c in copies:
        c.wait()


def local(hidden, head, token_ids, old_logp, advantages, lengths):
    vmem = pl.BlockSpec(memory_space=pltpu.VMEM)
    hbm = pl.BlockSpec(memory_space=pltpu.HBM)
    dma = pltpu.SemaphoreType.DMA
    keep = pltpu.with_memory_space_constraint
    gw, lr, en, gh = pl.pallas_call(
        main_kernel,
        out_shape=(
            pltpu.VMEM((DEPTH, COLS), BF16),
            pltpu.VMEM((1, GROUP), F32),
            pltpu.VMEM((1, GROUP), F32),
            pltpu.VMEM((8, DEPTH), BF16),
        ),
        in_specs=[hbm] * 6,
        out_specs=(vmem,) * 4,
        scratch_shapes=[
            pltpu.SMEM((8,), jnp.int32),
            pltpu.VMEM((1, SLOTS), jnp.int32),
            pltpu.VMEM((1, SLOTS), F32),
            pltpu.VMEM((1, SLOTS), F32),
            pltpu.VMEM((4, GROUP, DEPTH), BF16),
            pltpu.VMEM((DEPTH, COLS), BF16),
            pltpu.VMEM((ROWS, DEPTH), BF16),
            pltpu.VMEM((NC, 2, 2, 64, CC), F32),
            pltpu.VMEM((NC, 2, 64, CC), F32),
            pltpu.VMEM((NC, 64, CC), F32),
            pltpu.VMEM((NC, 64, CC), F32),
            pltpu.VMEM((64, COLS), F32),
            pltpu.VMEM((NC, 2, 2, 64, CC), F32),
            pltpu.VMEM((8, 128), F32),
            pltpu.VMEM((8, 128), F32),
            pltpu.VMEM((15, 8, 128), F32),
            pltpu.VMEM((15, 8, 128), F32),
            pltpu.VMEM((DEPTH, ROWS), BF16),
            pltpu.VMEM((ROWS, COLS), BF16),
            pltpu.VMEM((ROWS, COLS), BF16),
            pltpu.VMEM((NT, ROWS, TF), BF16),
            pltpu.VMEM((NT, 7, 32, TF), BF16),
            pltpu.VMEM((NT, 128, 256), BF16),
            pltpu.VMEM((NT, 7, 16, 256), BF16),
            pltpu.VMEM((2, 8, 16, 128), F32),
            pltpu.VMEM((2, 8, 16, 128), BF16),
            pltpu.VMEM((2, 8, 16, 128), BF16),
            pltpu.VMEM((ROWS, SLOTS), BF16),
            pltpu.VMEM((ROWS, ROWS), BF16),
            pltpu.VMEM((2, 128, 64), BF16),
            pltpu.VMEM((2, 128, 128), BF16),
            dma((6,)), dma((1,)), dma((1,)), dma((2, 2)), dma((2, 2)), dma((2,)), dma((2,)), dma((2,)), dma((2,)),
            dma((2, 2, 3)), dma((2, 2, 3)), dma((2, 7)), dma((2, 7)),
            dma((NC,)), dma((NC,)), dma((NC,)), dma((NC,)),
            dma((15,)), dma((15,)), dma((15,)), dma((15,)),
            dma((NC,)), dma((NC,)), dma((NC,)), dma((NC,)), dma((NC,)), dma((NC,)),
            dma((NT, 7)), dma((NT, 7)), dma((NT, 7)), dma((NT, 7)), dma((2, 7)), dma((2, 7)),
        ],
        compiler_params=pltpu.CompilerParams(
            collective_id=0, has_side_effects=True, vmem_limit_bytes=48 * 1024 * 1024
        ),
        name="main",
    )(*[keep(a, pltpu.HBM) for a in (lengths, token_ids[None], old_logp[None], advantages[None], hidden, head)])
    gw, lr, en, gh = pl.pallas_call(
        store_kernel,
        out_shape=(
            jax.ShapeDtypeStruct((DEPTH, COLS), BF16),
            jax.ShapeDtypeStruct((1, GROUP), F32),
            jax.ShapeDtypeStruct((1, GROUP), F32),
            jax.ShapeDtypeStruct((8, DEPTH), BF16),
        ),
        in_specs=[vmem] * 4,
        out_specs=(hbm,) * 4,
        scratch_shapes=[dma((4,))],
        compiler_params=pltpu.CompilerParams(vmem_limit_bytes=32 * 1024 * 1024),
        name="store",
    )(*[keep(a, pltpu.VMEM) for a in (gw, lr, en, gh)])
    return lr[0], en[0], gh, gw


def solution(mesh):
    in_specs = (P("dp", None), P("dp", "vocab"), P(), P(), P(), P())
    out_specs = (P("dp"), P("dp"), P("vocab", "dp"), P("dp", "vocab"))
    return jax.shard_map(local, mesh=mesh, in_specs=in_specs, out_specs=out_specs, check_vma=False)
```

```python
import functools

import jax
import jax.numpy as jnp
from jax import lax
from jax.experimental import pallas as pl
from jax.experimental.pallas import tpu as pltpu
from jax.sharding import PartitionSpec as P

kl_weight = 0.2
entropy_weight = 0.1

F32 = jnp.float32
BF16 = jnp.bfloat16
MESH = pl.DeviceIdType.MESH

RESP = 64
SLOTS = 512
ROWS = 256
GROUP = 128
DEPTH = 2048
COLS = 1280
CC = 256
NC = COLS // CC
TF = 512
TILES = ((0, 512, True), (1536, 512, False), (512, 512, True), (1024, 256, True), (1280, 256, True))
NT = len(TILES)
RING = (4, 3, 5, 2, 6, 1, 7)
XF = 1024
ZF = 384
DF = DEPTH - XF - ZF
XH = XF // 2


def iota(shape, dim):
    return lax.broadcasted_iota(jnp.int32, shape, dim)


def merge(parts):
    top = functools.reduce(jnp.maximum, [p[0:1] for p in parts])
    scales = [jnp.exp(p[0:1] - top) for p in parts]
    total = sum(p[1:2] * s for p, s in zip(parts, scales))
    weighted = sum(p[2:3] * s for p, s in zip(parts, scales))
    target = sum(p[3:4] for p in parts)
    return top, total, weighted, target


def plan_z(lens):
    ends = [0]
    for z in range(8):
        for x in range(4):
            ends.append(ends[-1] + jnp.clip(lens[2 * x + z // 4] - 16 * (z % 4), 0, 16))
    return ends


def plan_xy(lens):
    ends = [0]
    for m in range(8):
        for i in range(8):
            ends.append(ends[-1] + jnp.clip(lens[2 * (m // 2) + i // 4] - 16 * (i % 4) - 8 * (m % 2), 0, 8))
    return ends


def rank_of(lens, ends, slot, by_z):
    seq, pos = slot // RESP, slot % RESP
    if by_z:
        block, size = ((seq % 2) * 4 + pos // 16) * 4 + seq // 2, 16
    else:
        block, size = ((seq // 2) * 2 + (pos // 8) % 2) * 8 + (seq % 2) * 4 + pos // 16, 8
    first = jnp.zeros_like(slot)
    for b in range(1, len(ends) - 1):
        first = jnp.where(block == b, ends[b], first)
    length = jnp.zeros_like(slot)
    for s in range(8):
        length = jnp.where(seq == s, lens[s], length)
    return jnp.where(pos < length, first + pos % size, -1), length - pos


def row_of(rank):
    return jnp.where(rank >= 0, (rank % 8) * 32 + rank // 8, -1)


def onehot(mask):
    return mask.astype(F32).astype(BF16)


def main_kernel(
    len_hbm, tok_hbm, old_hbm, adv_hbm, hid_ref, head_ref,
    gw, lr_out, en_out, gh_out,
    len_ref, tok_ref, old_ref, adv_ref,
    spread, head_v, comp, lp, rxc, sy, ryy, logit, lg, st1, st2, stz, stxy, turned, dl_all, dl_z, part, rx1, s2, rx2, pack, give3, get3, pick_ref, order_ref, deal_ref, take_ref,
    loc_sem, hc_s, hc_r, hx_s, hx_r, hz_s, hz_r, hd_s, hd_r, fx_s, fx_r, fz_s, fz_r,
    lc_s, lc_r, ly_s, ly_r, z_s, z_r, xy_s, xy_r, gc_s, gc_r, gy_s, gy_r, gf_s, gf_r, a_s, a_r, b_s, b_r, g_s, g_r,
):
    dp = lax.axis_index("dp")
    v = lax.axis_index("vocab")
    y_hi, core = dp // 2, dp % 2
    x, z, y_lo = v // 16, (v // 2) % 8, v % 2
    m = x * 2 + y_lo

    def dp_id(d):
        return {"dp": d, "vocab": v}

    def z_id(k, far=False):
        return {"dp": y_hi * 2 + 1 - core if far else dp, "vocab": x * 16 + ((z + k) % 8) * 2 + y_lo}

    def xy_id(k, far=False):
        q = (m + k) % 8
        return {"dp": (1 - y_hi) * 2 + core if far else dp, "vocab": (q // 2) * 16 + z * 2 + q % 2}

    def remote(src, dst, ss, rs, dev):
        return pltpu.make_async_remote_copy(
            src_ref=src, dst_ref=dst, send_sem=ss, recv_sem=rs, device_id=dev, device_id_type=MESH
        )

    barrier = pltpu.get_barrier_semaphore()
    for k in range(1, 4):
        pl.semaphore_signal(barrier, inc=1, device_id=dp_id((dp + k) % 4), device_id_type=MESH)
    for k in range(1, 8):
        for far in (False, True):
            pl.semaphore_signal(barrier, inc=1, device_id=z_id(k, far), device_id_type=MESH)
            pl.semaphore_signal(barrier, inc=1, device_id=xy_id(k, far), device_id_type=MESH)
    small = [
        pltpu.make_async_copy(a, b, loc_sem.at[2 + i])
        for i, (a, b) in enumerate(((len_hbm, len_ref), (tok_hbm, tok_ref), (old_hbm, old_ref), (adv_hbm, adv_ref)))
    ]
    for c in small:
        c.start()

    own_copy = pltpu.make_async_copy(
        hid_ref.at[:, pl.ds(pl.multiple_of(dp * DEPTH, DEPTH), DEPTH)], spread.at[dp], loc_sem.at[1]
    )
    own_copy.start()
    head_copy = pltpu.make_async_copy(head_ref, head_v, loc_sem.at[0])
    head_copy.start()
    pl.semaphore_wait(barrier, 31)

    z_rows = pl.ds(pl.multiple_of(16 * z, 16), 16)
    x_rows = pl.ds(pl.multiple_of(32 * x, 32), 32)
    z_cols = pl.ds(XF, ZF)

    def cross(c, sems, rows, start, size):
        d = (1 - y_hi) * 2 + c
        src = hid_ref.at[rows, pl.ds(pl.multiple_of(d * DEPTH + start, 128), size)]
        return remote(src, spread.at[dp, rows, pl.ds(start, size)], sems[0].at[c], sems[1].at[core], dp_id(d))

    def cross_x(c, w):
        return cross(c, (hx_s.at[w], hx_r.at[w]), x_rows, w * XH, XH)

    def cross_z(c):
        return cross(c, (hz_s, hz_r), z_rows, XF, ZF)

    def cross_d(c):
        return cross(c, (hd_s, hd_r), pl.ds(0, GROUP), XF + ZF, DF)

    def landed(g, sems, rows, start, size):
        ref = spread.at[(1 - y_hi) * 2 + g, rows, pl.ds(start, size)]
        return remote(ref, ref, sems[0].at[g], sems[1].at[g], z_id(1))

    def near_core():
        d = y_hi * 2 + 1 - core
        src = hid_ref.at[:, pl.ds(pl.multiple_of(d * DEPTH, DEPTH), DEPTH)]
        return remote(src, spread.at[dp], hc_s.at[0], hc_r.at[0], dp_id(d))

    def pass_z(g, k):
        ref = spread.at[(1 - y_hi) * 2 + g, z_rows, z_cols]
        return remote(ref, ref, fz_s.at[g, k - 1], fz_r.at[g, k - 1], z_id(k))

    def pass_x(g, k, w):
        ref = spread.at[(1 - y_hi) * 2 + g, x_rows, pl.ds(w * XH, XH)]
        return remote(ref, ref, fx_s.at[w, g, k - 1], fx_r.at[w, g, k - 1], xy_id(2 * k))

    for c in (0, 1):
        cross_x(c, 0).start()
    for c in (0, 1):
        cross_z(c).start()
    for c in (0, 1):
        cross_x(c, 1).start()
    near_core().start()
    for c in (0, 1):
        cross_d(c).start()

    for c in small:
        c.wait()
    lens = [len_ref[s] for s in range(8)]
    ends_z, ends_xy = plan_z(lens), plan_xy(lens)
    slots = iota((1, SLOTS), 1)
    row_z = row_of(rank_of(lens, ends_z, slots, True)[0])
    hits = row_z == iota((ROWS, SLOTS), 0)
    pick_ref[...] = onehot(hits)

    def pass_half(w):
        for g in (0, 1):
            landed(g, (hx_s.at[w], hx_r.at[w]), x_rows, w * XH, XH).wait_recv()
            for k in (2, 1, 3):
                pass_x(g, k, w).start()

    pass_half(0)
    for g in (0, 1):
        landed(g, (hz_s, hz_r), z_rows, XF, ZF).wait_recv()
        for k in RING:
            pass_z(g, k).start()
    pass_half(1)

    pick_xy = onehot(row_of(rank_of(lens, ends_xy, slots, False)[0]) == iota((ROWS, SLOTS), 0))
    order_ref[...] = lax.dot_general(
        pick_xy, pick_ref[...], (((1,), (1,)), ((), ())), preferred_element_type=F32
    ).astype(BF16)
    tok = jnp.sum(jnp.where(hits, tok_ref[...], 0), axis=1, keepdims=True)
    base = 128 * y_hi + 64 * core
    my_mask = row_z == base + iota((64, SLOTS), 0)
    my_tok = jnp.sum(jnp.where(my_mask, tok_ref[...], 0), axis=1, keepdims=True)
    old = jnp.sum(jnp.where(hits, old_ref[...], 0.0), axis=1, keepdims=True)
    adv = jnp.sum(jnp.where(hits, adv_ref[...], 0.0), axis=1, keepdims=True)

    class By:
        pass

    by_xy, by_z = By(), By()
    by_xy.me, by_xy.peer, by_xy.other, by_xy.across = m, xy_id, z, z_id
    by_z.me, by_z.peer, by_z.other, by_z.across = z, z_id, m, xy_id
    by_xy.rank = lambda slot: rank_of(lens, ends_z, slot, True)
    by_z.rank = lambda slot: rank_of(lens, ends_xy, slot, False)
    by_xy.slot = lambda second, first: 128 * (first // 2) + 16 * second + 8 * (first % 2)
    by_z.slot = lambda second, first: 128 * (second // 2) + 16 * first + 8 * (second % 2)
    for i, by in enumerate((by_xy, by_z)):
        col = iota((128, 1), 0)
        first, left = by.rank(by.slot(col // 16, col % 8))
        rank = first + (by.me - first) % 8
        row = rank // 8 + 32 * ((col // 8) % 2)
        row = jnp.where((first >= 0) & (rank < first + jnp.minimum(left, 8)), row, -1)
        deal_ref[i] = onehot(row == iota((128, 64), 1))
        rank, _ = by.rank(by.slot(by.other, by.me) + col // 16)
        place = ((by.me - rank) % 8) * 16 + col % 16
        take_ref[i] = onehot(jnp.where(rank >= 0, place, -1) == iota((128, 128), 1))

    own_copy.wait()
    near_core().wait()

    def compact(half, first):
        def step(t, _):
            cols = pl.ds(pl.multiple_of(t * 512, 512), 512)
            full = spread[pl.ds(2 * half, 2), :, cols].reshape(256, 512)
            mine = pick_ref[:, pl.ds(pl.multiple_of(half * 256, 256), 256)]
            rows = jnp.dot(mine, full, preferred_element_type=F32).astype(BF16)
            comp[:, cols] = rows if first else comp[:, cols] + rows
            return 0

        lax.fori_loop(0, DEPTH // 512, step, 0)

    compact(y_hi, True)
    head_copy.wait()
    for g in (0, 1):
        cross_z(g).wait_send()
        cross_x(g, 0).wait_send()
        cross_x(g, 1).wait_send()
        cross_d(g).wait_send()
        landed(g, (hd_s, hd_r), pl.ds(0, GROUP), XF + ZF, DF).wait_recv()
        for k in range(1, 8):
            pass_z(g, k).wait()
        for k in range(1, 4):
            pass_x(g, k, 0).wait()
            pass_x(g, k, 1).wait()
    compact(1 - y_hi, False)

    def core_copy(j):
        return remote(
            lp.at[j, :, 1 - core], rxc.at[j],
            lc_s.at[j], lc_r.at[j], dp_id(y_hi * 2 + 1 - core),
        )

    def y_copy(j):
        return remote(sy.at[j], ryy.at[j], ly_s.at[j], ly_r.at[j], dp_id((1 - y_hi) * 2 + core))

    def chip_sum(j):
        core_copy(j).wait()
        sy[j] = lp[j, 1 - y_hi, core] + rxc[j, 1 - y_hi]
        y_copy(j).start()
        cols = pl.ds(pl.multiple_of(j * CC, CC), CC)
        logit[:, cols] = lp[j, y_hi, core] + rxc[j, y_hi]

    for j in range(NC):
        lp[j] = jnp.dot(
            comp[...], head_v[:, j * CC : j * CC + CC], preferred_element_type=F32
        ).reshape(2, 2, 64, CC)
        core_copy(j).start()
        if j > 0:
            chip_sum(j - 1)

    chip_sum(NC - 1)

    y_dev, c_dev = dp_id((1 - y_hi) * 2 + core), dp_id(y_hi * 2 + 1 - core)

    def give(j, sems, dev, side):
        ref = lg.at[j, side, core]
        return remote(ref, ref, sems[0].at[j], sems[1].at[j], dev)

    def full_sum(j):
        y_copy(j).wait()
        cols = pl.ds(pl.multiple_of(j * CC, CC), CC)
        l = logit[:, cols] + ryy[j]
        logit[:, cols] = l
        lg[j, y_hi, core] = l
        give(j, (gy_s, gy_r), y_dev, y_hi).start()
        give(j, (gc_s, gc_r), c_dev, y_hi).start()

    for j in range(NC):
        full_sum(j)

    eye = iota((64, 128), 0) + 64 * core == iota((64, 128), 1)
    eye_all = iota((128, 128), 0) == iota((128, 128), 1)

    def to_row(col):
        return jnp.sum(jnp.where(eye, col, 0.0), axis=0, keepdims=True)

    def to_col(row):
        return jnp.sum(jnp.where(eye_all, row, 0.0), axis=1, keepdims=True)

    l = logit[...]
    hit = iota((64, COLS), 1) == my_tok - v * COLS
    top = jnp.max(l, axis=1, keepdims=True)
    e = jnp.exp(l - top)
    st1[...] = jnp.concatenate(
        [
            jnp.max(jnp.where(eye, top, -1e30), axis=0, keepdims=True),
            to_row(jnp.sum(e, axis=1, keepdims=True)),
            to_row(jnp.sum(e * l, axis=1, keepdims=True)),
            to_row(jnp.sum(jnp.where(hit, l, 0.0), axis=1, keepdims=True)),
            jnp.zeros((4, 128), F32),
        ],
        axis=0,
    )

    stat_peers = [(k, True) for k in RING] + [(k, False) for k in RING] + [(0, True)]

    def z_copy(i):
        return remote(st1, stz.at[i], z_s.at[i], z_r.at[i], z_id(*stat_peers[i]))

    def xy_copy(i):
        return remote(st2, stxy.at[i], xy_s.at[i], xy_r.at[i], xy_id(*stat_peers[i]))

    for i in range(15):
        z_copy(i).start()

    def turn(t, _):
        cols = pl.ds(pl.multiple_of(t * 256, 256), 256)
        turned[cols, :] = comp[:, cols].astype(F32).T.astype(BF16)
        return 0

    lax.fori_loop(0, DEPTH // 256, turn, 0)
    for i in range(15):
        z_copy(i).wait()
    st2[...] = jnp.concatenate(
        list(merge([st1[...]] + [stz[i] for i in range(15)])) + [jnp.zeros((4, 128), F32)], axis=0
    )
    for i in range(15):
        xy_copy(i).start()

    def forward(j):
        give(j, (gy_s, gy_r), y_dev, 1 - y_hi).wait_recv()
        give(j, (gf_s, gf_r), c_dev, 1 - y_hi).start()

    for j in range(NC):
        forward(j)
    def arrive(j):
        give(j, (gc_s, gc_r), c_dev, y_hi).wait()
        give(j, (gf_s, gf_r), c_dev, 1 - y_hi).wait()
        give(j, (gy_s, gy_r), y_dev, y_hi).wait_send()

    for j in range(NC):
        arrive(j)
    for i in range(15):
        xy_copy(i).wait()

    def row_values(parts):
        top, total, weighted, target = merge(parts)
        lse = top + jnp.log(total)
        return lse, lse - weighted / total, target

    near_rows = row_values([st2[...]] + [stxy[i] for i in range(7, 14)])
    far_rows = row_values([stxy[i] for i in (0, 1, 2, 3, 4, 5, 6, 14)])
    low = y_hi == 0
    lse, entropy, target = [
        jnp.concatenate([to_col(jnp.where(low, a, b)), to_col(jnp.where(low, b, a))], axis=0)
        for a, b in zip(near_rows, far_rows)
    ]
    log_ratio = target - lse - old
    slope = (kl_weight - adv) * jnp.exp(log_ratio) - kl_weight

    def gradient(j):
        l = lg[j].reshape(ROWS, CC)
        hit = iota((ROWS, CC), 1) == tok - (v * COLS + j * CC)
        shifted = l - lse
        probs = jnp.exp(shifted)
        grad = slope * (hit.astype(F32) - probs) + entropy_weight * probs * (shifted + entropy)
        dl_all[:, pl.ds(pl.multiple_of(j * CC, CC), CC)] = grad.astype(BF16)

    for j in range(NC):
        gradient(j)

    by_xy.rows, by_z.rows = dl_all, dl_z
    by_xy.deal, by_xy.take, by_xy.pack, by_xy.give, by_xy.get = deal_ref.at[0], take_ref.at[0], pack.at[0], give3.at[0], get3.at[0]
    by_z.deal, by_z.take, by_z.pack, by_z.give, by_z.get = deal_ref.at[1], take_ref.at[1], pack.at[1], give3.at[1], get3.at[1]
    by_xy.s, by_xy.r, by_z.s, by_z.r = g_s.at[0], g_r.at[0], g_s.at[1], g_r.at[1]

    order = [(t, start, size, by_xy if xy else by_z) for t, (start, size, xy) in enumerate(TILES)]

    def first_copy(t, k, by):
        q, cols = (by.me + k) % 8, pl.ds(0, TILES[t][1])
        return remote(
            part.at[t, pl.ds(pl.multiple_of(q * 32, 32), 32), cols], rx1.at[t, k - 1, :, cols],
            a_s.at[t, k - 1], a_r.at[t, k - 1], by.peer(k),
        )

    for t, start, size, by in order:
        if by is by_z:
            def reorder(j, _):
                cols = pl.ds(pl.multiple_of(j * CC, CC), CC)
                dl_z[:, cols] = jnp.dot(order_ref[...], dl_all[:, cols], preferred_element_type=F32).astype(BF16)
                return 0

            lax.fori_loop(0, NC, reorder, 0)
        for h in range(0, size, 256):
            part[t, :, h : h + 256] = lax.dot_general(
                by.rows[...], head_v[start + h : start + h + 256, :], (((1,), (1,)), ((), ())),
                preferred_element_type=F32,
            ).astype(BF16)
        for k in RING:
            first_copy(t, k, by).start()

    def head_part(t, _):
        rows = pl.ds(pl.multiple_of(t * 256, 256), 256)
        gw[rows, :] = jnp.dot(turned[rows, :], dl_all[...], preferred_element_type=F32).astype(BF16)
        return 0

    lax.fori_loop(0, DEPTH // 256, head_part, 0)

    mask = row_of(rank_of(lens, ends_z, dp * GROUP + iota((1, GROUP), 1), True)[0]) == iota((ROWS, GROUP), 0)
    lr_out[...] = jnp.sum(jnp.where(mask, log_ratio, 0.0), axis=0, keepdims=True)
    en_out[...] = jnp.sum(jnp.where(mask, entropy, 0.0), axis=0, keepdims=True)

    def second_copy(t, k, by):
        q, cols = (by.other + k) % 8, pl.ds(0, TILES[t][1] // 2)
        return remote(
            s2.at[t, pl.ds(pl.multiple_of(q * 16, 16), 16), cols], rx2.at[t, k - 1, :, cols],
            b_s.at[t, k - 1], b_r.at[t, k - 1], by.across(k),
        )

    def third_copy(k, by):
        return remote(by.give.at[(by.me + k) % 8], by.get.at[k], by.s.at[k - 1], by.r.at[k - 1], by.peer(k))

    def each(make):
        for k in RING:
            make(k)

    for t, start, size, by in order:
        half = size // 2
        each(lambda k: first_copy(t, k, by).wait())
        acc = part[t, pl.ds(pl.multiple_of(by.me * 32, 32), 32), :size].astype(F32)
        for k in range(7):
            acc = acc + rx1[t, k, :, :size].astype(F32)
        both = jnp.concatenate([acc[:, :half], acc[:, half:]], axis=0).astype(BF16)
        s2[t, :, :half] = jnp.dot(by.deal[...], both, preferred_element_type=F32).astype(BF16)
        each(lambda k: second_copy(t, k, by).start())

    pack[...] = jnp.zeros_like(pack)
    for by in (by_xy, by_z):
        by.chunks, by.last = [], max(o[0] for o in order if o[3] is by)
    for t, start, size, by in order:
        half = size // 2
        each(lambda k: second_copy(t, k, by).wait())
        acc = s2[t, pl.ds(pl.multiple_of(by.other * 16, 16), 16), :half].astype(F32)
        for k in range(7):
            acc = acc + rx2[t, k, :, :half].astype(F32)
        for h in range(2):
            for e in range(0, half, 128):
                by.pack[:, len(by.chunks), :] = acc[8 * h : 8 * h + 8, e : e + 128]
                by.chunks.append(start + h * half + e)
        if t == by.last:
            by.give[...] = by.pack[...].astype(BF16)
            each(lambda k: third_copy(k, by).start())

    for by in (by_z, by_xy):
        by.get[0] = by.give[by.me]
        each(lambda k: third_copy(k, by).wait())
        rows = jnp.dot(by.take[...], by.get[...].reshape(128, 128), preferred_element_type=F32)
        by.pack[...] = rows.reshape(8, 16, 128)
        for c, start in enumerate(by.chunks):
            gh_out[:, start : start + 128] = by.pack[:, c, :].astype(BF16)


def store_kernel(*refs):
    copies = [pltpu.make_async_copy(refs[i], refs[4 + i], refs[8].at[i]) for i in range(4)]
    for c in copies:
        c.start()
    for c in copies:
        c.wait()


def local(hidden, head, token_ids, old_logp, advantages, lengths):
    vmem = pl.BlockSpec(memory_space=pltpu.VMEM)
    hbm = pl.BlockSpec(memory_space=pltpu.HBM)
    dma = pltpu.SemaphoreType.DMA
    keep = pltpu.with_memory_space_constraint
    gw, lr, en, gh = pl.pallas_call(
        main_kernel,
        out_shape=(
            pltpu.VMEM((DEPTH, COLS), BF16),
            pltpu.VMEM((1, GROUP), F32),
            pltpu.VMEM((1, GROUP), F32),
            pltpu.VMEM((8, DEPTH), BF16),
        ),
        in_specs=[hbm] * 6,
        out_specs=(vmem,) * 4,
        scratch_shapes=[
            pltpu.SMEM((8,), jnp.int32),
            pltpu.VMEM((1, SLOTS), jnp.int32),
            pltpu.VMEM((1, SLOTS), F32),
            pltpu.VMEM((1, SLOTS), F32),
            pltpu.VMEM((4, GROUP, DEPTH), BF16),
            pltpu.VMEM((DEPTH, COLS), BF16),
            pltpu.VMEM((ROWS, DEPTH), BF16),
            pltpu.VMEM((NC, 2, 2, 64, CC), F32),
            pltpu.VMEM((NC, 2, 64, CC), F32),
            pltpu.VMEM((NC, 64, CC), F32),
            pltpu.VMEM((NC, 64, CC), F32),
            pltpu.VMEM((64, COLS), F32),
            pltpu.VMEM((NC, 2, 2, 64, CC), F32),
            pltpu.VMEM((8, 128), F32),
            pltpu.VMEM((8, 128), F32),
            pltpu.VMEM((15, 8, 128), F32),
            pltpu.VMEM((15, 8, 128), F32),
            pltpu.VMEM((DEPTH, ROWS), BF16),
            pltpu.VMEM((ROWS, COLS), BF16),
            pltpu.VMEM((ROWS, COLS), BF16),
            pltpu.VMEM((NT, ROWS, TF), BF16),
            pltpu.VMEM((NT, 7, 32, TF), BF16),
            pltpu.VMEM((NT, 128, 256), BF16),
            pltpu.VMEM((NT, 7, 16, 256), BF16),
            pltpu.VMEM((2, 8, 16, 128), F32),
            pltpu.VMEM((2, 8, 16, 128), BF16),
            pltpu.VMEM((2, 8, 16, 128), BF16),
            pltpu.VMEM((ROWS, SLOTS), BF16),
            pltpu.VMEM((ROWS, ROWS), BF16),
            pltpu.VMEM((2, 128, 64), BF16),
            pltpu.VMEM((2, 128, 128), BF16),
            dma((6,)), dma((1,)), dma((1,)), dma((2, 2)), dma((2, 2)), dma((2,)), dma((2,)), dma((2,)), dma((2,)),
            dma((2, 2, 3)), dma((2, 2, 3)), dma((2, 7)), dma((2, 7)),
            dma((NC,)), dma((NC,)), dma((NC,)), dma((NC,)),
            dma((15,)), dma((15,)), dma((15,)), dma((15,)),
            dma((NC,)), dma((NC,)), dma((NC,)), dma((NC,)), dma((NC,)), dma((NC,)),
            dma((NT, 7)), dma((NT, 7)), dma((NT, 7)), dma((NT, 7)), dma((2, 7)), dma((2, 7)),
        ],
        compiler_params=pltpu.CompilerParams(
            collective_id=0, has_side_effects=True, vmem_limit_bytes=48 * 1024 * 1024
        ),
        name="main",
    )(*[keep(a, pltpu.HBM) for a in (lengths, token_ids[None], old_logp[None], advantages[None], hidden, head)])
    gw, lr, en, gh = pl.pallas_call(
        store_kernel,
        out_shape=(
            jax.ShapeDtypeStruct((DEPTH, COLS), BF16),
            jax.ShapeDtypeStruct((1, GROUP), F32),
            jax.ShapeDtypeStruct((1, GROUP), F32),
            jax.ShapeDtypeStruct((8, DEPTH), BF16),
        ),
        in_specs=[vmem] * 4,
        out_specs=(hbm,) * 4,
        scratch_shapes=[dma((4,))],
        compiler_params=pltpu.CompilerParams(vmem_limit_bytes=32 * 1024 * 1024),
        name="store",
    )(*[keep(a, pltpu.VMEM) for a in (gw, lr, en, gh)])
    return lr[0], en[0], gh, gw


def solution(mesh):
    in_specs = (P("dp", None), P("dp", "vocab"), P(), P(), P(), P())
    out_specs = (P("dp"), P("dp"), P("vocab", "dp"), P("dp", "vocab"))
    return jax.shard_map(local, mesh=mesh, in_specs=in_specs, out_specs=out_specs, check_vma=False)
```
